32 devices in a mesh: leaf: 8 (over y, x, core), col: 4 (over z).
Axes of the slice: x: 2, y: 2, z: 4, core: 2. Of those that a mesh axis runs over, the one named last changes fastest.
Arguments:
- basis: float32 [1024, 64, 256], P(('leaf', 'col')), may hold values from -0.4 to 0.4
- transfer: float32 [2040, 64, 64], P('leaf')
- top_transfer: float32 [6, 64, 64], replicated
- blocks0: bfloat16 [8192, 64, 64], P(('leaf', 'col')), may hold values from -6 to 6
- pairs0: int32 [8192, 2], P(('leaf', 'col')), may hold values from 0 to 1023, as said below
- counts0: int32 [32], P(('leaf', 'col')), may hold values from 128 to 256, as said below
- blocks1: bfloat16 [4096, 64, 64], P(('leaf', 'col')), may hold values from -6 to 6
- pairs1: int32 [4096, 2], P(('leaf', 'col')), may hold values from 0 to 511, as said below
- counts1: int32 [32], P(('leaf', 'col')), may hold values from 64 to 128, as said below
Outputs:
- projected0: bfloat16 [8192, 64, 64], P(('leaf', 'col'))
- projected1: bfloat16 [4096, 64, 64], P(('leaf', 'col'))
- root_factor: float32 [64, 64], replicated
- ancestor_factors: float32 [8, 3, 64, 64], P('leaf')
The draws below stay inside these ranges and needn't reach their ends.
Inputs may be any that keep to these rules, and one draw needn't show every extreme that they name: `pairs0`: the rows of one device (leaf index i, col index j) name a row cluster of the level within i's subtree (i * 128 / 2^l to (i + 1) * 128 / 2^l - 1) and a column cluster whose index modulo 4 is j. `pairs1`: as for pairs0, on the level above the leaves. `counts0`: slots at or past a device's count are padding; some device uses all 256 slots in every draw. `counts1`: slots at or past a device's count are padding; some device uses all 128 slots in every draw.
All inputs are finite; a program needn't handle non-finite values.
Results may differ from the reference program's by a relative error of at most 0.0065.
Values may be sent and summed in bfloat16 or wider, within the bound.
No kernel may reach another device: no remote copies, remote signals or barrier semaphores. Data moves between devices by JAX's collectives and lax.ppermute only.
A program may use at most 128 MiB of HBM per device.

```python
import jax
import jax.numpy as jnp
from jax import lax

K = 64
M = 256
LEAF_DEV = 128
B0 = 256
B1 = 128
LEAVES = 1024
XFER_DEV = 255
BLOCKS0 = 8192
BLOCKS1 = 4096
N_LEAF = 8
N_COL = 4


def near_identity(key, count):
    noise = jax.random.normal(key, (count, K, K), jnp.float32)
    eye = jnp.eye(K, dtype=jnp.float32)
    return (eye[None] + 0.4 * noise / K ** 0.5) * 0.5 ** 0.5


def draw_transfer(key, part):
    return near_identity(jax.random.fold_in(key, 11), N_LEAF * (2 * LEAF_DEV - 1))


def draw_top_transfer(key, part):
    return near_identity(jax.random.fold_in(key, 13), N_LEAF - 2)


def make_pairs(key, slots_dev, rows_dev):
    slots = N_LEAF * N_COL * slots_dev
    device = jnp.arange(slots, dtype=jnp.int32) // slots_dev
    leaf_pos = device // N_COL
    col_pos = device % N_COL
    key_row, key_col = jax.random.split(key)
    row = leaf_pos * rows_dev + jax.random.randint(key_row, (slots,), 0, rows_dev, dtype=jnp.int32)
    column = N_COL * jax.random.randint(key_col, (slots,), 0, rows_dev * N_LEAF // N_COL, dtype=jnp.int32) + col_pos
    return jnp.stack([row, column], axis=1).astype(jnp.int32)


def make_counts(key, slots_dev):
    devs = N_LEAF * N_COL
    counts = jax.random.randint(key, (devs,), slots_dev // 2, slots_dev + 1, dtype=jnp.int32)
    fullest = jax.random.randint(jax.random.fold_in(key, 7), (), 0, devs, dtype=jnp.int32)
    return counts.at[fullest].set(slots_dev).astype(jnp.int32)


def draw_pairs0(key, part):
    return make_pairs(jax.random.fold_in(key, 21), B0, LEAF_DEV)


def draw_pairs1(key, part):
    return make_pairs(jax.random.fold_in(key, 22), B0 // 2, LEAF_DEV // 2)


def draw_counts0(key, part):
    return make_counts(jax.random.fold_in(key, 31), B0)


def draw_counts1(key, part):
    return make_counts(jax.random.fold_in(key, 32), B0 // 2)


def shard_levels(rng, dims, cuts, low, top_value):
    gain = 1.0
    for dim, blocks in cuts:
        heights = jax.random.uniform(jax.random.fold_in(jax.random.fold_in(rng, 6), dim), (blocks,), jnp.float32, low / len(cuts), top_value / len(cuts))
        gain = gain * jnp.repeat(jnp.exp(heights), dims[dim] // blocks).reshape((-1,) + (1,) * (len(dims) - 1 - dim))
    return gain


def gaussian(stream_key, dims, width, limit, shards=(), kind=jnp.bfloat16):
    entries = width * jax.random.normal(stream_key, dims, jnp.float32)
    if shards:
        entries = entries * shard_levels(stream_key, dims, shards, -0.22, 0.18)
    return jnp.clip(entries, -limit, limit).astype(kind)


def setup_inputs(seed: int = 0) -> dict:
    arg_keys = jax.random.split(jax.random.key(seed), 10)
    return {
        "basis": gaussian(arg_keys[0], (LEAVES, K, M), 0.0625, 0.4, ((0, 32),), jnp.float32),
        "transfer": draw_transfer(jax.random.fold_in(arg_keys[9], 71), 0),
        "top_transfer": draw_top_transfer(jax.random.fold_in(arg_keys[9], 71), 0),
        "blocks0": gaussian(arg_keys[3], (BLOCKS0, K, K), 1.0, 6.0, ((0, 32),)),
        "pairs0": draw_pairs0(jax.random.fold_in(arg_keys[9], 71), 0),
        "counts0": draw_counts0(jax.random.fold_in(arg_keys[9], 71), 0),
        "blocks1": gaussian(arg_keys[6], (BLOCKS1, K, K), 1.0, 6.0, ((0, 32),)),
        "pairs1": draw_pairs1(jax.random.fold_in(arg_keys[9], 71), 0),
        "counts1": draw_counts1(jax.random.fold_in(arg_keys[9], 71), 0),
    }


def lift_gram(gram, xfer):
    product = jnp.einsum('cab,cbj->caj', gram, xfer, precision=lax.Precision.HIGHEST)
    return jnp.einsum('cak,caj->ckj', xfer, product, precision=lax.Precision.HIGHEST)

def factor(gram):
    return jnp.swapaxes(jnp.linalg.cholesky(gram), -1, -2)

def project_level(blocks, pairs, counts, factors, slots):
    devs = counts.shape[0]
    blocks_dev = blocks.reshape(devs, slots, K, K)
    pairs_dev = pairs.reshape(devs, slots, 2)

    def one_device(items):
        block_set, pair_set, used = items
        row_fac = jnp.take(factors, pair_set[:, 0], axis=0).astype(jnp.float32)
        col_fac = jnp.take(factors, pair_set[:, 1], axis=0).astype(jnp.float32)
        left = jnp.einsum('bik,bkj->bij', row_fac, block_set.astype(jnp.float32), precision=lax.Precision.HIGHEST).astype(jnp.bfloat16)
        result = jnp.einsum('bij,blj->bil', left.astype(jnp.float32), col_fac, precision=lax.Precision.HIGHEST)
        keep = jnp.arange(slots, dtype=jnp.int32) < used
        return jnp.where(keep[:, None, None], result, 0.0).astype(jnp.bfloat16)
    result = lax.map(one_device, (blocks_dev, pairs_dev, counts))
    return result.reshape(devs * slots, K, K)

def reference(basis, transfer, top_transfer, blocks0, pairs0, counts0, blocks1, pairs1, counts1):
    gram_now = jnp.einsum('ckm,cjm->ckj', basis, basis, precision=lax.Precision.HIGHEST)
    xfer_all = transfer.reshape(N_LEAF, XFER_DEV, K, K)
    grams = [gram_now]
    offset = 0
    count = LEAF_DEV
    while count > 1:
        xfer_level = xfer_all[:, offset:offset + count].reshape(N_LEAF * count, K, K)
        lifted = lift_gram(gram_now, xfer_level)
        gram_now = lifted[0::2] + lifted[1::2]
        offset += count
        count //= 2
        grams.append(gram_now)
    xfer_level = xfer_all[:, offset]
    off_top = 0
    level = N_LEAF
    height = 0
    ancestors = []
    while level > 1:
        if height > 0:
            xfer_level = top_transfer[off_top:off_top + level]
            off_top += level
        lifted = lift_gram(gram_now, xfer_level)
        gram_now = lifted[0::2] + lifted[1::2]
        level //= 2
        height += 1
        ancestors.append(jnp.repeat(factor(gram_now), 2 ** height, axis=0))
    ancestor_factors = jnp.stack(ancestors, axis=1)
    root_factor = factor(gram_now[0])
    factor0 = factor(grams[0]).astype(jnp.bfloat16)
    factor1 = factor(grams[1]).astype(jnp.bfloat16)
    projected0 = project_level(blocks0, pairs0, counts0, factor0, B0)
    projected1 = project_level(blocks1, pairs1, counts1, factor1, B1)
    return (projected0, projected1, root_factor, ancestor_factors)
```

```python
import functools

import jax
import jax.numpy as jnp
from jax import lax
from jax.experimental import pallas as pl
from jax.experimental.pallas import tpu as pltpu
from jax.sharding import PartitionSpec as P

BF, F32 = jnp.bfloat16, jnp.float32
EXACT = lax.Precision.HIGHEST
NT = (((1,), (1,)), ((), ()))
NN = (((1,), (0,)), ((), ()))
K = 64
H = K // 2
LANES = 128
SMEM = pl.BlockSpec(memory_space=pltpu.SMEM)
VMEM = pl.BlockSpec(memory_space=pltpu.VMEM)
PARAMS = pltpu.CompilerParams(vmem_limit_bytes=48 * 2**20)


def unhalf(x):
    return jnp.concatenate([x[:, :K], x[:, K:]], axis=0)


def halve(x):
    return jnp.concatenate([x[:H], x[H:]], axis=1)


def mul(x, y, dims):
    return lax.dot_general(x, y, dims, precision=EXACT, preferred_element_type=F32)


def lift(gram, xfer_t):
    return mul(mul(xfer_t, gram, NN), xfer_t, NT)


def unpack_transfers(xfer_ref, xt):
    @pl.loop(0, H)
    def _(q):
        xt[:, q, :] = jnp.concatenate([xfer_ref[:, q, :], xfer_ref[:, q + H, :]], axis=0).T


def cholesky_lanes(a):
    sub = lax.broadcasted_iota(jnp.int32, (8, a.shape[2]), 0)

    def cols(block):
        return pl.ds(pl.multiple_of(8 * block, 8), 8)

    for panel in range(K // 8):
        base = 8 * panel
        scale = []
        rows = [a[base + k, pl.ds(base, 8), :] for k in range(8)]
        for k in range(8):
            scale.append(lax.rsqrt(rows[k][k : k + 1, :]))
            rows[k] = rows[k] * scale[k]
            for i in range(k + 1, 8):
                rows[i] = rows[i] - rows[k][i : i + 1, :] * rows[k]
        for k in range(8):
            a[base + k, pl.ds(base, 8), :] = jnp.where(sub >= k, rows[k], 0.0)
        for j in range(panel + 1, K // 8):
            new = []
            for k in range(8):
                acc = a[base + k, pl.ds(8 * j, 8), :]
                for p in range(k):
                    acc = acc - rows[p][k : k + 1, :] * new[p]
                new.append(acc * scale[k])
            for k in range(8):
                a[base + k, pl.ds(8 * j, 8), :] = new[k]
        if panel < K // 8 - 1:

            @pl.loop(panel + 1, K // 8)
            def _(i_block):
                left = [a[base + k, cols(i_block), :] for k in range(8)]

                @pl.loop(i_block, K // 8)
                def _(j_block):
                    right = [a[base + k, cols(j_block), :] for k in range(8)]
                    for i in range(8):
                        acc = a[8 * i_block + i, cols(j_block), :]
                        for k in range(8):
                            acc = acc - left[k][i : i + 1, :] * right[k]
                        a[8 * i_block + i, cols(j_block), :] = acc

    for i in range(8, K):
        a[i, pl.ds(0, i // 8 * 8), :] = jnp.zeros((i // 8 * 8, a.shape[2]), F32)


def factor_halved(s, a):
    @pl.loop(0, H)
    def _(q):
        y = s[:, q, :].T
        a[q] = y[:K]
        a[q + H] = y[K:]

    cholesky_lanes(a)

    @pl.loop(0, H)
    def _(q):
        s[:, q, :] = jnp.concatenate([a[q], a[q + H]], axis=0).T


def factor_kernel(own, at_ref, basis_ref, xfer_ref, fac_ref, gram1_ref, xt, s, a):
    first = at_ref[1] * own
    unpack_transfers(xfer_ref, xt)

    @pl.loop(0, own // 2)
    def _(p):
        total = None
        for c in range(2):
            points = basis_ref[2 * p + c]
            gram = mul(points, points, NT)
            s[2 * p + c] = halve(gram)
            lifted = lift(gram, unhalf(xt[first + 2 * p + c]))
            total = lifted if total is None else total + lifted
        gram1_ref[p] = total
        s[own + p] = halve(total)

    factor_halved(s, a)
    fac_ref[...] = s[0 : own + own // 2].astype(BF)


def own_factors(at, basis, xfer_lanes):
    own = basis.shape[0]
    count = own + own // 2
    return pl.pallas_call(
        functools.partial(factor_kernel, own),
        out_shape=(
            jax.ShapeDtypeStruct((count, H, 2 * K), BF),
            jax.ShapeDtypeStruct((own // 2, K, K), F32),
        ),
        grid=(1,),
        in_specs=[
            SMEM,
            pl.BlockSpec(basis.shape, lambda i: (0, 0, 0)),
            pl.BlockSpec((K, K, LANES), lambda i: (0, 0, 0)),
        ],
        out_specs=(
            pl.BlockSpec((count, H, 2 * K), lambda i: (0, 0, 0)),
            pl.BlockSpec((own // 2, K, K), lambda i: (0, 0, 0)),
        ),
        scratch_shapes=[pltpu.VMEM((LANES, H, 2 * K), F32)] * 2 + [pltpu.VMEM((K, K, LANES), F32)],
        compiler_params=PARAMS,
    )(at, basis, xfer_lanes)


def chain_kernel(own, cols, at_ref, gram1_ref, xfer_ref, out_ref, xt, g):
    col = at_ref[1]
    unpack_transfers(xfer_ref, xt)
    g[...] = gram1_ref[...]
    offset = 0
    here = own // 2
    width = own * cols // 2
    while here > 1:

        def step(p, _, first=offset + col * here):
            low = lift(g[2 * p], unhalf(xt[first + 2 * p]))
            high = lift(g[2 * p + 1], unhalf(xt[first + 2 * p + 1]))
            g[p] = low + high
            return 0

        lax.fori_loop(0, here // 2, step, 0)
        offset += width
        width //= 2
        here //= 2
    gram = g[0]
    shift = 0
    while width >= 1:
        gram = lift(gram, unhalf(xt[offset + jnp.right_shift(col, shift)]))
        offset += width
        width //= 2
        shift += 1
    out_ref[...] = halve(gram)


def lifted_root(at, gram1, xfer_lanes, own, cols):
    return pl.pallas_call(
        functools.partial(chain_kernel, own, cols),
        out_shape=jax.ShapeDtypeStruct((H, 2 * K), F32),
        grid=(1,),
        in_specs=[
            SMEM,
            pl.BlockSpec(gram1.shape, lambda i: (0, 0, 0)),
            pl.BlockSpec((K, K, LANES), lambda i: (0, 0, 1)),
        ],
        out_specs=pl.BlockSpec((H, 2 * K), lambda i: (0, 0)),
        scratch_shapes=[pltpu.VMEM((LANES, H, 2 * K), F32), pltpu.VMEM(gram1.shape, F32)],
        compiler_params=PARAMS,
    )(at, gram1, xfer_lanes)


def top_kernel(leaves, cols, at_ref, parts_ref, top_ref, anc_ref, root_ref, s, a):
    group = 2 * cols
    level = []
    for m in range(leaves // 2):
        total = parts_ref[m * group]
        for c in range(1, group):
            total = total + parts_ref[m * group + c]
        level.append(unhalf(total))
    heights = []
    slot = 0
    off_top = 0
    while True:
        heights.append(slot)
        for m, gram in enumerate(level):
            s[slot + m] = halve(gram)
        slot += len(level)
        if len(level) == 1:
            break
        lifted = []
        for m, gram in enumerate(level):
            xfer = top_ref[off_top + m]
            lifted.append(lift(gram, xfer.T))
        off_top += len(level)
        level = [lifted[2 * m] + lifted[2 * m + 1] for m in range(len(level) // 2)]
    factor_halved(s, a)
    for h, start in enumerate(heights):
        anc_ref[0, h] = unhalf(s[start + jnp.right_shift(at_ref[0], h + 1)])
    root_ref[...] = unhalf(s[heights[-1]])


def top_factors(at, parts, top_transfer, leaves, cols):
    height = leaves.bit_length() - 1
    return pl.pallas_call(
        functools.partial(top_kernel, leaves, cols),
        out_shape=(
            jax.ShapeDtypeStruct((1, height, K, K), F32),
            jax.ShapeDtypeStruct((K, K), F32),
        ),
        in_specs=[SMEM, VMEM, VMEM],
        out_specs=(VMEM, VMEM),
        scratch_shapes=[pltpu.VMEM((LANES, H, 2 * K), F32), pltpu.VMEM((K, K, LANES), F32)],
        compiler_params=PARAMS,
    )(at, parts, top_transfer)


UNROLL = 16


def lane_groups(sizes):
    return [(which, lane) for which, size in enumerate(sizes) for lane in range(0, size, LANES)]


def left_kernel(groups, index_ref, table_ref, *refs):
    blocks, left_ref, bt = refs[:-2], refs[-2], refs[-1]
    for g, (which, lane) in enumerate(groups):
        src = blocks[which]

        @pl.loop(0, H)
        def _(q):
            lanes = pl.ds(lane, LANES)
            x = jnp.concatenate([src[q, :, lanes], src[q + H, :, lanes]], axis=0)
            bt[:, q, :] = x.astype(F32).T

        @pl.loop(0, LANES // UNROLL)
        def _(step):
            for u in range(UNROLL):
                b = step * UNROLL + u
                row = unhalf(table_ref[index_ref[LANES * g + b]])
                block = unhalf(bt[b].astype(BF))
                y = lax.dot_general(row, block, NN, preferred_element_type=F32)
                left_ref[LANES * g + b] = halve(y.astype(BF))


def left_products(table, index, blocks):
    groups = lane_groups([x.shape[2] for x in blocks])
    return pl.pallas_call(
        functools.partial(left_kernel, groups),
        out_shape=jax.ShapeDtypeStruct((LANES * len(groups), H, 2 * K), BF),
        in_specs=[SMEM, VMEM] + [VMEM] * len(blocks),
        out_specs=VMEM,
        scratch_shapes=[pltpu.VMEM((LANES, H, 2 * K), F32)],
        compiler_params=PARAMS,
    )(index, table, *blocks)


def right_kernel(groups, outs, index_ref, counts_ref, table_ref, left_ref, *refs):
    out_refs, pt = refs[:outs], refs[outs]
    for g, (which, lane) in enumerate(groups):
        dst = out_refs[which]

        @pl.loop(0, LANES // UNROLL)
        def _(step):
            for u in range(UNROLL):
                b = step * UNROLL + u
                col = unhalf(table_ref[index_ref[LANES * g + b]])
                left = unhalf(left_ref[LANES * g + b])
                y = lax.dot_general(left, col, NT, preferred_element_type=F32)
                pt[b] = halve(y)

        keep = lax.broadcasted_iota(jnp.int32, (2 * K, LANES), 1) < counts_ref[which] - lane

        @pl.loop(0, H)
        def _(q):
            y = jnp.where(keep, pt[:, q, :].T, 0.0).astype(BF)
            dst[q, :, pl.ds(lane, LANES)] = y[:K]
            dst[q + H, :, pl.ds(lane, LANES)] = y[K:]


def right_products(table, index, counts, left, sizes):
    groups = lane_groups(sizes)
    return pl.pallas_call(
        functools.partial(right_kernel, groups, len(sizes)),
        out_shape=tuple(jax.ShapeDtypeStruct((K, K, size), BF) for size in sizes),
        in_specs=[SMEM, SMEM, VMEM, VMEM],
        out_specs=(VMEM,) * len(sizes),
        scratch_shapes=[pltpu.VMEM((LANES, H, 2 * K), F32)],
        compiler_params=PARAMS,
    )(index, counts, table, left)


def on_device(basis, transfer, top_transfer, blocks0, pairs0, counts0, blocks1, pairs1, counts1):
    own = basis.shape[0]
    cols = lax.axis_size("col")
    leaves = lax.axis_size("leaf")
    leaf, col = lax.axis_index("leaf"), lax.axis_index("col")
    at = jnp.stack([leaf, col]).astype(jnp.int32)
    xfer_lanes = jnp.transpose(transfer, (1, 2, 0))
    lanes0, lanes1 = jnp.transpose(blocks0, (1, 2, 0)), jnp.transpose(blocks1, (1, 2, 0))

    factors, gram1 = own_factors(at, basis, xfer_lanes)
    count = own + own // 2
    row_table = lax.all_gather(factors, "col", axis=0, tiled=True)

    parts = count // cols
    part = lax.dynamic_index_in_dim(
        row_table.reshape(cols * parts, cols, H, 2 * K), col, axis=1, keepdims=False
    )
    col_table = lax.all_gather(part, "leaf", axis=0, tiled=True)

    def indices(pairs, level):
        size = own >> level
        row = pairs[:, 0] - leaf * (size * cols)
        row = row // size * count + level * own + row % size
        column = pairs[:, 1] // size * parts + level * (own // cols) + pairs[:, 1] % size // cols
        return row, column

    row0, column0 = indices(pairs0, 0)
    row1, column1 = indices(pairs1, 1)
    left = left_products(row_table, jnp.concatenate([row0, row1]), (lanes0, lanes1))

    lifted = lifted_root(at, gram1, xfer_lanes, own, cols)
    lifted_all = lax.all_gather(lifted, ("leaf", "col"), axis=0)
    ancestors, root = top_factors(at, lifted_all, top_transfer, leaves, cols)

    out0, out1 = right_products(
        col_table,
        jnp.concatenate([column0, column1]),
        jnp.concatenate([counts0, counts1]),
        left,
        (blocks0.shape[0], blocks1.shape[0]),
    )
    return (jnp.transpose(out0, (2, 0, 1)), jnp.transpose(out1, (2, 0, 1)), root, ancestors)


def solution(mesh):
    in_specs = (
        P(("leaf", "col"), None, None),
        P("leaf", None, None),
        P(),
        P(("leaf", "col"), None, None),
        P(("leaf", "col"), None),
        P(("leaf", "col")),
        P(("leaf", "col"), None, None),
        P(("leaf", "col"), None),
        P(("leaf", "col")),
    )
    out_specs = (
        P(("leaf", "col"), None, None),
        P(("leaf", "col"), None, None),
        P(),
        P("leaf", None, None, None),
    )
    return jax.shard_map(
        on_device, mesh=mesh, in_specs=in_specs, out_specs=out_specs, check_vma=False
    )
```

```python
import functools

import jax
import jax.numpy as jnp
from jax import lax
from jax.experimental import pallas as pl
from jax.experimental.pallas import tpu as pltpu
from jax.sharding import PartitionSpec as P

BF, F32 = jnp.bfloat16, jnp.float32
EXACT = lax.Precision.HIGHEST
NT = (((1,), (1,)), ((), ()))
NN = (((1,), (0,)), ((), ()))
K = 64
H = K // 2
LANES = 128
SMEM = pl.BlockSpec(memory_space=pltpu.SMEM)
VMEM = pl.BlockSpec(memory_space=pltpu.VMEM)
ANY = pl.BlockSpec(memory_space=pl.ANY)
TURN = 8
SLOTS = 64
PAIRS = 4
PARAMS = pltpu.CompilerParams(vmem_limit_bytes=48 * 2**20)


def unhalf(x):
    return jnp.concatenate([x[:, :K], x[:, K:]], axis=0)


def halve(x):
    return jnp.concatenate([x[:H], x[H:]], axis=1)


def mul(x, y, dims):
    return lax.dot_general(x, y, dims, precision=EXACT, preferred_element_type=F32)


def lift_all(grams, xfers_t):
    halfway = [mul(f, g, NN) for f, g in zip(xfers_t, grams)]
    return [mul(t, f, NT) for t, f in zip(halfway, xfers_t)]


def lift_pairs(grams, xfers_t):
    lifted = lift_all(grams, xfers_t)
    return [low + high for low, high in zip(lifted[0::2], lifted[1::2])]


def cost(flops, size):
    return pl.CostEstimate(flops=flops, bytes_accessed=size, transcendentals=0)


def unpack_transfers(xfer_ref, xt):
    @pl.loop(0, H // TURN)
    def _(step):
        at = [step * TURN + v for v in range(TURN)]
        turned = [jnp.concatenate([xfer_ref[:, q, :], xfer_ref[:, q + H, :]], axis=0).T for q in at]
        for q, y in zip(at, turned):
            xt[:, q, :] = y


def cholesky_lanes(a):
    sub = lax.broadcasted_iota(jnp.int32, (8, a.shape[2]), 0)

    def cols(block):
        return pl.ds(pl.multiple_of(8 * block, 8), 8)

    for panel in range(K // 8):
        base = 8 * panel
        scale = []
        rows = [a[base + k, pl.ds(base, 8), :] for k in range(8)]
        for k in range(8):
            scale.append(lax.rsqrt(rows[k][k : k + 1, :]))
            rows[k] = rows[k] * scale[k]
            for i in range(k + 1, 8):
                rows[i] = rows[i] - rows[k][i : i + 1, :] * rows[k]
        for k in range(8):
            a[base + k, pl.ds(base, 8), :] = jnp.where(sub >= k, rows[k], 0.0)
        for j in range(panel + 1, K // 8):
            new = []
            for k in range(8):
                acc = a[base + k, pl.ds(8 * j, 8), :]
                for p in range(k):
                    acc = acc - rows[p][k : k + 1, :] * new[p]
                new.append(acc * scale[k])
            for k in range(8):
                a[base + k, pl.ds(8 * j, 8), :] = new[k]
        if panel < K // 8 - 1:

            @pl.loop(panel + 1, K // 8)
            def _(i_block):
                left = [a[base + k, cols(i_block), :] for k in range(8)]

                @pl.loop(i_block, K // 8)
                def _(j_block):
                    right = [a[base + k, cols(j_block), :] for k in range(8)]
                    for i in range(8):
                        acc = a[8 * i_block + i, cols(j_block), :]
                        for k in range(8):
                            acc = acc - left[k][i : i + 1, :] * right[k]
                        a[8 * i_block + i, cols(j_block), :] = acc

    for i in range(8, K):
        a[i, pl.ds(0, i // 8 * 8), :] = jnp.zeros((i // 8 * 8, a.shape[2]), F32)


def factor_halved(s, a):
    @pl.loop(0, H // TURN)
    def _(step):
        at = [step * TURN + v for v in range(TURN)]
        turned = [s[:, q, :].T for q in at]
        for q, y in zip(at, turned):
            a[q] = y[:K]
            a[q + H] = y[K:]

    cholesky_lanes(a)

    @pl.loop(0, H // TURN)
    def _(step):
        at = [step * TURN + v for v in range(TURN)]
        turned = [jnp.concatenate([a[q], a[q + H]], axis=0).T for q in at]
        for q, y in zip(at, turned):
            s[:, q, :] = y


def factor_kernel(own, cols, at_ref, basis_ref, xfer_ref, fac_ref, sent_ref, gram1_ref, xt, s, a):
    col = at_ref[1]
    first = col * own
    unpack_transfers(xfer_ref, xt)

    pairs = min(PAIRS, own // 2)

    @pl.loop(0, own // 2 // pairs)
    def _(step):
        base = step * pairs
        at = [2 * base + c for c in range(2 * pairs)]
        points = [basis_ref[c] for c in at]
        grams = [mul(x, x, NT) for x in points]
        parents = lift_pairs(grams, [unhalf(xt[first + c]) for c in at])
        for c, gram in zip(at, grams):
            s[c] = halve(gram)
        for p, gram in enumerate(parents):
            gram1_ref[base + p] = gram
            s[own + base + p] = halve(gram)

    factor_halved(s, a)
    count = own + own // 2
    fac_ref[...] = s[0:count].astype(BF)
    for e in range(cols):
        for r in range(count // cols):
            sent_ref[e, r] = s[r * cols + jnp.bitwise_xor(col, e)].astype(BF)


def own_factors(at, basis, xfer_lanes, cols):
    own = basis.shape[0]
    count = own + own // 2
    rows = (count + 7) // 8 * 8
    shapes = (
        jax.ShapeDtypeStruct((count, H, 2 * K), BF),
        jax.ShapeDtypeStruct((cols, count // cols, H, 2 * K), BF),
        jax.ShapeDtypeStruct((own // 2, K, K), F32),
    )
    return pl.pallas_call(
        functools.partial(factor_kernel, own, cols),
        out_shape=shapes,
        grid=(1,),
        in_specs=[
            SMEM,
            pl.BlockSpec(basis.shape, lambda i: (0, 0, 0)),
            pl.BlockSpec((K, K, LANES), lambda i: (0, 0, 0)),
        ],
        out_specs=tuple(
            pl.BlockSpec(x.shape, lambda i, rank=len(x.shape): (0,) * rank) for x in shapes
        ),
        scratch_shapes=[
            pltpu.VMEM((LANES, H, 2 * K), F32),
            pltpu.VMEM((rows, H, 2 * K), F32),
            pltpu.VMEM((K, K, rows), F32),
        ],
        compiler_params=PARAMS,
        cost_estimate=cost(own * 2**24, 2**23),
    )(at, basis, xfer_lanes)


def chain_kernel(own, cols, at_ref, gram1_ref, xfer_ref, out_ref, xt):
    col = at_ref[1]
    unpack_transfers(xfer_ref, xt)
    grams = [gram1_ref[c] for c in range(own // 2)]
    offset = 0
    width = own * cols // 2
    while len(grams) > 1:
        here = len(grams)
        first = offset + col * here
        grams = lift_pairs(grams, [unhalf(xt[first + c]) for c in range(here)])
        offset += width
        width //= 2
    shift = 0
    while width >= 1:
        grams = lift_all(grams, [unhalf(xt[offset + jnp.right_shift(col, shift)])])
        offset += width
        width //= 2
        shift += 1
    out_ref[...] = halve(grams[0])


def lifted_root(at, gram1, xfer_lanes, own, cols):
    return pl.pallas_call(
        functools.partial(chain_kernel, own, cols),
        out_shape=jax.ShapeDtypeStruct((H, 2 * K), F32),
        grid=(1,),
        in_specs=[
            SMEM,
            pl.BlockSpec(gram1.shape, lambda i: (0, 0, 0)),
            pl.BlockSpec((K, K, LANES), lambda i: (0, 0, 1)),
        ],
        out_specs=pl.BlockSpec((H, 2 * K), lambda i: (0, 0)),
        scratch_shapes=[pltpu.VMEM((LANES, H, 2 * K), F32)],
        compiler_params=PARAMS,
        cost_estimate=cost(own * 2**24, 2**22),
    )(at, gram1, xfer_lanes)


def top_kernel(leaves, at_ref, top_ref, *refs):
    pairs = leaves // 2
    parts, (anc_ref, root_ref, level_ref, s, a) = refs[:pairs], refs[pairs:]
    pair = jnp.right_shift(at_ref[0], 1)
    for m in range(pairs):
        level_ref[jnp.bitwise_xor(pair, m)] = parts[m][...]
    level = [unhalf(level_ref[m]) for m in range(pairs)]
    heights = []
    slot = 0
    off_top = 0
    while True:
        heights.append(slot)
        for m, gram in enumerate(level):
            s[slot + m] = halve(gram)
        slot += len(level)
        if len(level) == 1:
            break
        level_xfers = [top_ref[off_top + m].T for m in range(len(level))]
        off_top += len(level)
        level = lift_pairs(level, level_xfers)
    factor_halved(s, a)
    for h, start in enumerate(heights):
        anc_ref[0, h] = unhalf(s[start + jnp.right_shift(at_ref[0], h + 1)])
    root_ref[...] = unhalf(s[heights[-1]])


def top_factors(at, parts, top_transfer, leaves):
    height = leaves.bit_length() - 1
    rows = (leaves - 1 + 7) // 8 * 8
    return pl.pallas_call(
        functools.partial(top_kernel, leaves),
        out_shape=(
            jax.ShapeDtypeStruct((1, height, K, K), F32),
            jax.ShapeDtypeStruct((K, K), F32),
        ),
        in_specs=[SMEM, VMEM] + [VMEM] * len(parts),
        out_specs=(VMEM, VMEM),
        scratch_shapes=[
            pltpu.VMEM((leaves // 2, H, 2 * K), F32),
            pltpu.VMEM((rows, H, 2 * K), F32),
            pltpu.VMEM((K, K, rows), F32),
        ],
        compiler_params=PARAMS,
        cost_estimate=cost(2**28, 2**20),
    )(at, top_transfer, *parts)


def lane_groups(sizes):
    return [(which, lane) for which, size in enumerate(sizes) for lane in range(0, size, LANES)]


def fill(table, pieces, sem):
    start = 0
    copies = []
    for n, piece in enumerate(pieces):
        copies.append(
            pltpu.make_async_copy(piece, table.at[pl.ds(start, piece.shape[0])], sem.at[n])
        )
        start += piece.shape[0]
    for copy in copies:
        copy.start()
    return copies


def left_kernel(groups, inputs, index_ref, *refs):
    blocks, pieces = refs[: inputs[0]], refs[inputs[0] : sum(inputs)]
    left_ref, bt, table, sem = refs[sum(inputs) :]
    copies = fill(table, pieces, sem)
    for g, (which, lane) in enumerate(groups):
        src = blocks[which]

        @pl.loop(0, H // TURN)
        def _(step):
            lanes = pl.ds(lane, LANES)
            at = [step * TURN + v for v in range(TURN)]
            x = [jnp.concatenate([src[q, :, lanes], src[q + H, :, lanes]], axis=0) for q in at]
            turned = [y.astype(F32).T for y in x]
            for q, y in zip(at, turned):
                bt[:, q, :] = y

        if g == 0:
            for copy in copies:
                copy.wait()

        @pl.loop(0, LANES // SLOTS)
        def _(step):
            at = [step * SLOTS + u for u in range(SLOTS)]
            rows = [unhalf(table[index_ref[LANES * g + b]]) for b in at]
            cells = [unhalf(bt[b].astype(BF)) for b in at]
            y = [lax.dot_general(r, c, NN, preferred_element_type=F32) for r, c in zip(rows, cells)]
            y = [halve(z.astype(BF)) for z in y]
            for b, z in zip(at, y):
                left_ref[LANES * g + b] = z


def left_products(pieces, index, blocks):
    groups = lane_groups([x.shape[2] for x in blocks])
    entries = sum(x.shape[0] for x in pieces)
    return pl.pallas_call(
        functools.partial(left_kernel, groups, (len(blocks), len(pieces))),
        out_shape=jax.ShapeDtypeStruct((LANES * len(groups), H, 2 * K), BF),
        in_specs=[SMEM] + [VMEM] * len(blocks) + [ANY] * len(pieces),
        out_specs=VMEM,
        scratch_shapes=[
            pltpu.VMEM((LANES, H, 2 * K), F32),
            pltpu.VMEM((entries, H, 2 * K), BF),
            pltpu.SemaphoreType.DMA((len(pieces),)),
        ],
        compiler_params=PARAMS,
        cost_estimate=cost(len(groups) * 2**31, 2**24),
    )(index, *blocks, *pieces)


def right_kernel(groups, outs, count, index_ref, counts_ref, left_ref, *refs):
    pieces, out_refs = refs[:count], refs[count : count + outs]
    pt, table, sem = refs[count + outs :]
    for copy in fill(table, pieces, sem):
        copy.wait()
    for g, (which, lane) in enumerate(groups):
        dst = out_refs[which]

        @pl.loop(0, LANES // SLOTS)
        def _(step):
            at = [step * SLOTS + u for u in range(SLOTS)]
            cols = [unhalf(table[index_ref[LANES * g + b]]) for b in at]
            left = [unhalf(left_ref[LANES * g + b]) for b in at]
            y = [lax.dot_general(x, c, NT, preferred_element_type=F32) for x, c in zip(left, cols)]
            y = [halve(z) for z in y]
            for b, z in zip(at, y):
                pt[b] = z

        keep = lax.broadcasted_iota(jnp.int32, (2 * K, LANES), 1) < counts_ref[which] - lane

        @pl.loop(0, H // TURN)
        def _(step):
            lanes = pl.ds(lane, LANES)
            at = [step * TURN + v for v in range(TURN)]
            turned = [pt[:, q, :].T for q in at]
            for q, y in zip(at, turned):
                y = jnp.where(keep, y, 0.0).astype(BF)
                dst[q, :, lanes] = y[:K]
                dst[q + H, :, lanes] = y[K:]


def right_products(pieces, index, counts, left, sizes):
    groups = lane_groups(sizes)
    entries = sum(x.shape[0] for x in pieces)
    return pl.pallas_call(
        functools.partial(right_kernel, groups, len(sizes), len(pieces)),
        out_shape=tuple(jax.ShapeDtypeStruct((K, K, size), BF) for size in sizes),
        in_specs=[SMEM, SMEM, VMEM] + [ANY] * len(pieces),
        out_specs=(VMEM,) * len(sizes),
        scratch_shapes=[
            pltpu.VMEM((LANES, H, 2 * K), F32),
            pltpu.VMEM((entries, H, 2 * K), BF),
            pltpu.SemaphoreType.DMA((len(pieces),)),
        ],
        compiler_params=PARAMS,
        cost_estimate=cost(len(groups) * 2**31, 2**24),
    )(index, counts, left, *pieces)


def swapped(x, axis, d):
    return lax.ppermute(x, axis, [(i, i ^ d) for i in range(lax.axis_size(axis))])


def on_device(basis, transfer, top_transfer, blocks0, pairs0, counts0, blocks1, pairs1, counts1):
    own = basis.shape[0]
    cols = lax.axis_size("col")
    leaves = lax.axis_size("leaf")
    leaf, col = lax.axis_index("leaf"), lax.axis_index("col")
    at = jnp.stack([leaf, col]).astype(jnp.int32)
    xfer_lanes = jnp.transpose(transfer, (1, 2, 0))
    lanes0, lanes1 = jnp.transpose(blocks0, (1, 2, 0)), jnp.transpose(blocks1, (1, 2, 0))
    count = own + own // 2
    parts = count // cols

    def indices(pairs, level):
        size = own >> level
        row = pairs[:, 0] - leaf * (size * cols)
        row = (row // size ^ col) * count + level * own + row % size
        owner = pairs[:, 1] // size
        away = owner // cols ^ leaf
        piece = (away & 1) * (leaves // 2) + (away >> 1)
        column = (piece * cols + (owner % cols ^ col)) * parts
        return row, column + level * (own // cols) + pairs[:, 1] % size // cols

    row0, column0 = indices(pairs0, 0)
    row1, column1 = indices(pairs1, 1)

    factors, sent, gram1 = own_factors(at, basis, xfer_lanes, cols)
    part = [sent[0]] + [swapped(sent[d], "col", d) for d in range(1, cols)]
    part = jnp.concatenate(part, axis=0)
    row_pieces = [factors] + [swapped(factors, "col", d) for d in range(1, cols)]
    same_core = [part] + [swapped(part, "leaf", d) for d in range(2, leaves, 2)]
    other_core = swapped(jnp.concatenate(same_core, axis=0), "leaf", 1)

    gram = lifted_root(at, gram1, xfer_lanes, own, cols)
    for bit in range(cols.bit_length() - 1):
        gram = gram + swapped(gram, "col", 1 << bit)
    gram = gram + swapped(gram, "leaf", 1)
    tops = [gram] + [swapped(gram, "leaf", d) for d in range(2, leaves, 2)]
    ancestors, root = top_factors(at, tops, top_transfer, leaves)

    left = left_products(row_pieces, jnp.concatenate([row0, row1]), (lanes0, lanes1))
    out0, out1 = right_products(
        same_core + [other_core],
        jnp.concatenate([column0, column1]),
        jnp.concatenate([counts0, counts1]),
        left,
        (blocks0.shape[0], blocks1.shape[0]),
    )
    return (jnp.transpose(out0, (2, 0, 1)), jnp.transpose(out1, (2, 0, 1)), root, ancestors)


def solution(mesh):
    in_specs = (
        P(("leaf", "col"), None, None),
        P("leaf", None, None),
        P(),
        P(("leaf", "col"), None, None),
        P(("leaf", "col"), None),
        P(("leaf", "col")),
        P(("leaf", "col"), None, None),
        P(("leaf", "col"), None),
        P(("leaf", "col")),
    )
    out_specs = (
        P(("leaf", "col"), None, None),
        P(("leaf", "col"), None, None),
        P(),
        P("leaf", None, None, None),
    )
    return jax.shard_map(
        on_device, mesh=mesh, in_specs=in_specs, out_specs=out_specs, check_vma=False
    )
```

```python
import functools

import jax
import jax.numpy as jnp
from jax import lax
from jax.experimental import pallas as pl
from jax.experimental.pallas import tpu as pltpu
from jax.sharding import PartitionSpec as P

BF, F32 = jnp.bfloat16, jnp.float32
EXACT = lax.Precision.HIGHEST
NT = (((1,), (1,)), ((), ()))
NN = (((1,), (0,)), ((), ()))
K = 64
H = K // 2
Q = K // 4
LANES = 128
SMEM = pl.BlockSpec(memory_space=pltpu.SMEM)
VMEM = pl.BlockSpec(memory_space=pltpu.VMEM)
ANY = pl.BlockSpec(memory_space=pl.ANY)
TURN = 8
SLOTS = 64
PAIRS = 4
PARAMS = pltpu.CompilerParams(vmem_limit_bytes=48 * 2**20)


def unhalf(x):
    return jnp.concatenate([x[:, :K], x[:, K:]], axis=0)


def halve(x):
    return jnp.concatenate([x[:H], x[H:]], axis=1)


def mul(x, y, dims):
    return lax.dot_general(x, y, dims, precision=EXACT, preferred_element_type=F32)


def lift_all(grams, xfers_t):
    halfway = [mul(f, g, NN) for f, g in zip(xfers_t, grams)]
    return [mul(t, f, NT) for t, f in zip(halfway, xfers_t)]


def lift_pairs(grams, xfers_t):
    lifted = lift_all(grams, xfers_t)
    return [low + high for low, high in zip(lifted[0::2], lifted[1::2])]


def cost(flops, size):
    return pl.CostEstimate(flops=flops, bytes_accessed=size, transcendentals=0)


def unpack_transfers(xfer_ref, xt):
    @pl.loop(0, H // TURN)
    def _(step):
        at = [step * TURN + v for v in range(TURN)]
        turned = [jnp.concatenate([xfer_ref[:, q, :], xfer_ref[:, q + H, :]], axis=0).T for q in at]
        for q, y in zip(at, turned):
            xt[:, q, :] = y


def cholesky_lanes(a):
    sub = lax.broadcasted_iota(jnp.int32, (8, a.shape[2]), 0)

    def cols(block):
        return pl.ds(pl.multiple_of(8 * block, 8), 8)

    for panel in range(K // 8):
        base = 8 * panel
        scale = []
        rows = [a[base + k, pl.ds(base, 8), :] for k in range(8)]
        for k in range(8):
            scale.append(lax.rsqrt(rows[k][k : k + 1, :]))
            rows[k] = rows[k] * scale[k]
            for i in range(k + 1, 8):
                rows[i] = rows[i] - rows[k][i : i + 1, :] * rows[k]
        for k in range(8):
            a[base + k, pl.ds(base, 8), :] = jnp.where(sub >= k, rows[k], 0.0)
        for j in range(panel + 1, K // 8):
            new = []
            for k in range(8):
                acc = a[base + k, pl.ds(8 * j, 8), :]
                for p in range(k):
                    acc = acc - rows[p][k : k + 1, :] * new[p]
                new.append(acc * scale[k])
            for k in range(8):
                a[base + k, pl.ds(8 * j, 8), :] = new[k]
        if panel < K // 8 - 1:

            @pl.loop(panel + 1, K // 8)
            def _(i_block):
                left = [a[base + k, cols(i_block), :] for k in range(8)]

                @pl.loop(i_block, K // 8)
                def _(j_block):
                    right = [a[base + k, cols(j_block), :] for k in range(8)]
                    for i in range(8):
                        acc = a[8 * i_block + i, cols(j_block), :]
                        for k in range(8):
                            acc = acc - left[k][i : i + 1, :] * right[k]
                        a[8 * i_block + i, cols(j_block), :] = acc

    for i in range(8, K):
        a[i, pl.ds(0, i // 8 * 8), :] = jnp.zeros((i // 8 * 8, a.shape[2]), F32)


def factor_halved(s, a):
    @pl.loop(0, H // TURN)
    def _(step):
        at = [step * TURN + v for v in range(TURN)]
        turned = [s[:, q, :].T for q in at]
        for q, y in zip(at, turned):
            a[q] = y[:K]
            a[q + H] = y[K:]

    cholesky_lanes(a)

    @pl.loop(0, H // TURN)
    def _(step):
        at = [step * TURN + v for v in range(TURN)]
        turned = [jnp.concatenate([a[q], a[q + H]], axis=0).T for q in at]
        for q, y in zip(at, turned):
            s[:, q, :] = y


def lane(low, high):
    at = lax.broadcasted_iota(jnp.int32, (Q, 2 * K), 1)
    return (at >= low) & (at < high)


def pack(four):
    top = [x[:Q] for x in four]
    low = [jnp.where(lane(0, Q), pltpu.roll(x[Q:], Q, 1), x[Q:]) for x in four]
    gap = lane(K, K + H)
    return jnp.concatenate(
        [
            jnp.where(gap, pltpu.roll(top[3], K, 1), top[0]),
            jnp.where(gap, pltpu.roll(top[3], H, 1), top[1]),
            jnp.where(gap, pltpu.roll(top[3], 2 * K - H, 1), top[2]),
            jnp.where(lane(0, K), low[0], pltpu.roll(low[1], K, 1)),
            jnp.where(lane(0, K), low[2], pltpu.roll(low[3], K, 1)),
        ],
        axis=0,
    )


def unpack(x):
    unit = [x[Q * n : Q * (n + 1)] for n in range(5)]
    full = []
    for m in range(3):
        full.append((unit[m], jnp.where(lane(H, K), pltpu.roll(unit[m], K, 1), 0.0)))
    first = jnp.where(lane(0, H), pltpu.roll(unit[0], K, 1), pltpu.roll(unit[1], 2 * K - H, 1))
    full.append((first, jnp.where(lane(H, K), pltpu.roll(unit[2], 2 * K - H, 1), 0.0)))
    out = []
    for m, (block0, block2) in enumerate(full):
        low = unit[3 + m // 2] if m % 2 == 0 else pltpu.roll(unit[3 + m // 2], K, 1)
        block1 = jnp.where(lane(Q, K), low, 0.0)
        block3 = jnp.where(lane(K - Q, K), pltpu.roll(low, K - Q, 1), 0.0)
        out.append(jnp.concatenate([block0, block1, block2, block3], axis=0)[:, :K])
    return out


def factor_kernel(own, cols, at_ref, basis_ref, xfer_ref, fac_ref, sent_ref, gram1_ref, xt, s, a):
    col = at_ref[1]
    first = col * own
    unpack_transfers(xfer_ref, xt)

    pairs = min(PAIRS, own // 2)

    @pl.loop(0, own // 2 // pairs)
    def _(step):
        base = step * pairs
        at = [2 * base + c for c in range(2 * pairs)]
        points = [basis_ref[c] for c in at]
        grams = [mul(x, x, NT) for x in points]
        parents = lift_pairs(grams, [unhalf(xt[first + c]) for c in at])
        for c, gram in zip(at, grams):
            s[c] = halve(gram)
        for p, gram in enumerate(parents):
            gram1_ref[base + p] = gram
            s[own + base + p] = halve(gram)

    factor_halved(s, a)
    count = own + own // 2
    for g in range(count // 4):
        fac_ref[g] = pack([s[4 * g + m] for m in range(4)]).astype(BF)
    for e in range(cols):
        for r in range(count // cols):
            sent_ref[e, r] = s[r * cols + jnp.bitwise_xor(col, e)].astype(BF)


def own_factors(at, basis, xfer_lanes, cols):
    own = basis.shape[0]
    count = own + own // 2
    rows = (count + 7) // 8 * 8
    shapes = (
        jax.ShapeDtypeStruct((count // 4, 5 * Q, 2 * K), BF),
        jax.ShapeDtypeStruct((cols, count // cols, H, 2 * K), BF),
        jax.ShapeDtypeStruct((own // 2, K, K), F32),
    )
    return pl.pallas_call(
        functools.partial(factor_kernel, own, cols),
        out_shape=shapes,
        grid=(1,),
        in_specs=[
            SMEM,
            pl.BlockSpec(basis.shape, lambda i: (0, 0, 0)),
            pl.BlockSpec((K, K, LANES), lambda i: (0, 0, 0)),
        ],
        out_specs=tuple(
            pl.BlockSpec(x.shape, lambda i, rank=len(x.shape): (0,) * rank) for x in shapes
        ),
        scratch_shapes=[
            pltpu.VMEM((LANES, H, 2 * K), F32),
            pltpu.VMEM((rows, H, 2 * K), F32),
            pltpu.VMEM((K, K, rows), F32),
        ],
        compiler_params=PARAMS,
        cost_estimate=cost(own * 2**24, 2**23),
    )(at, basis, xfer_lanes)


def chain_kernel(own, cols, at_ref, gram1_ref, xfer_ref, out_ref, xt):
    col = at_ref[1]
    unpack_transfers(xfer_ref, xt)
    grams = [gram1_ref[c] for c in range(own // 2)]
    offset = 0
    width = own * cols // 2
    while len(grams) > 1:
        here = len(grams)
        first = offset + col * here
        grams = lift_pairs(grams, [unhalf(xt[first + c]) for c in range(here)])
        offset += width
        width //= 2
    shift = 0
    while width >= 1:
        grams = lift_all(grams, [unhalf(xt[offset + jnp.right_shift(col, shift)])])
        offset += width
        width //= 2
        shift += 1
    out_ref[...] = halve(grams[0])


def lifted_root(at, gram1, xfer_lanes, own, cols):
    return pl.pallas_call(
        functools.partial(chain_kernel, own, cols),
        out_shape=jax.ShapeDtypeStruct((H, 2 * K), F32),
        grid=(1,),
        in_specs=[
            SMEM,
            pl.BlockSpec(gram1.shape, lambda i: (0, 0, 0)),
            pl.BlockSpec((K, K, LANES), lambda i: (0, 0, 1)),
        ],
        out_specs=pl.BlockSpec((H, 2 * K), lambda i: (0, 0)),
        scratch_shapes=[pltpu.VMEM((LANES, H, 2 * K), F32)],
        compiler_params=PARAMS,
        cost_estimate=cost(own * 2**24, 2**22),
    )(at, gram1, xfer_lanes)


def top_kernel(leaves, at_ref, top_ref, *refs):
    pairs = leaves // 2
    parts, (anc_ref, root_ref, level_ref, s, a) = refs[:pairs], refs[pairs:]
    pair = jnp.right_shift(at_ref[0], 1)
    for m in range(pairs):
        level_ref[jnp.bitwise_xor(pair, m)] = parts[m][...]
    level = [unhalf(level_ref[m]) for m in range(pairs)]
    heights = []
    slot = 0
    off_top = 0
    while True:
        heights.append(slot)
        for m, gram in enumerate(level):
            s[slot + m] = halve(gram)
        slot += len(level)
        if len(level) == 1:
            break
        level_xfers = [top_ref[off_top + m].T for m in range(len(level))]
        off_top += len(level)
        level = lift_pairs(level, level_xfers)
    factor_halved(s, a)
    for h, start in enumerate(heights):
        anc_ref[0, h] = unhalf(s[start + jnp.right_shift(at_ref[0], h + 1)])
    root_ref[...] = unhalf(s[heights[-1]])


def top_factors(at, parts, top_transfer, leaves):
    height = leaves.bit_length() - 1
    rows = (leaves - 1 + 7) // 8 * 8
    return pl.pallas_call(
        functools.partial(top_kernel, leaves),
        out_shape=(
            jax.ShapeDtypeStruct((1, height, K, K), F32),
            jax.ShapeDtypeStruct((K, K), F32),
        ),
        in_specs=[SMEM, VMEM] + [VMEM] * len(parts),
        out_specs=(VMEM, VMEM),
        scratch_shapes=[
            pltpu.VMEM((leaves // 2, H, 2 * K), F32),
            pltpu.VMEM((rows, H, 2 * K), F32),
            pltpu.VMEM((K, K, rows), F32),
        ],
        compiler_params=PARAMS,
        cost_estimate=cost(2**22, 2**17),
    )(at, top_transfer, *parts)


def lane_groups(sizes):
    return [(which, lane) for which, size in enumerate(sizes) for lane in range(0, size, LANES)]


def turn_kernel(groups, *refs):
    blocks, cells_ref, bt = refs[:-2], refs[-2], refs[-1]
    for g, (which, first) in enumerate(groups):
        src = blocks[which]

        @pl.loop(0, H // TURN)
        def _(step):
            lanes = pl.ds(first, LANES)
            at = [step * TURN + v for v in range(TURN)]
            x = [jnp.concatenate([src[q, :, lanes], src[q + H, :, lanes]], axis=0) for q in at]
            turned = [y.astype(F32).T for y in x]
            for q, y in zip(at, turned):
                bt[:, q, :] = y

        cells_ref[pl.ds(LANES * g, LANES)] = bt[...].astype(BF)


def turned_blocks(blocks):
    groups = lane_groups([x.shape[2] for x in blocks])
    return pl.pallas_call(
        functools.partial(turn_kernel, groups),
        out_shape=jax.ShapeDtypeStruct((LANES * len(groups), H, 2 * K), BF),
        in_specs=[VMEM] * len(blocks),
        out_specs=VMEM,
        scratch_shapes=[pltpu.VMEM((LANES, H, 2 * K), F32)],
        compiler_params=PARAMS,
        cost_estimate=cost(2**20, 2**20),
    )(*blocks)


def middle_kernel(index_ref, cells_ref, same_ref, other_ref, out_ref):
    entries = same_ref.shape[0]

    @pl.loop(0, cells_ref.shape[0] // SLOTS)
    def _(step):
        at = [step * SLOTS + u for u in range(SLOTS)]
        cols = []
        for b in at:
            n = index_ref[b]
            there = n >= entries
            n = jnp.where(there, n - entries, n)
            cols.append(unhalf(jnp.where(there, other_ref[n], same_ref[n])))
        cells = [unhalf(cells_ref[b]) for b in at]
        y = [lax.dot_general(x, c, NT, preferred_element_type=F32) for x, c in zip(cells, cols)]
        y = [halve(z.astype(BF)) for z in y]
        for b, z in zip(at, y):
            out_ref[b] = z


def middle_products(index, cells, same_core, other_core):
    return pl.pallas_call(
        middle_kernel,
        out_shape=jax.ShapeDtypeStruct(cells.shape, BF),
        in_specs=[SMEM] + [VMEM] * 3,
        out_specs=VMEM,
        compiler_params=PARAMS,
        cost_estimate=cost(cells.shape[0] * 2**19, 2**20),
    )(index, cells, same_core, other_core)


def outer_kernel(groups, outs, index_ref, counts_ref, middle_ref, *refs):
    pieces, out_refs = refs[:-outs - 4], refs[-outs - 4 : -4]
    pt, table, ready, sem = refs[-4:]
    packs = pieces[0].shape[0]
    for e, piece in enumerate(pieces):

        @pl.loop(0, packs)
        def _(g):
            four = unpack(piece[g].astype(F32))
            for m in range(4):
                table[4 * (e * packs + g) + m] = four[m].astype(BF)

    copies = []
    for g, (which, first) in enumerate(groups):

        @pl.loop(0, LANES // SLOTS)
        def _(step):
            at = [step * SLOTS + u for u in range(SLOTS)]
            rows = [table[index_ref[LANES * g + b]] for b in at]
            right = [unhalf(middle_ref[LANES * g + b]) for b in at]
            y = [lax.dot_general(r, x, NN, preferred_element_type=F32) for r, x in zip(rows, right)]
            y = [halve(z) for z in y]
            for b, z in zip(at, y):
                pt[b] = z

        keep = lax.broadcasted_iota(jnp.int32, (2 * K, LANES), 1) < counts_ref[which] - first

        @pl.loop(0, H // TURN)
        def _(step):
            at = [step * TURN + v for v in range(TURN)]
            turned = [pt[:, q, :].T for q in at]
            for q, y in zip(at, turned):
                y = jnp.where(keep, y, 0.0).astype(BF)
                ready[g, q] = y[:K]
                ready[g, q + H] = y[K:]

        out = out_refs[which].at[:, :, pl.ds(first, LANES)]
        copies.append(pltpu.make_async_copy(ready.at[g], out, sem.at[g]))
        copies[-1].start()
    for copy in copies:
        copy.wait()


def outer_products(pieces, index, counts, middle, sizes):
    groups = lane_groups(sizes)
    entries = 4 * sum(x.shape[0] for x in pieces)
    return pl.pallas_call(
        functools.partial(outer_kernel, groups, len(sizes)),
        out_shape=tuple(jax.ShapeDtypeStruct((K, K, size), BF) for size in sizes),
        in_specs=[SMEM, SMEM, VMEM] + [VMEM] * len(pieces),
        out_specs=(ANY,) * len(sizes),
        scratch_shapes=[
            pltpu.VMEM((LANES, H, 2 * K), F32),
            pltpu.VMEM((entries, K, K), BF),
            pltpu.VMEM((len(groups), K, K, LANES), BF),
            pltpu.SemaphoreType.DMA((len(groups),)),
        ],
        compiler_params=PARAMS,
        cost_estimate=cost(len(groups) * 2**26, 2**22),
    )(index, counts, middle, *pieces)


def swapped(x, axis, d):
    return lax.ppermute(x, axis, [(i, i ^ d) for i in range(lax.axis_size(axis))])


def on_device(basis, transfer, top_transfer, blocks0, pairs0, counts0, blocks1, pairs1, counts1):
    own = basis.shape[0]
    cols = lax.axis_size("col")
    leaves = lax.axis_size("leaf")
    leaf, col = lax.axis_index("leaf"), lax.axis_index("col")
    at = jnp.stack([leaf, col]).astype(jnp.int32)
    xfer_lanes = jnp.transpose(transfer, (1, 2, 0))
    lanes0, lanes1 = jnp.transpose(blocks0, (1, 2, 0)), jnp.transpose(blocks1, (1, 2, 0))
    count = own + own // 2
    parts = count // cols

    def indices(pairs, level):
        size = own >> level
        row = pairs[:, 0] - leaf * (size * cols)
        row = (row // size ^ col) * count + level * own + row % size
        owner = pairs[:, 1] // size
        away = owner // cols ^ leaf
        piece = (away & 1) * (leaves // 2) + (away >> 1)
        column = (piece * cols + (owner % cols ^ col)) * parts
        return row, column + level * (own // cols) + pairs[:, 1] % size // cols

    row0, column0 = indices(pairs0, 0)
    row1, column1 = indices(pairs1, 1)

    factors, sent, gram1 = own_factors(at, basis, xfer_lanes, cols)
    received = [swapped(sent[d], "col", d) for d in range(1, cols)]
    gram = lifted_root(at, gram1, xfer_lanes, own, cols)
    cells = turned_blocks((lanes0, lanes1))
    received, gram, factors, cells = lax.optimization_barrier((received, gram, factors, cells))

    part = jnp.concatenate([sent[0]] + received, axis=0)
    chips = [swapped(part, "leaf", d) for d in range(2, leaves, 2)]
    row_pieces = [factors] + [swapped(factors, "col", d) for d in range(1, cols - 1)]
    for bit in range(cols.bit_length() - 1):
        gram = gram + swapped(gram, "col", 1 << bit)
    gram = gram + swapped(gram, "leaf", 1)
    chips, row_pieces, gram = lax.optimization_barrier((chips, row_pieces, gram))

    row_pieces = row_pieces + [swapped(factors, "col", cols - 1)]
    same_core = jnp.concatenate([part] + chips, axis=0)
    other_core = swapped(same_core, "leaf", 1)
    tops = [gram] + [swapped(gram, "leaf", d) for d in range(2, leaves, 2)]
    ancestors, root = top_factors(at, tops, top_transfer, leaves)

    middle = middle_products(jnp.concatenate([column0, column1]), cells, same_core, other_core)
    out0, out1 = outer_products(
        row_pieces,
        jnp.concatenate([row0, row1]),
        jnp.concatenate([counts0, counts1]),
        middle,
        (blocks0.shape[0], blocks1.shape[0]),
    )
    return (jnp.transpose(out0, (2, 0, 1)), jnp.transpose(out1, (2, 0, 1)), root, ancestors)


def solution(mesh):
    in_specs = (
        P(("leaf", "col"), None, None),
        P("leaf", None, None),
        P(),
        P(("leaf", "col"), None, None),
        P(("leaf", "col"), None),
        P(("leaf", "col")),
        P(("leaf", "col"), None, None),
        P(("leaf", "col"), None),
        P(("leaf", "col")),
    )
    out_specs = (
        P(("leaf", "col"), None, None),
        P(("leaf", "col"), None, None),
        P(),
        P("leaf", None, None, None),
    )
    return jax.shard_map(
        on_device, mesh=mesh, in_specs=in_specs, out_specs=out_specs, check_vma=False
    )
```

```python
import functools
import math

import jax
import jax.numpy as jnp
from jax import lax
from jax.experimental import pallas as pl
from jax.experimental.pallas import tpu as pltpu
from jax.sharding import PartitionSpec as P

BF, F32 = jnp.bfloat16, jnp.float32
EXACT = lax.Precision.HIGHEST
NT = (((1,), (1,)), ((), ()))
NN = (((1,), (0,)), ((), ()))
K = 64
H = K // 2
Q = K // 4
LANES = 128
SMEM = pl.BlockSpec(memory_space=pltpu.SMEM)
VMEM = pl.BlockSpec(memory_space=pltpu.VMEM)
ANY = pl.BlockSpec(memory_space=pl.ANY)
HBM = pl.BlockSpec(memory_space=pltpu.HBM)
TERMS = 3
TURN = 8
SLOTS = 64
PAIRS = 4
PARAMS = pltpu.CompilerParams(vmem_limit_bytes=24 * 2**20)


def unhalf(x):
    return jnp.concatenate([x[:, :K], x[:, K:]], axis=0)


def halve(x):
    return jnp.concatenate([x[:H], x[H:]], axis=1)


def mul(x, y, dims):
    return lax.dot_general(x, y, dims, precision=EXACT, preferred_element_type=F32)


def lift_all(grams, xfers_t):
    halfway = [mul(f, g, NN) for f, g in zip(xfers_t, grams)]
    return [mul(t, f, NT) for t, f in zip(halfway, xfers_t)]


def lift_pairs(grams, xfers_t):
    lifted = lift_all(grams, xfers_t)
    return [low + high for low, high in zip(lifted[0::2], lifted[1::2])]


def cost(flops, size):
    return pl.CostEstimate(flops=flops, bytes_accessed=size, transcendentals=0)


def unpack_transfers(xfer_ref, xt):
    @pl.loop(0, H // TURN)
    def _(step):
        at = [step * TURN + v for v in range(TURN)]
        turned = [jnp.concatenate([xfer_ref[:, q, :], xfer_ref[:, q + H, :]], axis=0).T for q in at]
        for q, y in zip(at, turned):
            xt[:, q, :] = y


def cholesky_lanes(a):
    sub = lax.broadcasted_iota(jnp.int32, (8, a.shape[2]), 0)

    def cols(block):
        return pl.ds(pl.multiple_of(8 * block, 8), 8)

    for panel in range(K // 8):
        base = 8 * panel
        scale = []
        rows = [a[base + k, pl.ds(base, 8), :] for k in range(8)]
        for k in range(8):
            scale.append(lax.rsqrt(rows[k][k : k + 1, :]))
            rows[k] = rows[k] * scale[k]
            for i in range(k + 1, 8):
                rows[i] = rows[i] - rows[k][i : i + 1, :] * rows[k]
        for k in range(8):
            a[base + k, pl.ds(base, 8), :] = jnp.where(sub >= k, rows[k], 0.0)
        for j in range(panel + 1, K // 8):
            new = []
            for k in range(8):
                acc = a[base + k, pl.ds(8 * j, 8), :]
                for p in range(k):
                    acc = acc - rows[p][k : k + 1, :] * new[p]
                new.append(acc * scale[k])
            for k in range(8):
                a[base + k, pl.ds(8 * j, 8), :] = new[k]
        if panel < K // 8 - 1:

            @pl.loop(panel + 1, K // 8)
            def _(i_block):
                left = [a[base + k, cols(i_block), :] for k in range(8)]

                @pl.loop(i_block, K // 8)
                def _(j_block):
                    right = [a[base + k, cols(j_block), :] for k in range(8)]
                    for i in range(8):
                        acc = a[8 * i_block + i, cols(j_block), :]
                        for k in range(8):
                            acc = acc - left[k][i : i + 1, :] * right[k]
                        a[8 * i_block + i, cols(j_block), :] = acc

    for i in range(8, K):
        a[i, pl.ds(0, i // 8 * 8), :] = jnp.zeros((i // 8 * 8, a.shape[2]), F32)


def factor_halved(s, a):
    @pl.loop(0, H // TURN)
    def _(step):
        at = [step * TURN + v for v in range(TURN)]
        turned = [s[:, q, :].T for q in at]
        for q, y in zip(at, turned):
            a[q] = y[:K]
            a[q + H] = y[K:]

    cholesky_lanes(a)

    @pl.loop(0, H // TURN)
    def _(step):
        at = [step * TURN + v for v in range(TURN)]
        turned = [jnp.concatenate([a[q], a[q + H]], axis=0).T for q in at]
        for q, y in zip(at, turned):
            s[:, q, :] = y


def lane(low, high):
    at = lax.broadcasted_iota(jnp.int32, (Q, 2 * K), 1)
    return (at >= low) & (at < high)


def pack(four):
    top = [x[:Q] for x in four]
    low = [jnp.where(lane(0, Q), pltpu.roll(x[Q:], Q, 1), x[Q:]) for x in four]
    gap = lane(K, K + H)
    return jnp.concatenate(
        [
            jnp.where(gap, pltpu.roll(top[3], K, 1), top[0]),
            jnp.where(gap, pltpu.roll(top[3], H, 1), top[1]),
            jnp.where(gap, pltpu.roll(top[3], 2 * K - H, 1), top[2]),
            jnp.where(lane(0, K), low[0], pltpu.roll(low[1], K, 1)),
            jnp.where(lane(0, K), low[2], pltpu.roll(low[3], K, 1)),
        ],
        axis=0,
    )


def unpack(x):
    unit = [x[Q * n : Q * (n + 1)] for n in range(5)]
    full = []
    for m in range(3):
        full.append((unit[m], jnp.where(lane(H, K), pltpu.roll(unit[m], K, 1), 0.0)))
    first = jnp.where(lane(0, H), pltpu.roll(unit[0], K, 1), pltpu.roll(unit[1], 2 * K - H, 1))
    full.append((first, jnp.where(lane(H, K), pltpu.roll(unit[2], 2 * K - H, 1), 0.0)))
    out = []
    for m, (block0, block2) in enumerate(full):
        low = unit[3 + m // 2] if m % 2 == 0 else pltpu.roll(unit[3 + m // 2], K, 1)
        block1 = jnp.where(lane(Q, K), low, 0.0)
        block3 = jnp.where(lane(K - Q, K), pltpu.roll(low, K - Q, 1), 0.0)
        out.append(jnp.concatenate([block0, block1, block2, block3], axis=0)[:, :K])
    return out


def factor_kernel(
    own,
    cols,
    at_ref,
    all_basis_ref,
    all_xfer_ref,
    fac_ref,
    sent_ref,
    gram1_ref,
    xt,
    s,
    a,
    g0,
    basis_ref,
    xfer_ref,
    basis_sem,
    sem,
):
    col = at_ref[1]
    first = col * own
    pairs = min(PAIRS, own // 2)

    def chunk(step):
        rows = pl.ds(2 * pairs * step, 2 * pairs)
        return pltpu.make_async_copy(all_basis_ref.at[rows], basis_ref.at[rows], basis_sem.at[step])

    for step in range(own // 2 // pairs):
        chunk(step).start()
    copy = pltpu.make_async_copy(all_xfer_ref.at[:, :, pl.ds(0, LANES)], xfer_ref, sem)
    copy.start()

    @pl.loop(0, own // 2 // pairs)
    def _(step):
        chunk(step).wait()
        at = [2 * step * pairs + c for c in range(2 * pairs)]
        points = [basis_ref[c] for c in at]
        grams = [mul(x, x, NT) for x in points]
        for c, gram in zip(at, grams):
            g0[c] = gram
            s[c] = halve(gram)

    copy.wait()
    unpack_transfers(xfer_ref, xt)

    @pl.loop(0, own // 2 // pairs)
    def _(step):
        base = step * pairs
        at = [2 * base + c for c in range(2 * pairs)]
        parents = lift_pairs([g0[c] for c in at], [unhalf(xt[first + c]) for c in at])
        for p, gram in enumerate(parents):
            gram1_ref[base + p] = gram
            s[own + base + p] = halve(gram)

    factor_halved(s, a)
    count = own + own // 2
    for g in range(count // 4):
        fac_ref[g] = pack([s[4 * g + m] for m in range(4)]).astype(BF)
    for e in range(cols):
        for r in range(count // cols):
            sent_ref[e, r] = s[r * cols + jnp.bitwise_xor(col, e)].astype(BF)


def own_factors(at, basis, xfer_lanes, cols):
    own = basis.shape[0]
    count = own + own // 2
    rows = (count + 7) // 8 * 8
    shapes = (
        jax.ShapeDtypeStruct((count // 4, 5 * Q, 2 * K), BF),
        jax.ShapeDtypeStruct((cols, count // cols, H, 2 * K), BF),
        jax.ShapeDtypeStruct((own // 2, K, K), F32),
    )
    return pl.pallas_call(
        functools.partial(factor_kernel, own, cols),
        out_shape=shapes,
        in_specs=[
            SMEM,
            HBM,
            HBM,
        ],
        out_specs=(VMEM,) * len(shapes),
        scratch_shapes=[
            pltpu.VMEM((LANES, H, 2 * K), F32),
            pltpu.VMEM((rows, H, 2 * K), F32),
            pltpu.VMEM((K, K, rows), F32),
            pltpu.VMEM((own, K, K), F32),
            pltpu.VMEM(basis.shape, F32),
            pltpu.VMEM((K, K, LANES), F32),
            pltpu.SemaphoreType.DMA((own // 2 // min(PAIRS, own // 2),)),
            pltpu.SemaphoreType.DMA,
        ],
        compiler_params=pltpu.CompilerParams(vmem_limit_bytes=52 * 2**20),
        cost_estimate=cost(own * 2**24, 2**23),
    )(at, basis, xfer_lanes)


def chain_kernel(own, cols, at_ref, gram1_ref, xfer_ref, out_ref, xt):
    col = at_ref[1]
    unpack_transfers(xfer_ref, xt)
    grams = [gram1_ref[c] for c in range(own // 2)]
    offset = 0
    width = own * cols // 2
    while len(grams) > 1:
        here = len(grams)
        first = offset + col * here
        grams = lift_pairs(grams, [unhalf(xt[first + c]) for c in range(here)])
        offset += width
        width //= 2
    shift = 0
    while width >= 1:
        grams = lift_all(grams, [unhalf(xt[offset + jnp.right_shift(col, shift)])])
        offset += width
        width //= 2
        shift += 1
    rest = halve(grams[0])
    for n in range(TERMS):
        term = rest.astype(BF)
        out_ref[n] = term
        rest = rest - term.astype(F32)


def lifted_root(at, gram1, xfer_lanes, own, cols):
    return pl.pallas_call(
        functools.partial(chain_kernel, own, cols),
        out_shape=jax.ShapeDtypeStruct((TERMS, H, 2 * K), BF),
        grid=(1,),
        in_specs=[
            SMEM,
            pl.BlockSpec(gram1.shape, lambda i: (0, 0, 0)),
            pl.BlockSpec((K, K, LANES), lambda i: (0, 0, 1)),
        ],
        out_specs=pl.BlockSpec((TERMS, H, 2 * K), lambda i: (0, 0, 0)),
        scratch_shapes=[pltpu.VMEM((LANES, H, 2 * K), F32)],
        compiler_params=PARAMS,
        cost_estimate=cost(own * 2**24, 2**22),
    )(at, gram1, xfer_lanes)


def top_kernel(leaves, at_ref, top_ref, *refs):
    pairs = leaves // 2
    parts, (anc_ref, root_ref, level_ref, s, a) = refs[:-5], refs[-5:]
    pair = jnp.right_shift(at_ref[0], 1)
    for m in range(pairs):
        terms = [part[m] for part in parts]
        while len(terms) > 1:
            terms = [x + y for x, y in zip(terms[0::2], terms[1::2])]
        level_ref[jnp.bitwise_xor(pair, m)] = terms[0]
    level = [unhalf(level_ref[m]) for m in range(pairs)]
    heights = []
    slot = 0
    off_top = 0
    while True:
        heights.append(slot)
        for m, gram in enumerate(level):
            s[slot + m] = halve(gram)
        slot += len(level)
        if len(level) == 1:
            break
        level_xfers = [top_ref[off_top + m].T for m in range(len(level))]
        off_top += len(level)
        level = lift_pairs(level, level_xfers)
    factor_halved(s, a)
    for h, start in enumerate(heights):
        anc_ref[0, h] = unhalf(s[start + jnp.right_shift(at_ref[0], h + 1)])
    root_ref[...] = unhalf(s[heights[-1]])


def top_factors(at, parts, top_transfer, leaves):
    height = leaves.bit_length() - 1
    rows = (leaves - 1 + 7) // 8 * 8
    return pl.pallas_call(
        functools.partial(top_kernel, leaves),
        out_shape=(
            jax.ShapeDtypeStruct((1, height, K, K), F32),
            jax.ShapeDtypeStruct((K, K), F32),
        ),
        in_specs=[SMEM, VMEM] + [VMEM] * len(parts),
        out_specs=(VMEM, VMEM),
        scratch_shapes=[
            pltpu.VMEM((leaves // 2, H, 2 * K), F32),
            pltpu.VMEM((rows, H, 2 * K), F32),
            pltpu.VMEM((K, K, rows), F32),
        ],
        compiler_params=PARAMS,
        cost_estimate=cost(2**22, 2**17),
    )(at, top_transfer, *parts)


def lane_groups(sizes):
    return [(which, lane) for which, size in enumerate(sizes) for lane in range(0, size, LANES)]


def turn_kernel(groups, *refs):
    blocks, cells_ref, bt = refs[:-2], refs[-2], refs[-1]
    for g, (which, first) in enumerate(groups):
        src = blocks[which]

        @pl.loop(0, H // TURN)
        def _(step):
            lanes = pl.ds(first, LANES)
            at = [step * TURN + v for v in range(TURN)]
            x = [jnp.concatenate([src[q, :, lanes], src[q + H, :, lanes]], axis=0) for q in at]
            turned = [y.astype(F32).T for y in x]
            for q, y in zip(at, turned):
                bt[:, q, :] = y

        cells_ref[pl.ds(LANES * g, LANES)] = bt[...].astype(BF)


def turned_blocks(blocks):
    groups = lane_groups([x.shape[2] for x in blocks])
    return pl.pallas_call(
        functools.partial(turn_kernel, groups),
        out_shape=jax.ShapeDtypeStruct((LANES * len(groups), H, 2 * K), BF),
        in_specs=[VMEM] * len(blocks),
        out_specs=VMEM,
        scratch_shapes=[pltpu.VMEM((LANES, H, 2 * K), F32)],
        compiler_params=PARAMS,
        cost_estimate=cost(2**20, 2**20),
    )(*blocks)


def middle_kernel(index_ref, cells_ref, same_ref, other_ref, out_ref):
    entries = same_ref.shape[0]

    @pl.loop(0, cells_ref.shape[0] // SLOTS)
    def _(step):
        at = [step * SLOTS + u for u in range(SLOTS)]
        cols = []
        for b in at:
            n = index_ref[b]
            there = n >= entries
            n = jnp.where(there, n - entries, n)
            cols.append(unhalf(jnp.where(there, other_ref[n], same_ref[n])))
        cells = [unhalf(cells_ref[b]) for b in at]
        y = [lax.dot_general(x, c, NT, preferred_element_type=F32) for x, c in zip(cells, cols)]
        y = [halve(z.astype(BF)) for z in y]
        for b, z in zip(at, y):
            out_ref[b] = z


def middle_products(index, cells, same_core, other_core):
    return pl.pallas_call(
        middle_kernel,
        out_shape=jax.ShapeDtypeStruct(cells.shape, BF),
        in_specs=[SMEM] + [VMEM] * 3,
        out_specs=VMEM,
        compiler_params=PARAMS,
        cost_estimate=cost(cells.shape[0] * 2**19, 2**20),
    )(index, cells, same_core, other_core)


def outer_kernel(groups, outs, index_ref, counts_ref, middle_ref, *refs):
    pieces, out_refs = refs[:-outs - 4], refs[-outs - 4 : -4]
    pt, table, ready, sem = refs[-4:]
    packs = pieces[0].shape[0]
    together = math.gcd(packs, 6)
    for e, piece in enumerate(pieces):

        @pl.loop(0, packs // together)
        def _(step):
            at = [step * together + g for g in range(together)]
            full = [unpack(piece[g].astype(F32)) for g in at]
            for g, four in zip(at, full):
                for m in range(4):
                    table[4 * (e * packs + g) + m] = four[m].astype(BF)

    copies = []
    for g, (which, first) in enumerate(groups):

        @pl.loop(0, LANES // SLOTS)
        def _(step):
            at = [step * SLOTS + u for u in range(SLOTS)]
            rows = [table[index_ref[LANES * g + b]] for b in at]
            right = [unhalf(middle_ref[LANES * g + b]) for b in at]
            y = [lax.dot_general(r, x, NN, preferred_element_type=F32) for r, x in zip(rows, right)]
            y = [halve(z) for z in y]
            for b, z in zip(at, y):
                pt[b] = z

        keep = lax.broadcasted_iota(jnp.int32, (2 * K, LANES), 1) < counts_ref[which] - first

        @pl.loop(0, H // TURN)
        def _(step):
            at = [step * TURN + v for v in range(TURN)]
            turned = [pt[:, q, :].T for q in at]
            for q, y in zip(at, turned):
                y = jnp.where(keep, y, 0.0).astype(BF)
                ready[g, q] = y[:K]
                ready[g, q + H] = y[K:]

        out = out_refs[which].at[:, :, pl.ds(first, LANES)]
        copies.append(pltpu.make_async_copy(ready.at[g], out, sem.at[g]))
        copies[-1].start()
    for copy in copies:
        copy.wait()


def outer_products(pieces, index, counts, middle, sizes):
    groups = lane_groups(sizes)
    entries = 4 * sum(x.shape[0] for x in pieces)
    return pl.pallas_call(
        functools.partial(outer_kernel, groups, len(sizes)),
        out_shape=tuple(jax.ShapeDtypeStruct((K, K, size), BF) for size in sizes),
        in_specs=[SMEM, SMEM, VMEM] + [VMEM] * len(pieces),
        out_specs=(ANY,) * len(sizes),
        scratch_shapes=[
            pltpu.VMEM((LANES, H, 2 * K), F32),
            pltpu.VMEM((entries, K, K), BF),
            pltpu.VMEM((len(groups), K, K, LANES), BF),
            pltpu.SemaphoreType.DMA((len(groups),)),
        ],
        compiler_params=PARAMS,
        cost_estimate=cost(len(groups) * 2**26, 2**22),
    )(index, counts, middle, *pieces)


def swapped(x, axis, d):
    return lax.ppermute(x, axis, [(i, i ^ d) for i in range(lax.axis_size(axis))])


def on_device(basis, transfer, top_transfer, blocks0, pairs0, counts0, blocks1, pairs1, counts1):
    own = basis.shape[0]
    cols = lax.axis_size("col")
    leaves = lax.axis_size("leaf")
    leaf, col = lax.axis_index("leaf"), lax.axis_index("col")
    at = jnp.stack([leaf, col]).astype(jnp.int32)
    xfer_lanes = jnp.transpose(transfer, (1, 2, 0))
    lanes0, lanes1 = jnp.transpose(blocks0, (1, 2, 0)), jnp.transpose(blocks1, (1, 2, 0))
    count = own + own // 2
    parts = count // cols

    def indices(pairs, level):
        size = own >> level
        row = pairs[:, 0] - leaf * (size * cols)
        row = (row // size ^ col) * count + level * own + row % size
        owner = pairs[:, 1] // size
        away = owner // cols ^ leaf
        piece = (away & 1) * (leaves // 2) + (away >> 1)
        column = piece * (count + TERMS) + (owner % cols ^ col) * parts
        return row, column + level * (own // cols) + pairs[:, 1] % size // cols

    row0, column0 = indices(pairs0, 0)
    row1, column1 = indices(pairs1, 1)

    factors, sent, gram1 = own_factors(at, basis, xfer_lanes, cols)
    received = [swapped(sent[d], "col", d) for d in range(1, cols)]
    terms = lifted_root(at, gram1, xfer_lanes, own, cols)
    received, terms, factors, lanes0, lanes1 = lax.optimization_barrier(
        (received, terms, factors, lanes0, lanes1)
    )

    part = jnp.concatenate([sent[0]] + received + [terms], axis=0)
    chips = [swapped(part, "leaf", d) for d in range(2, leaves, 2)]
    row_pieces = [factors] + [swapped(factors, "col", d) for d in range(1, cols - 1)]
    cells = turned_blocks((lanes0, lanes1))
    chips, row_pieces, cells = lax.optimization_barrier((chips, row_pieces, cells))

    row_pieces = row_pieces + [swapped(factors, "col", cols - 1)]
    same_core = jnp.concatenate([part] + chips, axis=0)
    other_core = swapped(same_core, "leaf", 1)

    def sums(x):
        return x.reshape(leaves // 2, count + TERMS, H, 2 * K)[:, count:].astype(F32).sum(axis=1)

    pair_part = sums(same_core) + sums(other_core)
    tops = [pair_part] + [swapped(pair_part, "col", d) for d in range(1, cols)]
    ancestors, root = top_factors(at, tops, top_transfer, leaves)

    middle = middle_products(jnp.concatenate([column0, column1]), cells, same_core, other_core)
    out0, out1 = outer_products(
        row_pieces,
        jnp.concatenate([row0, row1]),
        jnp.concatenate([counts0, counts1]),
        middle,
        (blocks0.shape[0], blocks1.shape[0]),
    )
    return (jnp.transpose(out0, (2, 0, 1)), jnp.transpose(out1, (2, 0, 1)), root, ancestors)


def solution(mesh):
    in_specs = (
        P(("leaf", "col"), None, None),
        P("leaf", None, None),
        P(),
        P(("leaf", "col"), None, None),
        P(("leaf", "col"), None),
        P(("leaf", "col")),
        P(("leaf", "col"), None, None),
        P(("leaf", "col"), None),
        P(("leaf", "col")),
    )
    out_specs = (
        P(("leaf", "col"), None, None),
        P(("leaf", "col"), None, None),
        P(),
        P("leaf", None, None, None),
    )
    return jax.shard_map(
        on_device, mesh=mesh, in_specs=in_specs, out_specs=out_specs, check_vma=False
    )
```

```python
import functools
import math

import jax
import jax.numpy as jnp
from jax import lax
from jax.experimental import pallas as pl
from jax.experimental.pallas import tpu as pltpu
from jax.sharding import PartitionSpec as P

BF, F32 = jnp.bfloat16, jnp.float32
EXACT = lax.Precision.HIGHEST
NT = (((1,), (1,)), ((), ()))
NN = (((1,), (0,)), ((), ()))
K = 64
H = K // 2
Q = K // 4
LANES = 128
SMEM = pl.BlockSpec(memory_space=pltpu.SMEM)
VMEM = pl.BlockSpec(memory_space=pltpu.VMEM)
ANY = pl.BlockSpec(memory_space=pl.ANY)
HBM = pl.BlockSpec(memory_space=pltpu.HBM)
TERMS = 3
TURN = 8
SLOTS = 64
PAIRS = 4
PARAMS = pltpu.CompilerParams(vmem_limit_bytes=24 * 2**20)


def unhalf(x):
    return jnp.concatenate([x[:, :K], x[:, K:]], axis=0)


def halve(x):
    return jnp.concatenate([x[:H], x[H:]], axis=1)


def mul(x, y, dims):
    return lax.dot_general(x, y, dims, precision=EXACT, preferred_element_type=F32)


def lift_all(grams, xfers_t):
    halfway = [mul(f, g, NN) for f, g in zip(xfers_t, grams)]
    return [mul(t, f, NT) for t, f in zip(halfway, xfers_t)]


def lift_pairs(grams, xfers_t):
    lifted = lift_all(grams, xfers_t)
    return [low + high for low, high in zip(lifted[0::2], lifted[1::2])]


def cost(flops, size):
    return pl.CostEstimate(flops=flops, bytes_accessed=size, transcendentals=0)


def unpack_transfers(xfer_ref, xt):
    @pl.loop(0, H // TURN)
    def _(step):
        at = [step * TURN + v for v in range(TURN)]
        turned = [jnp.concatenate([xfer_ref[:, q, :], xfer_ref[:, q + H, :]], axis=0).T for q in at]
        for q, y in zip(at, turned):
            xt[:, q, :] = y


def cholesky_lanes(a):
    sub = lax.broadcasted_iota(jnp.int32, (8, a.shape[2]), 0)

    def cols(block):
        return pl.ds(8 * block, 8)

    for panel in range(K // 8):
        base = 8 * panel
        scale = []
        rows = [a[base + k, pl.ds(base, 8), :] for k in range(8)]
        for k in range(8):
            scale.append(lax.rsqrt(rows[k][k : k + 1, :]))
            rows[k] = rows[k] * scale[k]
            for i in range(k + 1, 8):
                rows[i] = rows[i] - rows[k][i : i + 1, :] * rows[k]
        for k in range(8):
            a[base + k, pl.ds(base, 8), :] = jnp.where(sub >= k, rows[k], 0.0)
        for j in range(panel + 1, K // 8):
            new = []
            for k in range(8):
                acc = a[base + k, pl.ds(8 * j, 8), :]
                for p in range(k):
                    acc = acc - rows[p][k : k + 1, :] * new[p]
                new.append(acc * scale[k])
            for k in range(8):
                a[base + k, pl.ds(8 * j, 8), :] = new[k]
        if panel < K // 8 - 1:

            for i_block in range(panel + 1, K // 8):
                left = [a[base + k, cols(i_block), :] for k in range(8)]

                for j_block in range(i_block, K // 8):
                    right = [a[base + k, cols(j_block), :] for k in range(8)]
                    for i in range(8):
                        acc = a[8 * i_block + i, cols(j_block), :]
                        for k in range(8):
                            acc = acc - left[k][i : i + 1, :] * right[k]
                        a[8 * i_block + i, cols(j_block), :] = acc

    for i in range(8, K):
        a[i, pl.ds(0, i // 8 * 8), :] = jnp.zeros((i // 8 * 8, a.shape[2]), F32)


def factor_halved(s, a):
    @pl.loop(0, H // TURN)
    def _(step):
        at = [step * TURN + v for v in range(TURN)]
        turned = [s[:, q, :].T for q in at]
        for q, y in zip(at, turned):
            a[q] = y[:K]
            a[q + H] = y[K:]

    cholesky_lanes(a)

    @pl.loop(0, H // TURN)
    def _(step):
        at = [step * TURN + v for v in range(TURN)]
        turned = [jnp.concatenate([a[q], a[q + H]], axis=0).T for q in at]
        for q, y in zip(at, turned):
            s[:, q, :] = y


def lane(low, high):
    at = lax.broadcasted_iota(jnp.int32, (Q, 2 * K), 1)
    return (at >= low) & (at < high)


def pack(four):
    top = [x[:Q] for x in four]
    low = [jnp.where(lane(0, Q), pltpu.roll(x[Q:], Q, 1), x[Q:]) for x in four]
    gap = lane(K, K + H)
    return jnp.concatenate(
        [
            jnp.where(gap, pltpu.roll(top[3], K, 1), top[0]),
            jnp.where(gap, pltpu.roll(top[3], H, 1), top[1]),
            jnp.where(gap, pltpu.roll(top[3], 2 * K - H, 1), top[2]),
            jnp.where(lane(0, K), low[0], pltpu.roll(low[1], K, 1)),
            jnp.where(lane(0, K), low[2], pltpu.roll(low[3], K, 1)),
        ],
        axis=0,
    )


def unpack(x):
    unit = [x[Q * n : Q * (n + 1)] for n in range(5)]
    full = []
    for m in range(3):
        full.append((unit[m], jnp.where(lane(H, K), pltpu.roll(unit[m], K, 1), 0.0)))
    first = jnp.where(lane(0, H), pltpu.roll(unit[0], K, 1), pltpu.roll(unit[1], 2 * K - H, 1))
    full.append((first, jnp.where(lane(H, K), pltpu.roll(unit[2], 2 * K - H, 1), 0.0)))
    out = []
    for m, (block0, block2) in enumerate(full):
        low = unit[3 + m // 2] if m % 2 == 0 else pltpu.roll(unit[3 + m // 2], K, 1)
        block1 = jnp.where(lane(Q, K), low, 0.0)
        block3 = jnp.where(lane(K - Q, K), pltpu.roll(low, K - Q, 1), 0.0)
        out.append(jnp.concatenate([block0, block1, block2, block3], axis=0)[:, :K])
    return out


def factor_kernel(
    own,
    cols,
    at_ref,
    all_basis_ref,
    all_xfer_ref,
    fac_ref,
    gram1_ref,
    *refs,
):
    sent_refs = refs[:cols]
    xt, s, a, g0, basis_ref, xfer_ref, basis_sem, sem = refs[cols:]
    col = at_ref[1]
    first = col * own
    pairs = min(PAIRS, own // 2)

    def chunk(step):
        rows = pl.ds(2 * pairs * step, 2 * pairs)
        return pltpu.make_async_copy(all_basis_ref.at[rows], basis_ref.at[rows], basis_sem.at[step])

    for step in range(own // 2 // pairs):
        chunk(step).start()
    copy = pltpu.make_async_copy(all_xfer_ref.at[:, :, pl.ds(0, LANES)], xfer_ref, sem)
    copy.start()

    @pl.loop(0, own // 2 // pairs)
    def _(step):
        chunk(step).wait()
        at = [2 * step * pairs + c for c in range(2 * pairs)]
        points = [basis_ref[c] for c in at]
        grams = [mul(x, x, NT) for x in points]
        for c, gram in zip(at, grams):
            g0[c] = gram
            s[c] = halve(gram)

    copy.wait()
    unpack_transfers(xfer_ref, xt)

    @pl.loop(0, own // 2 // pairs)
    def _(step):
        base = step * pairs
        at = [2 * base + c for c in range(2 * pairs)]
        parents = lift_pairs([g0[c] for c in at], [unhalf(xt[first + c]) for c in at])
        for p, gram in enumerate(parents):
            gram1_ref[base + p] = gram
            s[own + base + p] = halve(gram)

    factor_halved(s, a)
    count = own + own // 2
    for g in range(count // 4):
        fac_ref[g] = pack([s[4 * g + m] for m in range(4)]).astype(BF)
    for e in range(cols):
        for r in range(count // cols):
            sent_refs[e][r] = s[r * cols + jnp.bitwise_xor(col, e)].astype(BF)


def own_factors(at, basis, xfer_lanes, cols):
    own = basis.shape[0]
    count = own + own // 2
    rows = (count + 7) // 8 * 8
    shapes = (
        jax.ShapeDtypeStruct((count // 4, 5 * Q, 2 * K), BF),
        jax.ShapeDtypeStruct((own // 2, K, K), F32),
    ) + (jax.ShapeDtypeStruct((count // cols, H, 2 * K), BF),) * cols
    return pl.pallas_call(
        functools.partial(factor_kernel, own, cols),
        out_shape=shapes,
        in_specs=[
            SMEM,
            HBM,
            HBM,
        ],
        out_specs=(VMEM,) * len(shapes),
        scratch_shapes=[
            pltpu.VMEM((LANES, H, 2 * K), F32),
            pltpu.VMEM((rows, H, 2 * K), F32),
            pltpu.VMEM((K, K, rows), F32),
            pltpu.VMEM((own, K, K), F32),
            pltpu.VMEM(basis.shape, F32),
            pltpu.VMEM((K, K, LANES), F32),
            pltpu.SemaphoreType.DMA((own // 2 // min(PAIRS, own // 2),)),
            pltpu.SemaphoreType.DMA,
        ],
        compiler_params=pltpu.CompilerParams(vmem_limit_bytes=52 * 2**20),
        cost_estimate=cost(own * 2**24, 2**23),
    )(at, basis, xfer_lanes)


def chain_kernel(own, cols, at_ref, gram1_ref, xfer_ref, out_ref, xt):
    col = at_ref[1]
    unpack_transfers(xfer_ref, xt)
    grams = [gram1_ref[c] for c in range(own // 2)]
    offset = 0
    width = own * cols // 2
    while len(grams) > 1:
        here = len(grams)
        xfers = [unhalf(xt[offset + col * here + c]) for c in range(here)]
        offset += width
        width //= 2
        if here < 4:
            grams = lift_pairs(grams, xfers)
            continue
        here //= 2
        upper = [unhalf(xt[offset + col * here + c]) for c in range(here)]
        offset += width
        width //= 2
        xfers = [mul(upper[c // 2], x, NN) for c, x in enumerate(xfers)]
        low = lift_pairs(grams, xfers)
        grams = [x + y for x, y in zip(low[0::2], low[1::2])]
    shift = 0
    whole = None
    while width >= 1:
        xfer = unhalf(xt[offset + jnp.right_shift(col, shift)])
        whole = xfer if whole is None else mul(xfer, whole, NN)
        offset += width
        width //= 2
        shift += 1
    rest = halve(lift_all(grams, [whole])[0])
    for n in range(TERMS):
        term = rest.astype(BF)
        out_ref[n] = term
        rest = rest - term.astype(F32)


def lifted_root(at, gram1, xfer_lanes, own, cols):
    return pl.pallas_call(
        functools.partial(chain_kernel, own, cols),
        out_shape=jax.ShapeDtypeStruct((TERMS, H, 2 * K), BF),
        grid=(1,),
        in_specs=[
            SMEM,
            pl.BlockSpec(gram1.shape, lambda i: (0, 0, 0)),
            pl.BlockSpec((K, K, LANES), lambda i: (0, 0, 1)),
        ],
        out_specs=pl.BlockSpec((TERMS, H, 2 * K), lambda i: (0, 0, 0)),
        scratch_shapes=[pltpu.VMEM((LANES, H, 2 * K), F32)],
        compiler_params=PARAMS,
        cost_estimate=cost(own * 2**24, 2**22),
    )(at, gram1, xfer_lanes)


def top_kernel(leaves, at_ref, top_ref, *refs):
    pairs = leaves // 2
    parts, (anc_ref, root_ref, level_ref, s, a) = refs[:-5], refs[-5:]
    pair = jnp.right_shift(at_ref[0], 1)
    for m in range(pairs):
        terms = [part[m] for part in parts]
        while len(terms) > 1:
            terms = [x + y for x, y in zip(terms[0::2], terms[1::2])]
        level_ref[jnp.bitwise_xor(pair, m)] = terms[0]
    level = [unhalf(level_ref[m]) for m in range(pairs)]
    heights = []
    slot = 0
    off_top = 0
    while True:
        heights.append(slot)
        for m, gram in enumerate(level):
            s[slot + m] = halve(gram)
        slot += len(level)
        if len(level) == 1:
            break
        level_xfers = [top_ref[off_top + m].T for m in range(len(level))]
        off_top += len(level)
        level = lift_pairs(level, level_xfers)
    factor_halved(s, a)
    for h, start in enumerate(heights):
        anc_ref[0, h] = unhalf(s[start + jnp.right_shift(at_ref[0], h + 1)])
    root_ref[...] = unhalf(s[heights[-1]])


def top_factors(at, parts, top_transfer, leaves):
    height = leaves.bit_length() - 1
    rows = (leaves - 1 + 7) // 8 * 8
    return pl.pallas_call(
        functools.partial(top_kernel, leaves),
        out_shape=(
            jax.ShapeDtypeStruct((1, height, K, K), F32),
            jax.ShapeDtypeStruct((K, K), F32),
        ),
        in_specs=[SMEM, VMEM] + [VMEM] * len(parts),
        out_specs=(VMEM, VMEM),
        scratch_shapes=[
            pltpu.VMEM((leaves // 2, H, 2 * K), F32),
            pltpu.VMEM((rows, H, 2 * K), F32),
            pltpu.VMEM((K, K, rows), F32),
        ],
        compiler_params=PARAMS,
        cost_estimate=cost(2**22, 2**17),
    )(at, top_transfer, *parts)


def lane_groups(sizes):
    return [(which, lane) for which, size in enumerate(sizes) for lane in range(0, size, LANES)]


def turn_kernel(groups, *refs):
    blocks, cells_ref, bt = refs[:-2], refs[-2], refs[-1]
    for g, (which, first) in enumerate(groups):
        src = blocks[which]

        @pl.loop(0, H // TURN)
        def _(step):
            lanes = pl.ds(first, LANES)
            at = [step * TURN + v for v in range(TURN)]
            x = [jnp.concatenate([src[q, :, lanes], src[q + H, :, lanes]], axis=0) for q in at]
            turned = [y.astype(F32).T for y in x]
            for q, y in zip(at, turned):
                bt[:, q, :] = y

        cells_ref[pl.ds(LANES * g, LANES)] = bt[...].astype(BF)


def turned_blocks(blocks):
    groups = lane_groups([x.shape[2] for x in blocks])
    return pl.pallas_call(
        functools.partial(turn_kernel, groups),
        out_shape=jax.ShapeDtypeStruct((LANES * len(groups), H, 2 * K), BF),
        in_specs=[VMEM] * len(blocks),
        out_specs=VMEM,
        scratch_shapes=[pltpu.VMEM((LANES, H, 2 * K), F32)],
        compiler_params=PARAMS,
        cost_estimate=cost(2**20, 2**20),
    )(*blocks)


def join_kernel(inputs, *refs):
    start = 0
    for x in refs[:inputs]:
        refs[inputs][pl.ds(start, x.shape[0])] = x[...]
        start += x.shape[0]
    for n, x in enumerate(refs[:inputs] if len(refs) > inputs + 1 else ()):
        total = x[x.shape[0] - TERMS].astype(F32)
        for t in range(1, TERMS):
            total = total + x[x.shape[0] - TERMS + t].astype(F32)
        refs[inputs + 1][n] = total


def joined(pieces, sums=False):
    entries = sum(x.shape[0] for x in pieces)
    shapes = [jax.ShapeDtypeStruct((entries, H, 2 * K), BF)]
    if sums:
        shapes.append(jax.ShapeDtypeStruct((len(pieces), H, 2 * K), F32))
    return pl.pallas_call(
        functools.partial(join_kernel, len(pieces)),
        out_shape=tuple(shapes),
        in_specs=[VMEM] * len(pieces),
        out_specs=(VMEM,) * len(shapes),
        compiler_params=PARAMS,
        cost_estimate=cost(0, 2**18),
    )(*pieces)


def bits(size):
    assert size & (size - 1) == 0
    return size.bit_length() - 1


def row_entry(sizes, at_ref, level, row):
    own, cols = sizes[:2]
    size = own >> level
    row = row - at_ref[0] * (size * cols)
    owner = jnp.bitwise_xor(jnp.right_shift(row, bits(size)), at_ref[1])
    return owner * (own + own // 2) + level * own + jnp.bitwise_and(row, size - 1)


def column_entry(sizes, at_ref, level, column):
    own, cols = sizes[:2]
    size = own >> level
    count = own + own // 2
    owner = jnp.right_shift(column, bits(size))
    away = jnp.bitwise_xor(jnp.right_shift(owner, bits(cols)), at_ref[0])
    part = jnp.bitwise_xor(jnp.bitwise_and(owner, cols - 1), at_ref[1])
    entry = jnp.right_shift(away, 1) * (count + TERMS) + part * (count // cols)
    within = jnp.right_shift(jnp.bitwise_and(column, size - 1), bits(cols))
    return entry + level * (own // cols) + within, jnp.bitwise_and(away, 1) == 1


def middle_kernel(groups, sizes, at_ref, *refs):
    pairs, (cells_ref, same_ref, other_ref, out_ref) = refs[:-4], refs[-4:]
    for g, (level, first) in enumerate(groups):

        @pl.loop(0, LANES // SLOTS)
        def _(step):
            at = [step * SLOTS + u for u in range(SLOTS)]
            cols = []
            for b in at:
                n, there = column_entry(sizes, at_ref, level, pairs[level][1, first + b])
                cols.append(unhalf(jnp.where(there, other_ref[n], same_ref[n])))
            cells = [unhalf(cells_ref[LANES * g + b]) for b in at]
            y = [lax.dot_general(x, c, NT, preferred_element_type=F32) for x, c in zip(cells, cols)]
            y = [halve(z.astype(BF)) for z in y]
            for b, z in zip(at, y):
                out_ref[LANES * g + b] = z


def middle_products(sizes, at, pairs, cells, same_core, other_core):
    groups = lane_groups([x.shape[1] for x in pairs])
    return pl.pallas_call(
        functools.partial(middle_kernel, groups, sizes),
        out_shape=jax.ShapeDtypeStruct(cells.shape, BF),
        in_specs=[SMEM] * (1 + len(pairs)) + [VMEM] * 3,
        out_specs=VMEM,
        compiler_params=PARAMS,
        cost_estimate=cost(cells.shape[0] * 2**19, 2**20),
    )(at, *pairs, cells, same_core, other_core)


def outer_kernel(groups, sizes, outs, at_ref, *refs):
    pairs, counts, middle_ref = refs[:outs], refs[outs : 2 * outs], refs[2 * outs]
    pieces, out_refs = refs[2 * outs + 1 : -outs - 4], refs[-outs - 4 : -4]
    pt, table, ready, sem = refs[-4:]
    packs = pieces[0].shape[0]
    together = math.gcd(packs, 6)
    for e, piece in enumerate(pieces):

        @pl.loop(0, packs // together)
        def _(step):
            at = [step * together + g for g in range(together)]
            full = [unpack(piece[g].astype(F32)) for g in at]
            for g, four in zip(at, full):
                for m in range(4):
                    table[4 * (e * packs + g) + m] = four[m].astype(BF)

    copies = []
    for g, (which, first) in enumerate(groups):

        @pl.loop(0, LANES // SLOTS)
        def _(step):
            at = [step * SLOTS + u for u in range(SLOTS)]
            rows = [table[row_entry(sizes, at_ref, which, pairs[which][0, first + b])] for b in at]
            right = [unhalf(middle_ref[LANES * g + b]) for b in at]
            y = [lax.dot_general(r, x, NN, preferred_element_type=F32) for r, x in zip(rows, right)]
            y = [halve(z) for z in y]
            for b, z in zip(at, y):
                pt[b] = z

        keep = lax.broadcasted_iota(jnp.int32, (2 * K, LANES), 1) < counts[which][0] - first

        @pl.loop(0, H // TURN)
        def _(step):
            at = [step * TURN + v for v in range(TURN)]
            turned = [pt[:, q, :].T for q in at]
            for q, y in zip(at, turned):
                y = jnp.where(keep, y, 0.0).astype(BF)
                ready[g, q] = y[:K]
                ready[g, q + H] = y[K:]

        out = out_refs[which].at[:, :, pl.ds(first, LANES)]
        copies.append(pltpu.make_async_copy(ready.at[g], out, sem.at[g]))
        copies[-1].start()
    for copy in copies:
        copy.wait()


def outer_products(sizes, at, pairs, counts, middle, pieces):
    slots = [x.shape[1] for x in pairs]
    groups = lane_groups(slots)
    entries = 4 * sum(x.shape[0] for x in pieces)
    return pl.pallas_call(
        functools.partial(outer_kernel, groups, sizes, len(slots)),
        out_shape=tuple(jax.ShapeDtypeStruct((K, K, size), BF) for size in slots),
        in_specs=[SMEM] * (1 + 2 * len(slots)) + [VMEM] * (1 + len(pieces)),
        out_specs=(ANY,) * len(slots),
        scratch_shapes=[
            pltpu.VMEM((LANES, H, 2 * K), F32),
            pltpu.VMEM((entries, K, K), BF),
            pltpu.VMEM((len(groups), K, K, LANES), BF),
            pltpu.SemaphoreType.DMA((len(groups),)),
        ],
        compiler_params=PARAMS,
        cost_estimate=cost(len(groups) * 2**26, 2**22),
    )(at, *pairs, *counts, middle, *pieces)


def swapped(x, axis, d):
    return lax.ppermute(x, axis, [(i, i ^ d) for i in range(lax.axis_size(axis))])


def on_device(basis, transfer, top_transfer, blocks0, pairs0, counts0, blocks1, pairs1, counts1):
    own = basis.shape[0]
    cols = lax.axis_size("col")
    leaves = lax.axis_size("leaf")
    at = jnp.stack([lax.axis_index("leaf"), lax.axis_index("col")]).astype(jnp.int32)
    xfer_lanes = jnp.transpose(transfer, (1, 2, 0))
    lanes0, lanes1 = jnp.transpose(blocks0, (1, 2, 0)), jnp.transpose(blocks1, (1, 2, 0))
    sizes = (own, cols)
    pairs = (jnp.transpose(pairs0), jnp.transpose(pairs1))

    factors, gram1, *sent = own_factors(at, basis, xfer_lanes, cols)
    received = [swapped(sent[d], "col", d) for d in range(1, cols)]
    terms = lifted_root(at, gram1, xfer_lanes, own, cols)
    received, terms, factors, lanes0, lanes1 = lax.optimization_barrier(
        (received, terms, factors, lanes0, lanes1)
    )

    (part,) = joined([sent[0]] + received + [terms])
    chips = [swapped(part, "leaf", d) for d in range(2, leaves, 2)]
    row_pieces = [factors] + [swapped(factors, "col", d) for d in range(1, cols - 1)]
    cells = turned_blocks((lanes0, lanes1))
    chips, row_pieces, cells = lax.optimization_barrier((chips, row_pieces, cells))

    row_pieces = row_pieces + [swapped(factors, "col", cols - 1)]
    same_core, pair_part = joined([part] + chips, sums=True)
    other_core = swapped(same_core, "leaf", 1)
    there = other_core.reshape(leaves // 2, part.shape[0], H, 2 * K)[:, -TERMS:].astype(F32)
    other_part = there[:, 0]
    for t in range(1, TERMS):
        other_part = other_part + there[:, t]
    pair_part = pair_part + other_part
    tops = [pair_part] + [swapped(pair_part, "col", d) for d in range(1, cols)]
    ancestors, root = top_factors(at, tops, top_transfer, leaves)

    middle = middle_products(sizes, at, pairs, cells, same_core, other_core)
    out0, out1 = outer_products(sizes, at, pairs, (counts0, counts1), middle, row_pieces)
    return (jnp.transpose(out0, (2, 0, 1)), jnp.transpose(out1, (2, 0, 1)), root, ancestors)


def solution(mesh):
    in_specs = (
        P(("leaf", "col"), None, None),
        P("leaf", None, None),
        P(),
        P(("leaf", "col"), None, None),
        P(("leaf", "col"), None),
        P(("leaf", "col")),
        P(("leaf", "col"), None, None),
        P(("leaf", "col"), None),
        P(("leaf", "col")),
    )
    out_specs = (
        P(("leaf", "col"), None, None),
        P(("leaf", "col"), None, None),
        P(),
        P("leaf", None, None, None),
    )
    return jax.shard_map(
        on_device, mesh=mesh, in_specs=in_specs, out_specs=out_specs, check_vma=False
    )
```

```python
import functools
import math

import jax
import jax.numpy as jnp
from jax import lax
from jax.experimental import pallas as pl
from jax.experimental.pallas import tpu as pltpu
from jax.sharding import PartitionSpec as P

BF, F32 = jnp.bfloat16, jnp.float32
EXACT = lax.Precision.HIGHEST
NT = (((1,), (1,)), ((), ()))
NN = (((1,), (0,)), ((), ()))
K = 64
H = K // 2
Q = K // 4
LANES = 128
SMEM = pl.BlockSpec(memory_space=pltpu.SMEM)
VMEM = pl.BlockSpec(memory_space=pltpu.VMEM)
ANY = pl.BlockSpec(memory_space=pl.ANY)
HBM = pl.BlockSpec(memory_space=pltpu.HBM)
TERMS = 3
TURN = 8
SLOTS = 64
PAIRS = 8
PARAMS = pltpu.CompilerParams(vmem_limit_bytes=24 * 2**20)


def unhalf(x):
    return jnp.concatenate([x[:, :K], x[:, K:]], axis=0)


def halve(x):
    return jnp.concatenate([x[:H], x[H:]], axis=1)


def bf16_terms(x):
    high = x.astype(BF)
    rest = x - high.astype(F32)
    mid = rest.astype(BF)
    return high, mid, (rest - mid.astype(F32)).astype(BF)


def mul(x, y, dims):
    if x.shape[1] != K:
        return lax.dot_general(x, y, dims, precision=EXACT, preferred_element_type=F32)
    h, m, l = bf16_terms(x)
    p, q, r = bf16_terms(y)
    axis = dims[0][1][0]
    dot = functools.partial(lax.dot_general, dimension_numbers=dims, preferred_element_type=F32)
    main = dot(jnp.concatenate([h, h, m, m], axis=1), jnp.concatenate([p, q, p, q], axis=axis))
    return main + dot(jnp.concatenate([h, l], axis=1), jnp.concatenate([r, p], axis=axis))


def lift_all(grams, xfers_t):
    halfway = [mul(f, g, NN) for f, g in zip(xfers_t, grams)]
    return [mul(t, f, NT) for t, f in zip(halfway, xfers_t)]


def lift_pairs(grams, xfers_t):
    lifted = lift_all(grams, xfers_t)
    return [low + high for low, high in zip(lifted[0::2], lifted[1::2])]


def cost(flops, size):
    return pl.CostEstimate(flops=flops, bytes_accessed=size, transcendentals=0)


def unpack_transfers(xfer_ref, xt):
    @pl.loop(0, H // TURN)
    def _(step):
        at = [step * TURN + v for v in range(TURN)]
        turned = [jnp.concatenate([xfer_ref[:, q, :], xfer_ref[:, q + H, :]], axis=0).T for q in at]
        for q, y in zip(at, turned):
            xt[:, q, :] = y


def cholesky_lanes(a):
    sub = lax.broadcasted_iota(jnp.int32, (8, a.shape[2]), 0)

    def cols(block):
        return pl.ds(8 * block, 8)

    for panel in range(K // 8):
        base = 8 * panel
        scale = []
        rows = [a[base + k, pl.ds(base, 8), :] for k in range(8)]
        for k in range(8):
            scale.append(lax.rsqrt(rows[k][k : k + 1, :]))
            rows[k] = rows[k] * scale[k]
            for i in range(k + 1, 8):
                rows[i] = rows[i] - rows[k][i : i + 1, :] * rows[k]
        for k in range(8):
            a[base + k, pl.ds(base, 8), :] = jnp.where(sub >= k, rows[k], 0.0)
        for j in range(panel + 1, K // 8):
            new = []
            for k in range(8):
                acc = a[base + k, pl.ds(8 * j, 8), :]
                for p in range(k):
                    acc = acc - rows[p][k : k + 1, :] * new[p]
                new.append(acc * scale[k])
            for k in range(8):
                a[base + k, pl.ds(8 * j, 8), :] = new[k]
        if panel < K // 8 - 1:

            for i_block in range(panel + 1, K // 8):
                left = [a[base + k, cols(i_block), :] for k in range(8)]

                for j_block in range(i_block, K // 8):
                    right = [a[base + k, cols(j_block), :] for k in range(8)]
                    for i in range(8):
                        acc = a[8 * i_block + i, cols(j_block), :]
                        for k in range(8):
                            acc = acc - left[k][i : i + 1, :] * right[k]
                        a[8 * i_block + i, cols(j_block), :] = acc

    for i in range(8, K):
        a[i, pl.ds(0, i // 8 * 8), :] = jnp.zeros((i // 8 * 8, a.shape[2]), F32)


def factor_halved(s, a):
    @pl.loop(0, H // TURN)
    def _(step):
        at = [step * TURN + v for v in range(TURN)]
        turned = [s[:, q, :].T for q in at]
        for q, y in zip(at, turned):
            a[q] = y[:K]
            a[q + H] = y[K:]

    cholesky_lanes(a)

    @pl.loop(0, H // TURN)
    def _(step):
        at = [step * TURN + v for v in range(TURN)]
        turned = [jnp.concatenate([a[q], a[q + H]], axis=0).T for q in at]
        for q, y in zip(at, turned):
            s[:, q, :] = y


def packed(matrices):
    return matrices % 4 == 0


def slabs(matrices):
    return matrices // 4 * 5 if packed(matrices) else 2 * matrices


def lane(low, high):
    at = lax.broadcasted_iota(jnp.int32, (Q, 2 * K), 1)
    return (at >= low) & (at < high)


def pack(four):
    top = [x[:Q] for x in four]
    low = [jnp.where(lane(0, Q), pltpu.roll(x[Q:], Q, 1), x[Q:]) for x in four]
    gap = lane(K, K + H)
    return jnp.concatenate(
        [
            jnp.where(gap, pltpu.roll(top[3], K, 1), top[0]),
            jnp.where(gap, pltpu.roll(top[3], H, 1), top[1]),
            jnp.where(gap, pltpu.roll(top[3], 2 * K - H, 1), top[2]),
            jnp.where(lane(0, K), low[0], pltpu.roll(low[1], K, 1)),
            jnp.where(lane(0, K), low[2], pltpu.roll(low[3], K, 1)),
        ],
        axis=0,
    )


def unpack(unit):
    full = []
    for m in range(3):
        full.append((unit[m], jnp.where(lane(H, K), pltpu.roll(unit[m], K, 1), 0.0)))
    first = jnp.where(lane(0, H), pltpu.roll(unit[0], K, 1), pltpu.roll(unit[1], 2 * K - H, 1))
    full.append((first, jnp.where(lane(H, K), pltpu.roll(unit[2], 2 * K - H, 1), 0.0)))
    out = []
    for m, (block0, block2) in enumerate(full):
        low = unit[3 + m // 2] if m % 2 == 0 else pltpu.roll(unit[3 + m // 2], K, 1)
        block1 = jnp.where(lane(Q, K), low, 0.0)
        block3 = jnp.where(lane(K - Q, K), pltpu.roll(low, K - Q, 1), 0.0)
        out.append(jnp.concatenate([block0, block1, block2, block3], axis=0)[:, :K])
    return out


def factor_kernel(
    own,
    cols,
    at_ref,
    all_basis_ref,
    all_xfer_ref,
    fac_ref,
    gram1_ref,
    *refs,
):
    sent_refs = refs[:cols]
    xt, s, a, g0, basis_ref, xfer_ref, basis_sem, sem = refs[cols:]
    col = at_ref[1]
    first = col * own
    pairs = min(PAIRS, own // 2)

    def chunk(step):
        rows = pl.ds(2 * pairs * step, 2 * pairs)
        return pltpu.make_async_copy(all_basis_ref.at[rows], basis_ref.at[rows], basis_sem.at[step])

    for step in range(own // 2 // pairs):
        chunk(step).start()
    copy = pltpu.make_async_copy(all_xfer_ref.at[:, :, pl.ds(0, LANES)], xfer_ref, sem)
    copy.start()

    @pl.loop(0, own // 2 // pairs)
    def _(step):
        chunk(step).wait()
        at = [2 * step * pairs + c for c in range(2 * pairs)]
        points = [basis_ref[c] for c in at]
        grams = [mul(x, x, NT) for x in points]
        for c, gram in zip(at, grams):
            g0[c] = gram
            s[c] = halve(gram)

    copy.wait()
    unpack_transfers(xfer_ref, xt)

    @pl.loop(0, own // 2 // pairs)
    def _(step):
        base = step * pairs
        at = [2 * base + c for c in range(2 * pairs)]
        parents = lift_pairs([g0[c] for c in at], [unhalf(xt[first + c]) for c in at])
        for p, gram in enumerate(parents):
            gram1_ref[base + p] = gram
            s[own + base + p] = halve(gram)

    factor_halved(s, a)
    count = own + own // 2
    for g in range(count // 4):
        fac_ref[g] = pack([s[4 * g + m] for m in range(4)]).astype(BF)
    for e in range(cols):
        mine = [s[r * cols + jnp.bitwise_xor(col, e)] for r in range(count // cols)]
        start = 0
        for x in [pack(mine[n : n + 4]) for n in range(0, len(mine), 4)] if packed(len(mine)) else mine:
            for n in range(x.shape[0] // Q):
                sent_refs[e][start + n] = x[Q * n : Q * (n + 1)].astype(BF)
            start += x.shape[0] // Q


def own_factors(at, basis, xfer_lanes, cols):
    own = basis.shape[0]
    count = own + own // 2
    rows = (count + 7) // 8 * 8
    shapes = (
        jax.ShapeDtypeStruct((count // 4, 5 * Q, 2 * K), BF),
        jax.ShapeDtypeStruct((own // 2, K, K), F32),
    ) + (jax.ShapeDtypeStruct((slabs(count // cols), Q, 2 * K), BF),) * cols
    return pl.pallas_call(
        functools.partial(factor_kernel, own, cols),
        out_shape=shapes,
        in_specs=[
            SMEM,
            HBM,
            HBM,
        ],
        out_specs=(VMEM,) * len(shapes),
        scratch_shapes=[
            pltpu.VMEM((LANES, H, 2 * K), F32),
            pltpu.VMEM((rows, H, 2 * K), F32),
            pltpu.VMEM((K, K, rows), F32),
            pltpu.VMEM((own, K, K), F32),
            pltpu.VMEM(basis.shape, F32),
            pltpu.VMEM((K, K, LANES), F32),
            pltpu.SemaphoreType.DMA((own // 2 // min(PAIRS, own // 2),)),
            pltpu.SemaphoreType.DMA,
        ],
        compiler_params=pltpu.CompilerParams(vmem_limit_bytes=52 * 2**20),
        cost_estimate=cost(own * 2**24, 2**23),
    )(at, basis, xfer_lanes)


def chain_kernel(own, cols, at_ref, gram1_ref, xfer_ref, out_ref, xt):
    col = at_ref[1]
    unpack_transfers(xfer_ref, xt)
    grams = [gram1_ref[c] for c in range(own // 2)]
    offset = 0
    width = own * cols // 2
    while len(grams) > 1:
        here = len(grams)
        xfers = [unhalf(xt[offset + col * here + c]) for c in range(here)]
        offset += width
        width //= 2
        if here < 4:
            grams = lift_pairs(grams, xfers)
            continue
        here //= 2
        upper = [unhalf(xt[offset + col * here + c]) for c in range(here)]
        offset += width
        width //= 2
        xfers = [mul(upper[c // 2], x, NN) for c, x in enumerate(xfers)]
        low = lift_pairs(grams, xfers)
        grams = [x + y for x, y in zip(low[0::2], low[1::2])]
    shift = 0
    whole = None
    while width >= 1:
        xfer = unhalf(xt[offset + jnp.right_shift(col, shift)])
        whole = xfer if whole is None else mul(xfer, whole, NN)
        offset += width
        width //= 2
        shift += 1
    rest = halve(lift_all(grams, [whole])[0])
    for n in range(TERMS):
        term = rest.astype(BF)
        out_ref[2 * n] = term[:Q]
        out_ref[2 * n + 1] = term[Q:]
        rest = rest - term.astype(F32)


def lifted_root(at, gram1, xfer_lanes, own, cols):
    return pl.pallas_call(
        functools.partial(chain_kernel, own, cols),
        out_shape=jax.ShapeDtypeStruct((2 * TERMS, Q, 2 * K), BF),
        grid=(1,),
        in_specs=[
            SMEM,
            pl.BlockSpec(gram1.shape, lambda i: (0, 0, 0)),
            pl.BlockSpec((K, K, LANES), lambda i: (0, 0, 1)),
        ],
        out_specs=pl.BlockSpec((2 * TERMS, Q, 2 * K), lambda i: (0, 0, 0)),
        scratch_shapes=[pltpu.VMEM((LANES, H, 2 * K), F32)],
        compiler_params=PARAMS,
        cost_estimate=cost(own * 2**24, 2**22),
    )(at, gram1, xfer_lanes)


def top_kernel(leaves, at_ref, top_ref, *refs):
    pairs = leaves // 2
    parts, (anc_ref, root_ref, level_ref, s, a) = refs[:-5], refs[-5:]
    pair = jnp.right_shift(at_ref[0], 1)
    for m in range(pairs):
        terms = [part[m].reshape(H, 2 * K) for part in parts]
        while len(terms) > 1:
            terms = [x + y for x, y in zip(terms[0::2], terms[1::2])]
        level_ref[jnp.bitwise_xor(pair, m)] = terms[0]
    level = [unhalf(level_ref[m]) for m in range(pairs)]
    heights = []
    slot = 0
    off_top = 0
    while True:
        heights.append(slot)
        for m, gram in enumerate(level):
            s[slot + m] = halve(gram)
        slot += len(level)
        if len(level) == 1:
            break
        level_xfers = [top_ref[off_top + m].T for m in range(len(level))]
        off_top += len(level)
        level = lift_pairs(level, level_xfers)
    factor_halved(s, a)
    for h, start in enumerate(heights):
        anc_ref[0, h] = unhalf(s[start + jnp.right_shift(at_ref[0], h + 1)])
    root_ref[...] = unhalf(s[heights[-1]])


def top_factors(at, parts, top_transfer, leaves):
    height = leaves.bit_length() - 1
    rows = (leaves - 1 + 7) // 8 * 8
    return pl.pallas_call(
        functools.partial(top_kernel, leaves),
        out_shape=(
            jax.ShapeDtypeStruct((1, height, K, K), F32),
            jax.ShapeDtypeStruct((K, K), F32),
        ),
        in_specs=[SMEM, VMEM] + [VMEM] * len(parts),
        out_specs=(VMEM, VMEM),
        scratch_shapes=[
            pltpu.VMEM((leaves // 2, H, 2 * K), F32),
            pltpu.VMEM((rows, H, 2 * K), F32),
            pltpu.VMEM((K, K, rows), F32),
        ],
        compiler_params=PARAMS,
        cost_estimate=cost(2**22, 2**17),
    )(at, top_transfer, *parts)


def lane_groups(sizes):
    return [(which, lane) for which, size in enumerate(sizes) for lane in range(0, size, LANES)]


def turn_kernel(groups, *refs):
    blocks, cells_ref, bt = refs[:-2], refs[-2], refs[-1]
    for g, (which, first) in enumerate(groups):
        src = blocks[which]

        @pl.loop(0, H // TURN)
        def _(step):
            lanes = pl.ds(first, LANES)
            at = [step * TURN + v for v in range(TURN)]
            x = [jnp.concatenate([src[q, :, lanes], src[q + H, :, lanes]], axis=0) for q in at]
            turned = [y.astype(F32).T for y in x]
            for q, y in zip(at, turned):
                bt[:, q, :] = y

        cells_ref[pl.ds(LANES * g, LANES)] = bt[...].astype(BF)


def turned_blocks(blocks):
    groups = lane_groups([x.shape[2] for x in blocks])
    return pl.pallas_call(
        functools.partial(turn_kernel, groups),
        out_shape=jax.ShapeDtypeStruct((LANES * len(groups), H, 2 * K), BF),
        in_specs=[VMEM] * len(blocks),
        out_specs=VMEM,
        scratch_shapes=[pltpu.VMEM((LANES, H, 2 * K), F32)],
        compiler_params=PARAMS,
        cost_estimate=cost(2**20, 2**20),
    )(*blocks)


def join_kernel(inputs, *refs):
    start = 0
    for x in refs[:inputs]:
        refs[inputs][pl.ds(start, x.shape[0])] = x[...]
        start += x.shape[0]
    for n, x in enumerate(refs[:inputs] if len(refs) > inputs + 1 else ()):
        last = x.shape[0] - 2 * TERMS
        total = x[last : last + 2].astype(F32)
        for t in range(1, TERMS):
            total = total + x[last + 2 * t : last + 2 * t + 2].astype(F32)
        refs[inputs + 1][n] = total


def joined(pieces, sums=False):
    entries = sum(x.shape[0] for x in pieces)
    shapes = [jax.ShapeDtypeStruct((entries, Q, 2 * K), BF)]
    if sums:
        shapes.append(jax.ShapeDtypeStruct((len(pieces), 2, Q, 2 * K), F32))
    return pl.pallas_call(
        functools.partial(join_kernel, len(pieces)),
        out_shape=tuple(shapes),
        in_specs=[VMEM] * len(pieces),
        out_specs=(VMEM,) * len(shapes),
        compiler_params=PARAMS,
        cost_estimate=cost(0, 2**18),
    )(*pieces)


def bits(size):
    assert size & (size - 1) == 0
    return size.bit_length() - 1


def row_entry(sizes, at_ref, level, row):
    own, cols = sizes[:2]
    size = own >> level
    row = row - at_ref[0] * (size * cols)
    owner = jnp.bitwise_xor(jnp.right_shift(row, bits(size)), at_ref[1])
    return owner * (own + own // 2) + level * own + jnp.bitwise_and(row, size - 1)


def column_entry(sizes, at_ref, level, column):
    own, cols, leaves = sizes
    size = own >> level
    count = own + own // 2
    owner = jnp.right_shift(column, bits(size))
    away = jnp.bitwise_xor(jnp.right_shift(owner, bits(cols)), at_ref[0])
    part = jnp.bitwise_xor(jnp.bitwise_and(owner, cols - 1), at_ref[1])
    piece = jnp.bitwise_and(away, 1) * (leaves // 2) + jnp.right_shift(away, 1)
    entry = piece * count + part * (count // cols)
    within = jnp.right_shift(jnp.bitwise_and(column, size - 1), bits(cols))
    return entry + level * (own // cols) + within


def fill_column_table(table, start, ref, sizes):
    own, cols, leaves = sizes
    count = own + own // 2
    parts = count // cols
    step = slabs(parts)
    length = ref.shape[0] // (leaves // 2)

    @pl.loop(0, leaves // 2)
    def _(p):
        found = []
        for e in range(cols):
            first = p * length + e * step
            if packed(parts):
                for g in range(parts // 4):
                    found += unpack([ref[first + 5 * g + n].astype(F32) for n in range(5)])
            else:
                for r in range(parts):
                    two = [ref[first + 2 * r + n] for n in range(2)]
                    found.append(unhalf(jnp.concatenate(two, axis=0)))
        for n, x in enumerate(found):
            table[start + p * count + n] = x.astype(BF)


def middle_kernel(groups, sizes, at_ref, *refs):
    pairs, (cells_ref, same_ref, other_ref, out_ref, table) = refs[:-5], refs[-5:]
    fill_column_table(table, 0, same_ref, sizes)
    fill_column_table(table, table.shape[0] // 2, other_ref, sizes)
    for g, (level, first) in enumerate(groups):

        @pl.loop(0, LANES // SLOTS)
        def _(step):
            at = [step * SLOTS + u for u in range(SLOTS)]
            cols = [table[column_entry(sizes, at_ref, level, pairs[level][1, first + b])] for b in at]
            cells = [unhalf(cells_ref[LANES * g + b]) for b in at]
            y = [lax.dot_general(x, c, NT, preferred_element_type=F32) for x, c in zip(cells, cols)]
            y = [halve(z.astype(BF)) for z in y]
            for b, z in zip(at, y):
                out_ref[LANES * g + b] = z


def middle_products(sizes, at, pairs, cells, same_core, other_core):
    groups = lane_groups([x.shape[1] for x in pairs])
    return pl.pallas_call(
        functools.partial(middle_kernel, groups, sizes),
        out_shape=jax.ShapeDtypeStruct(cells.shape, BF),
        in_specs=[SMEM] * (1 + len(pairs)) + [VMEM] * 3,
        out_specs=VMEM,
        scratch_shapes=[pltpu.VMEM((sizes[2] * (sizes[0] + sizes[0] // 2), K, K), BF)],
        compiler_params=pltpu.CompilerParams(vmem_limit_bytes=36 * 2**20),
        cost_estimate=cost(cells.shape[0] * 2**19, 2**20),
    )(at, *pairs, cells, same_core, other_core)


def outer_kernel(groups, sizes, outs, at_ref, *refs):
    pairs, counts, middle_ref = refs[:outs], refs[outs : 2 * outs], refs[2 * outs]
    pieces, out_refs = refs[2 * outs + 1 : -outs - 4], refs[-outs - 4 : -4]
    pt, table, ready, sem = refs[-4:]
    packs = pieces[0].shape[0]
    together = math.gcd(packs, 6)
    for e, piece in enumerate(pieces):

        @pl.loop(0, packs // together)
        def _(step):
            at = [step * together + g for g in range(together)]
            full = [unpack([piece[g, Q * n : Q * (n + 1)].astype(F32) for n in range(5)]) for g in at]
            for g, four in zip(at, full):
                for m in range(4):
                    table[4 * (e * packs + g) + m] = four[m].astype(BF)

    copies = []
    for g, (which, first) in enumerate(groups):

        @pl.loop(0, LANES // SLOTS)
        def _(step):
            at = [step * SLOTS + u for u in range(SLOTS)]
            rows = [table[row_entry(sizes, at_ref, which, pairs[which][0, first + b])] for b in at]
            right = [unhalf(middle_ref[LANES * g + b]) for b in at]
            y = [lax.dot_general(r, x, NN, preferred_element_type=F32) for r, x in zip(rows, right)]
            y = [halve(z) for z in y]
            for b, z in zip(at, y):
                pt[b] = z

        keep = lax.broadcasted_iota(jnp.int32, (2 * K, LANES), 1) < counts[which][0] - first

        @pl.loop(0, H // TURN)
        def _(step):
            at = [step * TURN + v for v in range(TURN)]
            turned = [pt[:, q, :].T for q in at]
            for q, y in zip(at, turned):
                y = jnp.where(keep, y, 0.0).astype(BF)
                ready[g, q] = y[:K]
                ready[g, q + H] = y[K:]

        out = out_refs[which].at[:, :, pl.ds(first, LANES)]
        copies.append(pltpu.make_async_copy(ready.at[g], out, sem.at[g]))
        copies[-1].start()
    for copy in copies:
        copy.wait()


def outer_products(sizes, at, pairs, counts, middle, pieces):
    slots = [x.shape[1] for x in pairs]
    groups = lane_groups(slots)
    entries = 4 * sum(x.shape[0] for x in pieces)
    return pl.pallas_call(
        functools.partial(outer_kernel, groups, sizes, len(slots)),
        out_shape=tuple(jax.ShapeDtypeStruct((K, K, size), BF) for size in slots),
        in_specs=[SMEM] * (1 + 2 * len(slots)) + [VMEM] * (1 + len(pieces)),
        out_specs=(ANY,) * len(slots),
        scratch_shapes=[
            pltpu.VMEM((LANES, H, 2 * K), F32),
            pltpu.VMEM((entries, K, K), BF),
            pltpu.VMEM((len(groups), K, K, LANES), BF),
            pltpu.SemaphoreType.DMA((len(groups),)),
        ],
        compiler_params=PARAMS,
        cost_estimate=cost(len(groups) * 2**26, 2**22),
    )(at, *pairs, *counts, middle, *pieces)


def swapped(x, axis, d):
    return lax.ppermute(x, axis, [(i, i ^ d) for i in range(lax.axis_size(axis))])


def on_device(basis, transfer, top_transfer, blocks0, pairs0, counts0, blocks1, pairs1, counts1):
    own = basis.shape[0]
    cols = lax.axis_size("col")
    leaves = lax.axis_size("leaf")
    at = jnp.stack([lax.axis_index("leaf"), lax.axis_index("col")]).astype(jnp.int32)
    xfer_lanes = jnp.transpose(transfer, (1, 2, 0))
    lanes0, lanes1 = jnp.transpose(blocks0, (1, 2, 0)), jnp.transpose(blocks1, (1, 2, 0))
    sizes = (own, cols, leaves)
    pairs = (jnp.transpose(pairs0), jnp.transpose(pairs1))

    factors, gram1, *sent = own_factors(at, basis, xfer_lanes, cols)
    received = [swapped(sent[d], "col", d) for d in range(1, cols)]
    terms = lifted_root(at, gram1, xfer_lanes, own, cols)
    received, terms, factors, lanes0, lanes1 = lax.optimization_barrier(
        (received, terms, factors, lanes0, lanes1)
    )

    (part,) = joined([sent[0]] + received + [terms])
    chips = [swapped(part, "leaf", d) for d in range(2, leaves, 2)]
    early = {d: swapped(factors, "col", d) for d in range(cols // 2, cols - 1)}
    cells = turned_blocks((lanes0, lanes1))
    chips, early, cells = lax.optimization_barrier((chips, early, cells))

    rows = [early[d] if d in early else swapped(factors, "col", d) for d in range(1, cols)]
    row_pieces = [factors] + rows
    same_core, pair_part = joined([part] + chips, sums=True)
    other_core = swapped(same_core, "leaf", 1)
    there = other_core.reshape(leaves // 2, part.shape[0], Q, 2 * K)[:, -2 * TERMS :].astype(F32)
    other_part = there[:, 0:2]
    for t in range(1, TERMS):
        other_part = other_part + there[:, 2 * t : 2 * t + 2]
    pair_part = pair_part + other_part
    tops = [pair_part] + [swapped(pair_part, "col", d) for d in range(1, cols)]
    ancestors, root = top_factors(at, tops, top_transfer, leaves)

    middle = middle_products(sizes, at, pairs, cells, same_core, other_core)
    out0, out1 = outer_products(sizes, at, pairs, (counts0, counts1), middle, row_pieces)
    return (jnp.transpose(out0, (2, 0, 1)), jnp.transpose(out1, (2, 0, 1)), root, ancestors)


def solution(mesh):
    in_specs = (
        P(("leaf", "col"), None, None),
        P("leaf", None, None),
        P(),
        P(("leaf", "col"), None, None),
        P(("leaf", "col"), None),
        P(("leaf", "col")),
        P(("leaf", "col"), None, None),
        P(("leaf", "col"), None),
        P(("leaf", "col")),
    )
    out_specs = (
        P(("leaf", "col"), None, None),
        P(("leaf", "col"), None, None),
        P(),
        P("leaf", None, None, None),
    )
    return jax.shard_map(
        on_device, mesh=mesh, in_specs=in_specs, out_specs=out_specs, check_vma=False
    )
```

```python
import functools
import math

import jax
import jax.numpy as jnp
from jax import lax
from jax.experimental import pallas as pl
from jax.experimental.pallas import tpu as pltpu
from jax.sharding import PartitionSpec as P

BF, F32 = jnp.bfloat16, jnp.float32
EXACT = lax.Precision.HIGHEST
NT = (((1,), (1,)), ((), ()))
NN = (((1,), (0,)), ((), ()))
K = 64
H = K // 2
Q = K // 4
LANES = 128
SMEM = pl.BlockSpec(memory_space=pltpu.SMEM)
VMEM = pl.BlockSpec(memory_space=pltpu.VMEM)
ANY = pl.BlockSpec(memory_space=pl.ANY)
HBM = pl.BlockSpec(memory_space=pltpu.HBM)
TERMS = 3
TURN = 16
SLOTS = 128
PAIRS = 8
PARAMS = pltpu.CompilerParams(vmem_limit_bytes=24 * 2**20)


def unhalf(x):
    return jnp.concatenate([x[:, :K], x[:, K:]], axis=0)


def halve(x):
    return jnp.concatenate([x[:H], x[H:]], axis=1)


def bf16_terms(x):
    high = x.astype(BF)
    rest = x - high.astype(F32)
    mid = rest.astype(BF)
    return high, mid, (rest - mid.astype(F32)).astype(BF)


def mul(x, y, dims):
    if x.shape[1] != K:
        return lax.dot_general(x, y, dims, precision=EXACT, preferred_element_type=F32)
    h, m, l = bf16_terms(x)
    p, q, r = bf16_terms(y)
    axis = dims[0][1][0]
    dot = functools.partial(lax.dot_general, dimension_numbers=dims, preferred_element_type=F32)
    main = dot(jnp.concatenate([h, h, m, m], axis=1), jnp.concatenate([p, q, p, q], axis=axis))
    return main + dot(jnp.concatenate([h, l], axis=1), jnp.concatenate([r, p], axis=axis))


def lift_all(grams, xfers_t):
    halfway = [mul(f, g, NN) for f, g in zip(xfers_t, grams)]
    return [mul(t, f, NT) for t, f in zip(halfway, xfers_t)]


def lift_pairs(grams, xfers_t):
    lifted = lift_all(grams, xfers_t)
    return [low + high for low, high in zip(lifted[0::2], lifted[1::2])]


def cost(flops, size):
    return pl.CostEstimate(flops=flops, bytes_accessed=size, transcendentals=0)


def unpack_transfers(xfer_ref, xt):
    @pl.loop(0, H // TURN)
    def _(step):
        at = [step * TURN + v for v in range(TURN)]
        turned = [jnp.concatenate([xfer_ref[:, q, :], xfer_ref[:, q + H, :]], axis=0).T for q in at]
        for q, y in zip(at, turned):
            xt[:, q, :] = y


def cholesky_lanes(a):
    sub = lax.broadcasted_iota(jnp.int32, (8, a.shape[2]), 0)

    def cols(block):
        return pl.ds(8 * block, 8)

    for panel in range(K // 8):
        base = 8 * panel
        scale = []
        rows = [a[base + k, pl.ds(base, 8), :] for k in range(8)]
        for k in range(8):
            scale.append(lax.rsqrt(rows[k][k : k + 1, :]))
            rows[k] = rows[k] * scale[k]
            for i in range(k + 1, 8):
                rows[i] = rows[i] - rows[k][i : i + 1, :] * rows[k]
        for k in range(8):
            a[base + k, pl.ds(base, 8), :] = jnp.where(sub >= k, rows[k], 0.0)
        for j in range(panel + 1, K // 8):
            new = []
            for k in range(8):
                acc = a[base + k, pl.ds(8 * j, 8), :]
                for p in range(k):
                    acc = acc - rows[p][k : k + 1, :] * new[p]
                new.append(acc * scale[k])
            for k in range(8):
                a[base + k, pl.ds(8 * j, 8), :] = new[k]
        if panel < K // 8 - 1:

            for i_block in range(panel + 1, K // 8):
                left = [a[base + k, cols(i_block), :] for k in range(8)]

                for j_block in range(i_block, K // 8):
                    right = [a[base + k, cols(j_block), :] for k in range(8)]
                    for i in range(8):
                        acc = a[8 * i_block + i, cols(j_block), :]
                        for k in range(8):
                            acc = acc - left[k][i : i + 1, :] * right[k]
                        a[8 * i_block + i, cols(j_block), :] = acc

    for i in range(8, K):
        a[i, pl.ds(0, i // 8 * 8), :] = jnp.zeros((i // 8 * 8, a.shape[2]), F32)


def factor_halved(s, a):
    @pl.loop(0, H // TURN)
    def _(step):
        at = [step * TURN + v for v in range(TURN)]
        turned = [s[:, q, :].T for q in at]
        for q, y in zip(at, turned):
            a[q] = y[:K]
            a[q + H] = y[K:]

    cholesky_lanes(a)

    @pl.loop(0, H // TURN)
    def _(step):
        at = [step * TURN + v for v in range(TURN)]
        turned = [jnp.concatenate([a[q], a[q + H]], axis=0).T for q in at]
        for q, y in zip(at, turned):
            s[:, q, :] = y


def packed(matrices):
    return matrices % 4 == 0


def slabs(matrices):
    return matrices // 4 * 5 if packed(matrices) else 2 * matrices


def lane(low, high):
    at = lax.broadcasted_iota(jnp.int32, (Q, 2 * K), 1)
    return (at >= low) & (at < high)


def pack(four):
    top = [x[:Q] for x in four]
    low = [jnp.where(lane(0, Q), pltpu.roll(x[Q:], Q, 1), x[Q:]) for x in four]
    gap = lane(K, K + H)
    return jnp.concatenate(
        [
            jnp.where(gap, pltpu.roll(top[3], K, 1), top[0]),
            jnp.where(gap, pltpu.roll(top[3], H, 1), top[1]),
            jnp.where(gap, pltpu.roll(top[3], 2 * K - H, 1), top[2]),
            jnp.where(lane(0, K), low[0], pltpu.roll(low[1], K, 1)),
            jnp.where(lane(0, K), low[2], pltpu.roll(low[3], K, 1)),
        ],
        axis=0,
    )


def unpack(unit):
    full = []
    for m in range(3):
        full.append((unit[m], jnp.where(lane(H, K), pltpu.roll(unit[m], K, 1), 0.0)))
    first = jnp.where(lane(0, H), pltpu.roll(unit[0], K, 1), pltpu.roll(unit[1], 2 * K - H, 1))
    full.append((first, jnp.where(lane(H, K), pltpu.roll(unit[2], 2 * K - H, 1), 0.0)))
    out = []
    for m, (block0, block2) in enumerate(full):
        low = unit[3 + m // 2] if m % 2 == 0 else pltpu.roll(unit[3 + m // 2], K, 1)
        block1 = jnp.where(lane(Q, K), low, 0.0)
        block3 = jnp.where(lane(K - Q, K), pltpu.roll(low, K - Q, 1), 0.0)
        out.append(jnp.concatenate([block0, block1, block2, block3], axis=0)[:, :K])
    return out


def factor_kernel(
    own,
    cols,
    at_ref,
    all_basis_ref,
    all_xfer_ref,
    fac_ref,
    gram1_ref,
    *refs,
):
    sent_refs = refs[:cols]
    xt, s, a, g0, basis_ref, xfer_ref, basis_sem, sem = refs[cols:]
    col = at_ref[1]
    first = col * own
    pairs = min(PAIRS, own // 2)

    def chunk(step):
        rows = pl.ds(2 * pairs * step, 2 * pairs)
        return pltpu.make_async_copy(all_basis_ref.at[rows], basis_ref.at[rows], basis_sem.at[step])

    for step in range(own // 2 // pairs):
        chunk(step).start()
    copy = pltpu.make_async_copy(all_xfer_ref.at[:, :, pl.ds(0, LANES)], xfer_ref, sem)
    copy.start()

    @pl.loop(0, own // 2 // pairs)
    def _(step):
        chunk(step).wait()
        at = [2 * step * pairs + c for c in range(2 * pairs)]
        points = [basis_ref[c] for c in at]
        grams = [mul(x, x, NT) for x in points]
        for c, gram in zip(at, grams):
            g0[c] = gram
            s[c] = halve(gram)

    copy.wait()
    unpack_transfers(xfer_ref, xt)

    @pl.loop(0, own // 2 // pairs)
    def _(step):
        base = step * pairs
        at = [2 * base + c for c in range(2 * pairs)]
        parents = lift_pairs([g0[c] for c in at], [unhalf(xt[first + c]) for c in at])
        for p, gram in enumerate(parents):
            gram1_ref[base + p] = gram
            s[own + base + p] = halve(gram)

    factor_halved(s, a)
    count = own + own // 2
    for g in range(count // 4):
        fac_ref[g] = pack([s[4 * g + m] for m in range(4)]).astype(BF)
    for e in range(cols):
        mine = [s[r * cols + jnp.bitwise_xor(col, e)] for r in range(count // cols)]
        start = 0
        for x in [pack(mine[n : n + 4]) for n in range(0, len(mine), 4)] if packed(len(mine)) else mine:
            for n in range(x.shape[0] // Q):
                sent_refs[e][start + n] = x[Q * n : Q * (n + 1)].astype(BF)
            start += x.shape[0] // Q


def own_factors(at, basis, xfer_lanes, cols):
    own = basis.shape[0]
    count = own + own // 2
    rows = (count + 7) // 8 * 8
    shapes = (
        jax.ShapeDtypeStruct((count // 4, 5 * Q, 2 * K), BF),
        jax.ShapeDtypeStruct((own // 2, K, K), F32),
    ) + (jax.ShapeDtypeStruct((slabs(count // cols), Q, 2 * K), BF),) * cols
    return pl.pallas_call(
        functools.partial(factor_kernel, own, cols),
        out_shape=shapes,
        in_specs=[
            SMEM,
            HBM,
            HBM,
        ],
        out_specs=(VMEM,) * len(shapes),
        scratch_shapes=[
            pltpu.VMEM((LANES, H, 2 * K), F32),
            pltpu.VMEM((rows, H, 2 * K), F32),
            pltpu.VMEM((K, K, rows), F32),
            pltpu.VMEM((own, K, K), F32),
            pltpu.VMEM(basis.shape, F32),
            pltpu.VMEM((K, K, LANES), F32),
            pltpu.SemaphoreType.DMA((own // 2 // min(PAIRS, own // 2),)),
            pltpu.SemaphoreType.DMA,
        ],
        compiler_params=pltpu.CompilerParams(vmem_limit_bytes=52 * 2**20),
        cost_estimate=cost(own * 2**24, 2**23),
    )(at, basis, xfer_lanes)


def chain_kernel(own, cols, at_ref, gram1_ref, xfer_ref, out_ref, xt):
    col = at_ref[1]
    unpack_transfers(xfer_ref, xt)
    grams = [gram1_ref[c] for c in range(own // 2)]
    offset = 0
    width = own * cols // 2
    while len(grams) > 1:
        here = len(grams)
        xfers = [unhalf(xt[offset + col * here + c]) for c in range(here)]
        offset += width
        width //= 2
        if here < 4:
            grams = lift_pairs(grams, xfers)
            continue
        here //= 2
        upper = [unhalf(xt[offset + col * here + c]) for c in range(here)]
        offset += width
        width //= 2
        xfers = [mul(upper[c // 2], x, NN) for c, x in enumerate(xfers)]
        low = lift_pairs(grams, xfers)
        grams = [x + y for x, y in zip(low[0::2], low[1::2])]
    shift = 0
    whole = None
    while width >= 1:
        xfer = unhalf(xt[offset + jnp.right_shift(col, shift)])
        whole = xfer if whole is None else mul(xfer, whole, NN)
        offset += width
        width //= 2
        shift += 1
    rest = halve(lift_all(grams, [whole])[0])
    for n in range(TERMS):
        term = rest.astype(BF)
        out_ref[2 * n] = term[:Q]
        out_ref[2 * n + 1] = term[Q:]
        rest = rest - term.astype(F32)


def lifted_root(at, gram1, xfer_lanes, own, cols):
    return pl.pallas_call(
        functools.partial(chain_kernel, own, cols),
        out_shape=jax.ShapeDtypeStruct((2 * TERMS, Q, 2 * K), BF),
        grid=(1,),
        in_specs=[
            SMEM,
            pl.BlockSpec(gram1.shape, lambda i: (0, 0, 0)),
            pl.BlockSpec((K, K, LANES), lambda i: (0, 0, 1)),
        ],
        out_specs=pl.BlockSpec((2 * TERMS, Q, 2 * K), lambda i: (0, 0, 0)),
        scratch_shapes=[pltpu.VMEM((LANES, H, 2 * K), F32)],
        compiler_params=PARAMS,
        cost_estimate=cost(own * 2**24, 2**22),
    )(at, gram1, xfer_lanes)


def top_kernel(leaves, at_ref, top_ref, *refs):
    pairs = leaves // 2
    parts, (anc_ref, root_ref, level_ref, s, a) = refs[:-5], refs[-5:]
    pair = jnp.right_shift(at_ref[0], 1)
    for m in range(pairs):
        terms = [part[m].reshape(H, 2 * K) for part in parts]
        while len(terms) > 1:
            terms = [x + y for x, y in zip(terms[0::2], terms[1::2])]
        level_ref[jnp.bitwise_xor(pair, m)] = terms[0]
    level = [unhalf(level_ref[m]) for m in range(pairs)]
    heights = []
    slot = 0
    off_top = 0
    while True:
        heights.append(slot)
        for m, gram in enumerate(level):
            s[slot + m] = halve(gram)
        slot += len(level)
        if len(level) == 1:
            break
        level_xfers = [top_ref[off_top + m].T for m in range(len(level))]
        off_top += len(level)
        level = lift_pairs(level, level_xfers)
    factor_halved(s, a)
    for h, start in enumerate(heights):
        anc_ref[0, h] = unhalf(s[start + jnp.right_shift(at_ref[0], h + 1)])
    root_ref[...] = unhalf(s[heights[-1]])


def top_factors(at, parts, top_transfer, leaves):
    height = leaves.bit_length() - 1
    rows = (leaves - 1 + 7) // 8 * 8
    return pl.pallas_call(
        functools.partial(top_kernel, leaves),
        out_shape=(
            jax.ShapeDtypeStruct((1, height, K, K), F32),
            jax.ShapeDtypeStruct((K, K), F32),
        ),
        in_specs=[SMEM, VMEM] + [VMEM] * len(parts),
        out_specs=(VMEM, VMEM),
        scratch_shapes=[
            pltpu.VMEM((leaves // 2, H, 2 * K), F32),
            pltpu.VMEM((rows, H, 2 * K), F32),
            pltpu.VMEM((K, K, rows), F32),
        ],
        compiler_params=PARAMS,
        cost_estimate=cost(2**22, 2**17),
    )(at, top_transfer, *parts)


def lane_groups(sizes):
    return [(which, lane) for which, size in enumerate(sizes) for lane in range(0, size, LANES)]


def turn_kernel(groups, *refs):
    blocks, cells_ref, bt = refs[:-2], refs[-2], refs[-1]
    for g, (which, first) in enumerate(groups):
        src = blocks[which]

        @pl.loop(0, H // TURN)
        def _(step):
            lanes = pl.ds(first, LANES)
            at = [step * TURN + v for v in range(TURN)]
            x = [jnp.concatenate([src[q, :, lanes], src[q + H, :, lanes]], axis=0) for q in at]
            turned = [y.astype(F32).T for y in x]
            for q, y in zip(at, turned):
                bt[:, q, :] = y

        cells_ref[pl.ds(LANES * g, LANES)] = bt[...].astype(BF)


def turned_blocks(blocks):
    groups = lane_groups([x.shape[2] for x in blocks])
    return pl.pallas_call(
        functools.partial(turn_kernel, groups),
        out_shape=jax.ShapeDtypeStruct((LANES * len(groups), H, 2 * K), BF),
        in_specs=[VMEM] * len(blocks),
        out_specs=VMEM,
        scratch_shapes=[pltpu.VMEM((LANES, H, 2 * K), F32)],
        compiler_params=PARAMS,
        cost_estimate=cost(2**20, 2**20),
    )(*blocks)


def join_kernel(inputs, *refs):
    pieces, out = refs[: inputs[0]], refs[sum(inputs) :]
    start = 0
    for x in pieces:
        out[0][pl.ds(start, x.shape[0])] = x[...]
        start += x.shape[0]
    if len(out) == 1:
        return
    for n, x in enumerate(pieces):
        last = x.shape[0] - 2 * TERMS
        total = x[last : last + 2].astype(F32)
        for t in range(1, TERMS):
            total = total + x[last + 2 * t : last + 2 * t + 2].astype(F32)
        out[1][n] = total
    start = 0
    for x in refs[inputs[0] : sum(inputs)]:
        out[2][pl.ds(start, x.shape[0])] = x[...]
        start += x.shape[0]


def joined(pieces, packs=()):
    shapes = [jax.ShapeDtypeStruct((sum(x.shape[0] for x in pieces), Q, 2 * K), BF)]
    if packs:
        shapes.append(jax.ShapeDtypeStruct((len(pieces), 2, Q, 2 * K), F32))
        shapes.append(jax.ShapeDtypeStruct((sum(x.shape[0] for x in packs), 5 * Q, 2 * K), BF))
    return pl.pallas_call(
        functools.partial(join_kernel, (len(pieces), len(packs))),
        out_shape=tuple(shapes),
        in_specs=[VMEM] * (len(pieces) + len(packs)),
        out_specs=(VMEM,) * len(shapes),
        compiler_params=PARAMS,
        cost_estimate=cost(0, 2**18),
    )(*pieces, *packs)


def bits(size):
    assert size & (size - 1) == 0
    return size.bit_length() - 1


def row_entry(sizes, at_ref, level, row):
    own, cols = sizes[:2]
    size = own >> level
    row = row - at_ref[0] * (size * cols)
    owner = jnp.bitwise_xor(jnp.right_shift(row, bits(size)), at_ref[1])
    return owner * (own + own // 2) + level * own + jnp.bitwise_and(row, size - 1)


def column_entry(sizes, at_ref, level, column):
    own, cols, leaves = sizes
    size = own >> level
    count = own + own // 2
    owner = jnp.right_shift(column, bits(size))
    away = jnp.bitwise_xor(jnp.right_shift(owner, bits(cols)), at_ref[0])
    part = jnp.bitwise_xor(jnp.bitwise_and(owner, cols - 1), at_ref[1])
    piece = jnp.bitwise_and(away, 1) * (leaves // 2) + jnp.right_shift(away, 1)
    entry = piece * count + part * (count // cols)
    within = jnp.right_shift(jnp.bitwise_and(column, size - 1), bits(cols))
    return entry + level * (own // cols) + within


def fill_column_table(table, start, ref, sizes):
    own, cols, leaves = sizes
    count = own + own // 2
    parts = count // cols
    step = slabs(parts)
    length = ref.shape[0] // (leaves // 2)

    @pl.loop(0, leaves // 2)
    def _(p):
        found = []
        for e in range(cols):
            first = p * length + e * step
            if packed(parts):
                for g in range(parts // 4):
                    found += unpack([ref[first + 5 * g + n].astype(F32) for n in range(5)])
            else:
                for r in range(parts):
                    two = [ref[first + 2 * r + n] for n in range(2)]
                    found.append(unhalf(jnp.concatenate(two, axis=0)))
        for n, x in enumerate(found):
            table[start + p * count + n] = x.astype(BF)


def middle_kernel(groups, sizes, at_ref, *refs):
    pairs, (cells_ref, same_ref, other_ref, out_ref, table) = refs[:-5], refs[-5:]
    fill_column_table(table, 0, same_ref, sizes)
    fill_column_table(table, table.shape[0] // 2, other_ref, sizes)
    for g, (level, first) in enumerate(groups):

        @pl.loop(0, LANES // SLOTS)
        def _(step):
            at = [step * SLOTS + u for u in range(SLOTS)]
            cols = [table[column_entry(sizes, at_ref, level, pairs[level][1, first + b])] for b in at]
            cells = [unhalf(cells_ref[LANES * g + b]) for b in at]
            y = [lax.dot_general(x, c, NT, preferred_element_type=F32) for x, c in zip(cells, cols)]
            y = [halve(z.astype(BF)) for z in y]
            for b, z in zip(at, y):
                out_ref[LANES * g + b] = z


def middle_products(sizes, at, pairs, cells, same_core, other_core):
    groups = lane_groups([x.shape[1] for x in pairs])
    return pl.pallas_call(
        functools.partial(middle_kernel, groups, sizes),
        out_shape=jax.ShapeDtypeStruct(cells.shape, BF),
        in_specs=[SMEM] * (1 + len(pairs)) + [VMEM] * 3,
        out_specs=VMEM,
        scratch_shapes=[pltpu.VMEM((sizes[2] * (sizes[0] + sizes[0] // 2), K, K), BF)],
        compiler_params=pltpu.CompilerParams(vmem_limit_bytes=36 * 2**20),
        cost_estimate=cost(cells.shape[0] * 2**19, 2**20),
    )(at, *pairs, cells, same_core, other_core)


def outer_kernel(groups, sizes, outs, orders, at_ref, *refs):
    pairs, counts, middle_ref = refs[:outs], refs[outs : 2 * outs], refs[2 * outs]
    pieces, out_refs = refs[2 * outs + 1 : -outs - 4], refs[-outs - 4 : -4]
    pt, table, ready, sem = refs[-4:]
    packs = (sizes[0] + sizes[0] // 2) // 4
    together = math.gcd(packs, 6)
    for piece, order in zip(pieces, orders):
        for n, e in enumerate(order):

            @pl.loop(0, packs // together)
            def _(step):
                at = [step * together + g for g in range(together)]
                units = [[piece[n * packs + g, Q * u : Q * (u + 1)] for u in range(5)] for g in at]
                full = [unpack([x.astype(F32) for x in five]) for five in units]
                for g, four in zip(at, full):
                    for m in range(4):
                        table[4 * (e * packs + g) + m] = four[m].astype(BF)

    copies = []
    for g, (which, first) in enumerate(groups):

        @pl.loop(0, LANES // SLOTS)
        def _(step):
            at = [step * SLOTS + u for u in range(SLOTS)]
            rows = [table[row_entry(sizes, at_ref, which, pairs[which][0, first + b])] for b in at]
            right = [unhalf(middle_ref[LANES * g + b]) for b in at]
            y = [lax.dot_general(r, x, NN, preferred_element_type=F32) for r, x in zip(rows, right)]
            y = [halve(z) for z in y]
            for b, z in zip(at, y):
                pt[b] = z

        keep = lax.broadcasted_iota(jnp.int32, (2 * K, LANES), 1) < counts[which][0] - first

        @pl.loop(0, H // TURN)
        def _(step):
            at = [step * TURN + v for v in range(TURN)]
            turned = [pt[:, q, :].T for q in at]
            for q, y in zip(at, turned):
                y = jnp.where(keep, y, 0.0).astype(BF)
                ready[g, q] = y[:K]
                ready[g, q + H] = y[K:]

        out = out_refs[which].at[:, :, pl.ds(first, LANES)]
        copies.append(pltpu.make_async_copy(ready.at[g], out, sem.at[g]))
        copies[-1].start()
    for copy in copies:
        copy.wait()


def outer_products(sizes, at, pairs, counts, middle, pieces, orders):
    slots = [x.shape[1] for x in pairs]
    groups = lane_groups(slots)
    entries = 4 * sum(x.shape[0] for x in pieces)
    return pl.pallas_call(
        functools.partial(outer_kernel, groups, sizes, len(slots), orders),
        out_shape=tuple(jax.ShapeDtypeStruct((K, K, size), BF) for size in slots),
        in_specs=[SMEM] * (1 + 2 * len(slots)) + [VMEM] * (1 + len(pieces)),
        out_specs=(ANY,) * len(slots),
        scratch_shapes=[
            pltpu.VMEM((LANES, H, 2 * K), F32),
            pltpu.VMEM((entries, K, K), BF),
            pltpu.VMEM((len(groups), K, K, LANES), BF),
            pltpu.SemaphoreType.DMA((len(groups),)),
        ],
        compiler_params=PARAMS,
        cost_estimate=cost(len(groups) * 2**26, 2**22),
    )(at, *pairs, *counts, middle, *pieces)


def swapped(x, axis, d):
    return lax.ppermute(x, axis, [(i, i ^ d) for i in range(lax.axis_size(axis))])


def on_device(basis, transfer, top_transfer, blocks0, pairs0, counts0, blocks1, pairs1, counts1):
    own = basis.shape[0]
    cols = lax.axis_size("col")
    leaves = lax.axis_size("leaf")
    at = jnp.stack([lax.axis_index("leaf"), lax.axis_index("col")]).astype(jnp.int32)
    xfer_lanes = jnp.transpose(transfer, (1, 2, 0))
    lanes0, lanes1 = jnp.transpose(blocks0, (1, 2, 0)), jnp.transpose(blocks1, (1, 2, 0))
    sizes = (own, cols, leaves)
    pairs = (jnp.transpose(pairs0), jnp.transpose(pairs1))

    factors, gram1, *sent = own_factors(at, basis, xfer_lanes, cols)
    received = [swapped(sent[d], "col", d) for d in range(1, cols)]
    terms = lifted_root(at, gram1, xfer_lanes, own, cols)
    received, terms, factors, lanes0, lanes1 = lax.optimization_barrier(
        (received, terms, factors, lanes0, lanes1)
    )

    (part,) = joined([sent[0]] + received + [terms])
    chips = [swapped(part, "leaf", d) for d in range(2, leaves, 2)]
    bit = cols // 2
    early = swapped(factors, "col", bit)
    cells = turned_blocks((lanes0, lanes1))
    chips, early, cells = lax.optimization_barrier((chips, early, cells))

    same_core, pair_part, rows = joined([part] + chips, [factors, early])
    other_core = swapped(same_core, "leaf", 1)
    orders = [0, bit]
    while True:
        bit //= 2
        forwarded = swapped(rows, "col", bit)
        orders = [orders, [e ^ bit for e in orders]]
        if bit == 1:
            break
        rows = jnp.concatenate([rows, forwarded], axis=0)
        orders = orders[0] + orders[1]
    there = other_core.reshape(leaves // 2, part.shape[0], Q, 2 * K)[:, -2 * TERMS :].astype(F32)
    other_part = there[:, 0:2]
    for t in range(1, TERMS):
        other_part = other_part + there[:, 2 * t : 2 * t + 2]
    pair_part = pair_part + other_part
    for d in range(1, bits(cols)):
        pair_part = pair_part + swapped(pair_part, "col", cols >> d)
    middle = middle_products(sizes, at, pairs, cells, same_core, other_core)
    pair_part, middle = lax.optimization_barrier((pair_part, middle))
    tops = [pair_part, swapped(pair_part, "col", 1)]
    out0, out1 = outer_products(
        sizes, at, pairs, (counts0, counts1), middle, [rows, forwarded], orders
    )
    ancestors, root = top_factors(at, tops, top_transfer, leaves)
    return (jnp.transpose(out0, (2, 0, 1)), jnp.transpose(out1, (2, 0, 1)), root, ancestors)


def solution(mesh):
    in_specs = (
        P(("leaf", "col"), None, None),
        P("leaf", None, None),
        P(),
        P(("leaf", "col"), None, None),
        P(("leaf", "col"), None),
        P(("leaf", "col")),
        P(("leaf", "col"), None, None),
        P(("leaf", "col"), None),
        P(("leaf", "col")),
    )
    out_specs = (
        P(("leaf", "col"), None, None),
        P(("leaf", "col"), None, None),
        P(),
        P("leaf", None, None, None),
    )
    return jax.shard_map(
        on_device, mesh=mesh, in_specs=in_specs, out_specs=out_specs, check_vma=False
    )
```

```python
import functools
import math

import jax
import jax.numpy as jnp
from jax import lax
from jax.experimental import pallas as pl
from jax.experimental.pallas import tpu as pltpu
from jax.sharding import PartitionSpec as P

BF, F32 = jnp.bfloat16, jnp.float32
EXACT = lax.Precision.HIGHEST
NT = (((1,), (1,)), ((), ()))
NN = (((1,), (0,)), ((), ()))
K = 64
H = K // 2
Q = K // 4
LANES = 128
SMEM = pl.BlockSpec(memory_space=pltpu.SMEM)
VMEM = pl.BlockSpec(memory_space=pltpu.VMEM)
ANY = pl.BlockSpec(memory_space=pl.ANY)
HBM = pl.BlockSpec(memory_space=pltpu.HBM)
TERMS = 3
TURN = 16
SLOTS = 128
PAIRS = 8
PARAMS = pltpu.CompilerParams(vmem_limit_bytes=24 * 2**20)


def unhalf(x):
    return jnp.concatenate([x[:, :K], x[:, K:]], axis=0)


def halve(x):
    return jnp.concatenate([x[:H], x[H:]], axis=1)


def bf16_terms(x):
    high = x.astype(BF)
    rest = x - high.astype(F32)
    mid = rest.astype(BF)
    return high, mid, (rest - mid.astype(F32)).astype(BF)


def mul(x, y, dims):
    if x.shape[1] != K:
        return lax.dot_general(x, y, dims, precision=EXACT, preferred_element_type=F32)
    h, m, l = bf16_terms(x)
    p, q, r = bf16_terms(y)
    axis = dims[0][1][0]
    dot = functools.partial(lax.dot_general, dimension_numbers=dims, preferred_element_type=F32)
    main = dot(jnp.concatenate([h, h, m, m], axis=1), jnp.concatenate([p, q, p, q], axis=axis))
    return main + dot(jnp.concatenate([h, l], axis=1), jnp.concatenate([r, p], axis=axis))


def lift_all(grams, xfers_t):
    halfway = [mul(f, g, NN) for f, g in zip(xfers_t, grams)]
    return [mul(t, f, NT) for t, f in zip(halfway, xfers_t)]


def lift_pairs(grams, xfers_t):
    lifted = lift_all(grams, xfers_t)
    return [low + high for low, high in zip(lifted[0::2], lifted[1::2])]


def cost(flops, size):
    return pl.CostEstimate(flops=flops, bytes_accessed=size, transcendentals=0)


def unpack_transfers(xfer_ref, xt):
    @pl.loop(0, H // TURN)
    def _(step):
        at = [step * TURN + v for v in range(TURN)]
        turned = [jnp.concatenate([xfer_ref[:, q, :], xfer_ref[:, q + H, :]], axis=0).T for q in at]
        for q, y in zip(at, turned):
            xt[:, q, :] = y


def cholesky_lanes(a):
    sub = lax.broadcasted_iota(jnp.int32, (8, a.shape[2]), 0)

    def cols(block):
        return pl.ds(8 * block, 8)

    for panel in range(K // 8):
        base = 8 * panel
        scale = []
        rows = [a[base + k, pl.ds(base, 8), :] for k in range(8)]
        for k in range(8):
            scale.append(lax.rsqrt(rows[k][k : k + 1, :]))
            rows[k] = rows[k] * scale[k]
            for i in range(k + 1, 8):
                rows[i] = rows[i] - rows[k][i : i + 1, :] * rows[k]
        for k in range(8):
            a[base + k, pl.ds(base, 8), :] = jnp.where(sub >= k, rows[k], 0.0)
        for j in range(panel + 1, K // 8):
            new = []
            for k in range(8):
                acc = a[base + k, pl.ds(8 * j, 8), :]
                for p in range(k):
                    acc = acc - rows[p][k : k + 1, :] * new[p]
                new.append(acc * scale[k])
            for k in range(8):
                a[base + k, pl.ds(8 * j, 8), :] = new[k]
        if panel < K // 8 - 1:

            for i_block in range(panel + 1, K // 8):
                left = [a[base + k, cols(i_block), :] for k in range(8)]

                for j_block in range(i_block, K // 8):
                    right = [a[base + k, cols(j_block), :] for k in range(8)]
                    for i in range(8):
                        acc = a[8 * i_block + i, cols(j_block), :]
                        for k in range(8):
                            acc = acc - left[k][i : i + 1, :] * right[k]
                        a[8 * i_block + i, cols(j_block), :] = acc

    for i in range(8, K):
        a[i, pl.ds(0, i // 8 * 8), :] = jnp.zeros((i // 8 * 8, a.shape[2]), F32)


def factor_halved(s, a):
    @pl.loop(0, H // TURN)
    def _(step):
        at = [step * TURN + v for v in range(TURN)]
        turned = [s[:, q, :].T for q in at]
        for q, y in zip(at, turned):
            a[q] = y[:K]
            a[q + H] = y[K:]

    cholesky_lanes(a)

    @pl.loop(0, H // TURN)
    def _(step):
        at = [step * TURN + v for v in range(TURN)]
        turned = [jnp.concatenate([a[q], a[q + H]], axis=0).T for q in at]
        for q, y in zip(at, turned):
            s[:, q, :] = y


def packed(matrices):
    return matrices % 4 == 0


def slabs(matrices):
    return matrices // 4 * 5 if packed(matrices) else 2 * matrices


def lane(low, high):
    at = lax.broadcasted_iota(jnp.int32, (Q, 2 * K), 1)
    return (at >= low) & (at < high)


def pack(four):
    top = [x[:Q] for x in four]
    low = [jnp.where(lane(0, Q), pltpu.roll(x[Q:], Q, 1), x[Q:]) for x in four]
    gap = lane(K, K + H)
    return jnp.concatenate(
        [
            jnp.where(gap, pltpu.roll(top[3], K, 1), top[0]),
            jnp.where(gap, pltpu.roll(top[3], H, 1), top[1]),
            jnp.where(gap, pltpu.roll(top[3], 2 * K - H, 1), top[2]),
            jnp.where(lane(0, K), low[0], pltpu.roll(low[1], K, 1)),
            jnp.where(lane(0, K), low[2], pltpu.roll(low[3], K, 1)),
        ],
        axis=0,
    )


def rolled(x, by):
    return jnp.concatenate([x[:, 2 * K - by :], x[:, : 2 * K - by]], axis=1)


def unpack(unit):
    zero = jnp.zeros_like(unit[0])
    full = []
    for m in range(3):
        full.append((unit[m], jnp.where(lane(H, K), rolled(unit[m], K), zero)))
    first = jnp.where(lane(0, H), rolled(unit[0], K), rolled(unit[1], 2 * K - H))
    full.append((first, jnp.where(lane(H, K), rolled(unit[2], 2 * K - H), zero)))
    out = []
    for m, (block0, block2) in enumerate(full):
        low = unit[3 + m // 2] if m % 2 == 0 else rolled(unit[3 + m // 2], K)
        block1 = jnp.where(lane(Q, K), low, zero)
        block3 = jnp.where(lane(K - Q, K), rolled(low, K - Q), zero)
        out.append(jnp.concatenate([block0, block1, block2, block3], axis=0)[:, :K])
    return out


def factor_kernel(
    own,
    cols,
    at_ref,
    all_basis_ref,
    all_xfer_ref,
    fac_ref,
    gram1_ref,
    *refs,
):
    sent_refs = refs[:cols]
    xt, s, a, g0, basis_ref, xfer_ref, basis_sem, sem = refs[cols:]
    col = at_ref[1]
    first = col * own
    pairs = min(PAIRS, own // 2)

    def chunk(step):
        rows = pl.ds(2 * pairs * step, 2 * pairs)
        return pltpu.make_async_copy(all_basis_ref.at[rows], basis_ref.at[rows], basis_sem.at[step])

    for step in range(own // 2 // pairs):
        chunk(step).start()
    copy = pltpu.make_async_copy(all_xfer_ref.at[:, :, pl.ds(0, LANES)], xfer_ref, sem)
    copy.start()

    @pl.loop(0, own // 2 // pairs)
    def _(step):
        chunk(step).wait()
        at = [2 * step * pairs + c for c in range(2 * pairs)]
        points = [basis_ref[c] for c in at]
        grams = [mul(x, x, NT) for x in points]
        for c, gram in zip(at, grams):
            g0[c] = gram
            s[c] = halve(gram)

    copy.wait()
    unpack_transfers(xfer_ref, xt)

    @pl.loop(0, own // 2 // pairs)
    def _(step):
        base = step * pairs
        at = [2 * base + c for c in range(2 * pairs)]
        parents = lift_pairs([g0[c] for c in at], [unhalf(xt[first + c]) for c in at])
        for p, gram in enumerate(parents):
            gram1_ref[base + p] = gram
            s[own + base + p] = halve(gram)

    factor_halved(s, a)
    count = own + own // 2
    for g in range(count // 4):
        fac_ref[g] = pack([s[4 * g + m] for m in range(4)]).astype(BF)
    for e in range(cols):
        mine = [s[r * cols + jnp.bitwise_xor(col, e)] for r in range(count // cols)]
        start = 0
        for x in [pack(mine[n : n + 4]) for n in range(0, len(mine), 4)] if packed(len(mine)) else mine:
            for n in range(x.shape[0] // Q):
                sent_refs[e][start + n] = x[Q * n : Q * (n + 1)].astype(BF)
            start += x.shape[0] // Q


def own_factors(at, basis, xfer_lanes, cols):
    own = basis.shape[0]
    count = own + own // 2
    rows = (count + 7) // 8 * 8
    shapes = (
        jax.ShapeDtypeStruct((count // 4, 5 * Q, 2 * K), BF),
        jax.ShapeDtypeStruct((own // 2, K, K), F32),
    ) + (jax.ShapeDtypeStruct((slabs(count // cols), Q, 2 * K), BF),) * cols
    return pl.pallas_call(
        functools.partial(factor_kernel, own, cols),
        out_shape=shapes,
        in_specs=[
            SMEM,
            HBM,
            HBM,
        ],
        out_specs=(VMEM,) * len(shapes),
        scratch_shapes=[
            pltpu.VMEM((LANES, H, 2 * K), F32),
            pltpu.VMEM((rows, H, 2 * K), F32),
            pltpu.VMEM((K, K, rows), F32),
            pltpu.VMEM((own, K, K), F32),
            pltpu.VMEM(basis.shape, F32),
            pltpu.VMEM((K, K, LANES), F32),
            pltpu.SemaphoreType.DMA((own // 2 // min(PAIRS, own // 2),)),
            pltpu.SemaphoreType.DMA,
        ],
        compiler_params=pltpu.CompilerParams(vmem_limit_bytes=52 * 2**20),
        cost_estimate=cost(own * 2**24, 2**23),
    )(at, basis, xfer_lanes)


def chain_kernel(own, cols, at_ref, gram1_ref, xfer_ref, out_ref, xt):
    col = at_ref[1]
    unpack_transfers(xfer_ref, xt)
    grams = [gram1_ref[c] for c in range(own // 2)]
    offset = 0
    width = own * cols // 2
    while len(grams) > 1:
        here = len(grams)
        xfers = [unhalf(xt[offset + col * here + c]) for c in range(here)]
        offset += width
        width //= 2
        if here < 4:
            grams = lift_pairs(grams, xfers)
            continue
        here //= 2
        upper = [unhalf(xt[offset + col * here + c]) for c in range(here)]
        offset += width
        width //= 2
        xfers = [mul(upper[c // 2], x, NN) for c, x in enumerate(xfers)]
        low = lift_pairs(grams, xfers)
        grams = [x + y for x, y in zip(low[0::2], low[1::2])]
    shift = 0
    whole = None
    while width >= 1:
        xfer = unhalf(xt[offset + jnp.right_shift(col, shift)])
        whole = xfer if whole is None else mul(xfer, whole, NN)
        offset += width
        width //= 2
        shift += 1
    rest = halve(lift_all(grams, [whole])[0])
    for n in range(TERMS):
        term = rest.astype(BF)
        out_ref[2 * n] = term[:Q]
        out_ref[2 * n + 1] = term[Q:]
        rest = rest - term.astype(F32)


def lifted_root(at, gram1, xfer_lanes, own, cols):
    return pl.pallas_call(
        functools.partial(chain_kernel, own, cols),
        out_shape=jax.ShapeDtypeStruct((2 * TERMS, Q, 2 * K), BF),
        grid=(1,),
        in_specs=[
            SMEM,
            pl.BlockSpec(gram1.shape, lambda i: (0, 0, 0)),
            pl.BlockSpec((K, K, LANES), lambda i: (0, 0, 1)),
        ],
        out_specs=pl.BlockSpec((2 * TERMS, Q, 2 * K), lambda i: (0, 0, 0)),
        scratch_shapes=[pltpu.VMEM((LANES, H, 2 * K), F32)],
        compiler_params=PARAMS,
        cost_estimate=cost(own * 2**24, 2**22),
    )(at, gram1, xfer_lanes)


def top_kernel(leaves, at_ref, top_ref, *refs):
    pairs = leaves // 2
    parts, (anc_ref, root_ref, level_ref, s, a) = refs[:-5], refs[-5:]
    pair = jnp.right_shift(at_ref[0], 1)
    for m in range(pairs):
        terms = [part[m].reshape(H, 2 * K) for part in parts]
        while len(terms) > 1:
            terms = [x + y for x, y in zip(terms[0::2], terms[1::2])]
        level_ref[jnp.bitwise_xor(pair, m)] = terms[0]
    level = [unhalf(level_ref[m]) for m in range(pairs)]
    heights = []
    slot = 0
    off_top = 0
    while True:
        heights.append(slot)
        for m, gram in enumerate(level):
            s[slot + m] = halve(gram)
        slot += len(level)
        if len(level) == 1:
            break
        level_xfers = [top_ref[off_top + m].T for m in range(len(level))]
        off_top += len(level)
        level = lift_pairs(level, level_xfers)
    factor_halved(s, a)
    for h, start in enumerate(heights):
        anc_ref[0, h] = unhalf(s[start + jnp.right_shift(at_ref[0], h + 1)])
    root_ref[...] = unhalf(s[heights[-1]])


def top_factors(at, parts, top_transfer, leaves):
    height = leaves.bit_length() - 1
    rows = (leaves - 1 + 7) // 8 * 8
    return pl.pallas_call(
        functools.partial(top_kernel, leaves),
        out_shape=(
            jax.ShapeDtypeStruct((1, height, K, K), F32),
            jax.ShapeDtypeStruct((K, K), F32),
        ),
        in_specs=[SMEM, VMEM] + [VMEM] * len(parts),
        out_specs=(VMEM, VMEM),
        scratch_shapes=[
            pltpu.VMEM((leaves // 2, H, 2 * K), F32),
            pltpu.VMEM((rows, H, 2 * K), F32),
            pltpu.VMEM((K, K, rows), F32),
        ],
        compiler_params=PARAMS,
        cost_estimate=cost(2**22, 2**17),
    )(at, top_transfer, *parts)


def lane_groups(sizes):
    return [(which, lane) for which, size in enumerate(sizes) for lane in range(0, size, LANES)]


def turn_kernel(groups, *refs):
    blocks, cells_ref, bt = refs[:-2], refs[-2], refs[-1]
    for g, (which, first) in enumerate(groups):
        src = blocks[which]

        @pl.loop(0, H // TURN)
        def _(step):
            lanes = pl.ds(first, LANES)
            at = [step * TURN + v for v in range(TURN)]
            x = [jnp.concatenate([src[q, :, lanes], src[q + H, :, lanes]], axis=0) for q in at]
            turned = [y.astype(F32).T for y in x]
            for q, y in zip(at, turned):
                bt[:, q, :] = y

        @pl.loop(0, LANES // TURN)
        def _(step):
            at = [step * TURN + u for u in range(TURN)]
            cells = [unhalf(bt[b].astype(BF)) for b in at]
            for b, x in zip(at, cells):
                cells_ref[LANES * g + b] = x


def turned_blocks(blocks):
    groups = lane_groups([x.shape[2] for x in blocks])
    return pl.pallas_call(
        functools.partial(turn_kernel, groups),
        out_shape=jax.ShapeDtypeStruct((LANES * len(groups), K, K), BF),
        in_specs=[VMEM] * len(blocks),
        out_specs=VMEM,
        scratch_shapes=[pltpu.VMEM((LANES, H, 2 * K), F32)],
        compiler_params=PARAMS,
        cost_estimate=cost(2**20, 2**20),
    )(*blocks)


def join_kernel(inputs, *refs):
    pieces, out = refs[: inputs[0]], refs[sum(inputs) :]
    start = 0
    for x in pieces:
        out[0][pl.ds(start, x.shape[0])] = x[...]
        start += x.shape[0]
    if len(out) == 1:
        return
    for n, x in enumerate(pieces):
        last = x.shape[0] - 2 * TERMS
        total = x[last : last + 2].astype(F32)
        for t in range(1, TERMS):
            total = total + x[last + 2 * t : last + 2 * t + 2].astype(F32)
        out[1][n] = total
    start = 0
    for x in refs[inputs[0] : sum(inputs)]:
        out[2][pl.ds(start, x.shape[0])] = x[...]
        start += x.shape[0]


def joined(pieces, packs=()):
    shapes = [jax.ShapeDtypeStruct((sum(x.shape[0] for x in pieces), Q, 2 * K), BF)]
    if packs:
        shapes.append(jax.ShapeDtypeStruct((len(pieces), 2, Q, 2 * K), F32))
        shapes.append(jax.ShapeDtypeStruct((sum(x.shape[0] for x in packs), 5 * Q, 2 * K), BF))
    return pl.pallas_call(
        functools.partial(join_kernel, (len(pieces), len(packs))),
        out_shape=tuple(shapes),
        in_specs=[VMEM] * (len(pieces) + len(packs)),
        out_specs=(VMEM,) * len(shapes),
        compiler_params=PARAMS,
        cost_estimate=cost(0, 2**18),
    )(*pieces, *packs)


def bits(size):
    assert size & (size - 1) == 0
    return size.bit_length() - 1


def row_entry(sizes, at_ref, level, row):
    own, cols = sizes[:2]
    size = own >> level
    row = row - at_ref[0] * (size * cols)
    owner = jnp.bitwise_xor(jnp.right_shift(row, bits(size)), at_ref[1])
    return owner * (own + own // 2) + level * own + jnp.bitwise_and(row, size - 1)


def column_entry(sizes, at_ref, level, column):
    own, cols, leaves = sizes
    size = own >> level
    count = own + own // 2
    owner = jnp.right_shift(column, bits(size))
    away = jnp.bitwise_xor(jnp.right_shift(owner, bits(cols)), at_ref[0])
    part = jnp.bitwise_xor(jnp.bitwise_and(owner, cols - 1), at_ref[1])
    piece = jnp.bitwise_and(away, 1) * (leaves // 2) + jnp.right_shift(away, 1)
    entry = piece * count + part * (count // cols)
    within = jnp.right_shift(jnp.bitwise_and(column, size - 1), bits(cols))
    return entry + level * (own // cols) + within


def fill_column_table(table, start, ref, sizes):
    own, cols, leaves = sizes
    count = own + own // 2
    parts = count // cols
    step = slabs(parts)
    length = ref.shape[0] // (leaves // 2)

    @pl.loop(0, leaves // 2)
    def _(p):
        found = []
        for e in range(cols):
            first = p * length + e * step
            if packed(parts):
                for g in range(parts // 4):
                    found += unpack([ref[first + 5 * g + n] for n in range(5)])
            else:
                for r in range(parts):
                    two = [ref[first + 2 * r + n] for n in range(2)]
                    found.append(unhalf(jnp.concatenate(two, axis=0)))
        for n, x in enumerate(found):
            table[start + p * count + n] = x


def middle_kernel(groups, sizes, at_ref, *refs):
    pairs, (cells_ref, same_ref, other_ref, out_ref, table) = refs[:-5], refs[-5:]
    fill_column_table(table, 0, same_ref, sizes)
    fill_column_table(table, table.shape[0] // 2, other_ref, sizes)
    for g, (level, first) in enumerate(groups):

        @pl.loop(0, LANES // SLOTS)
        def _(step):
            at = [step * SLOTS + u for u in range(SLOTS)]
            cols = [table[column_entry(sizes, at_ref, level, pairs[level][1, first + b])] for b in at]
            cells = [cells_ref[LANES * g + b] for b in at]
            y = [lax.dot_general(x, c, NT, preferred_element_type=F32) for x, c in zip(cells, cols)]
            for b, z in zip(at, y):
                out_ref[LANES * g + b] = z.astype(BF)


def middle_products(sizes, at, pairs, cells, same_core, other_core):
    groups = lane_groups([x.shape[1] for x in pairs])
    return pl.pallas_call(
        functools.partial(middle_kernel, groups, sizes),
        out_shape=jax.ShapeDtypeStruct((cells.shape[0], K, K), BF),
        in_specs=[SMEM] * (1 + len(pairs)) + [VMEM] * 3,
        out_specs=VMEM,
        scratch_shapes=[pltpu.VMEM((sizes[2] * (sizes[0] + sizes[0] // 2), K, K), BF)],
        compiler_params=pltpu.CompilerParams(vmem_limit_bytes=36 * 2**20),
        cost_estimate=cost(cells.shape[0] * 2**19, 2**20),
    )(at, *pairs, cells, same_core, other_core)


def outer_kernel(groups, sizes, outs, orders, at_ref, *refs):
    pairs, counts, middle_ref = refs[:outs], refs[outs : 2 * outs], refs[2 * outs]
    pieces, out_refs = refs[2 * outs + 1 : -outs - 4], refs[-outs - 4 : -4]
    pt, table, ready, sem = refs[-4:]
    packs = (sizes[0] + sizes[0] // 2) // 4
    together = math.gcd(packs, 6)
    for piece, order in zip(pieces, orders):
        for n, e in enumerate(order):

            @pl.loop(0, packs // together)
            def _(step):
                at = [step * together + g for g in range(together)]
                units = [[piece[n * packs + g, Q * u : Q * (u + 1)] for u in range(5)] for g in at]
                full = [unpack(five) for five in units]
                for g, four in zip(at, full):
                    for m in range(4):
                        table[4 * (e * packs + g) + m] = four[m]

    copies = []
    for g, (which, first) in enumerate(groups):

        @pl.loop(0, LANES // SLOTS)
        def _(step):
            at = [step * SLOTS + u for u in range(SLOTS)]
            rows = [table[row_entry(sizes, at_ref, which, pairs[which][0, first + b])] for b in at]
            right = [middle_ref[LANES * g + b] for b in at]
            y = [lax.dot_general(r, x, NN, preferred_element_type=F32) for r, x in zip(rows, right)]
            y = [halve(z) for z in y]
            for b, z in zip(at, y):
                pt[b] = z

        keep = lax.broadcasted_iota(jnp.int32, (2 * K, LANES), 1) < counts[which][0] - first

        @pl.loop(0, H // TURN)
        def _(step):
            at = [step * TURN + v for v in range(TURN)]
            turned = [pt[:, q, :].T for q in at]
            for q, y in zip(at, turned):
                y = jnp.where(keep, y, 0.0).astype(BF)
                ready[g, q] = y[:K]
                ready[g, q + H] = y[K:]

        out = out_refs[which].at[:, :, pl.ds(first, LANES)]
        copies.append(pltpu.make_async_copy(ready.at[g], out, sem.at[g]))
        copies[-1].start()
    for copy in copies:
        copy.wait()


def outer_products(sizes, at, pairs, counts, middle, pieces, orders):
    slots = [x.shape[1] for x in pairs]
    groups = lane_groups(slots)
    entries = 4 * sum(x.shape[0] for x in pieces)
    return pl.pallas_call(
        functools.partial(outer_kernel, groups, sizes, len(slots), orders),
        out_shape=tuple(jax.ShapeDtypeStruct((K, K, size), BF) for size in slots),
        in_specs=[SMEM] * (1 + 2 * len(slots)) + [VMEM] * (1 + len(pieces)),
        out_specs=(ANY,) * len(slots),
        scratch_shapes=[
            pltpu.VMEM((LANES, H, 2 * K), F32),
            pltpu.VMEM((entries, K, K), BF),
            pltpu.VMEM((len(groups), K, K, LANES), BF),
            pltpu.SemaphoreType.DMA((len(groups),)),
        ],
        compiler_params=PARAMS,
        cost_estimate=cost(len(groups) * 2**26, 2**22),
    )(at, *pairs, *counts, middle, *pieces)


def swapped(x, axis, d):
    return lax.ppermute(x, axis, [(i, i ^ d) for i in range(lax.axis_size(axis))])


def on_device(basis, transfer, top_transfer, blocks0, pairs0, counts0, blocks1, pairs1, counts1):
    own = basis.shape[0]
    cols = lax.axis_size("col")
    leaves = lax.axis_size("leaf")
    at = jnp.stack([lax.axis_index("leaf"), lax.axis_index("col")]).astype(jnp.int32)
    xfer_lanes = jnp.transpose(transfer, (1, 2, 0))
    lanes0, lanes1 = jnp.transpose(blocks0, (1, 2, 0)), jnp.transpose(blocks1, (1, 2, 0))
    sizes = (own, cols, leaves)
    pairs = (jnp.transpose(pairs0), jnp.transpose(pairs1))

    factors, gram1, *sent = own_factors(at, basis, xfer_lanes, cols)
    received = [swapped(sent[d], "col", d) for d in range(1, cols)]
    terms = lifted_root(at, gram1, xfer_lanes, own, cols)
    received, terms, factors, lanes0, lanes1 = lax.optimization_barrier(
        (received, terms, factors, lanes0, lanes1)
    )

    (part,) = joined([sent[0]] + received + [terms])
    chips = [swapped(part, "leaf", d) for d in range(2, leaves, 2)]
    bit = cols // 2
    early = swapped(factors, "col", bit)
    cells = turned_blocks((lanes0, lanes1))
    chips, early, cells = lax.optimization_barrier((chips, early, cells))

    same_core, pair_part, rows = joined([part] + chips, [factors, early])
    other_core = swapped(same_core, "leaf", 1)
    orders = [0, bit]
    while True:
        bit //= 2
        forwarded = swapped(rows, "col", bit)
        orders = [orders, [e ^ bit for e in orders]]
        if bit == 1:
            break
        rows = jnp.concatenate([rows, forwarded], axis=0)
        orders = orders[0] + orders[1]
    there = other_core.reshape(leaves // 2, part.shape[0], Q, 2 * K)[:, -2 * TERMS :].astype(F32)
    other_part = there[:, 0:2]
    for t in range(1, TERMS):
        other_part = other_part + there[:, 2 * t : 2 * t + 2]
    pair_part = pair_part + other_part
    for d in range(1, bits(cols)):
        pair_part = pair_part + swapped(pair_part, "col", cols >> d)
    middle = middle_products(sizes, at, pairs, cells, same_core, other_core)
    pair_part, middle = lax.optimization_barrier((pair_part, middle))
    tops = [pair_part, swapped(pair_part, "col", 1)]
    out0, out1 = outer_products(
        sizes, at, pairs, (counts0, counts1), middle, [rows, forwarded], orders
    )
    ancestors, root = top_factors(at, tops, top_transfer, leaves)
    return (jnp.transpose(out0, (2, 0, 1)), jnp.transpose(out1, (2, 0, 1)), root, ancestors)


def solution(mesh):
    in_specs = (
        P(("leaf", "col"), None, None),
        P("leaf", None, None),
        P(),
        P(("leaf", "col"), None, None),
        P(("leaf", "col"), None),
        P(("leaf", "col")),
        P(("leaf", "col"), None, None),
        P(("leaf", "col"), None),
        P(("leaf", "col")),
    )
    out_specs = (
        P(("leaf", "col"), None, None),
        P(("leaf", "col"), None, None),
        P(),
        P("leaf", None, None, None),
    )
    return jax.shard_map(
        on_device, mesh=mesh, in_specs=in_specs, out_specs=out_specs, check_vma=False
    )
```

```python
import functools
import math

import jax
import jax.numpy as jnp
from jax import lax
from jax.experimental import pallas as pl
from jax.experimental.pallas import tpu as pltpu
from jax.sharding import PartitionSpec as P

BF, F32 = jnp.bfloat16, jnp.float32
EXACT = lax.Precision.HIGHEST
NT = (((1,), (1,)), ((), ()))
NN = (((1,), (0,)), ((), ()))
K = 64
H = K // 2
Q = K // 4
LANES = 128
SMEM = pl.BlockSpec(memory_space=pltpu.SMEM)
VMEM = pl.BlockSpec(memory_space=pltpu.VMEM)
ANY = pl.BlockSpec(memory_space=pl.ANY)
HBM = pl.BlockSpec(memory_space=pltpu.HBM)
TERMS = 3
TURN = 16
SLOTS = 128
PAIRS = 8
PARAMS = pltpu.CompilerParams(vmem_limit_bytes=24 * 2**20)


def unhalf(x):
    return jnp.concatenate([x[:, :K], x[:, K:]], axis=0)


def halve(x):
    return jnp.concatenate([x[:H], x[H:]], axis=1)


def bf16_terms(x):
    high = x.astype(BF)
    rest = x - high.astype(F32)
    mid = rest.astype(BF)
    return high, mid, (rest - mid.astype(F32)).astype(BF)


def mul(x, y, dims):
    if x.shape[1] != K:
        return lax.dot_general(x, y, dims, precision=EXACT, preferred_element_type=F32)
    h, m, l = bf16_terms(x)
    p, q, r = bf16_terms(y)
    axis = dims[0][1][0]
    dot = functools.partial(lax.dot_general, dimension_numbers=dims, preferred_element_type=F32)
    main = dot(jnp.concatenate([h, h, m, m], axis=1), jnp.concatenate([p, q, p, q], axis=axis))
    return main + dot(jnp.concatenate([h, l], axis=1), jnp.concatenate([r, p], axis=axis))


def lift_all(grams, xfers_t):
    halfway = [mul(f, g, NN) for f, g in zip(xfers_t, grams)]
    return [mul(t, f, NT) for t, f in zip(halfway, xfers_t)]


def lift_pairs(grams, xfers_t):
    lifted = lift_all(grams, xfers_t)
    return [low + high for low, high in zip(lifted[0::2], lifted[1::2])]


def cost(flops, size):
    return pl.CostEstimate(flops=flops, bytes_accessed=size, transcendentals=0)


def unpack_transfers(xfer_ref, xt):
    @pl.loop(0, H // TURN)
    def _(step):
        at = [step * TURN + v for v in range(TURN)]
        turned = [jnp.concatenate([xfer_ref[:, q, :], xfer_ref[:, q + H, :]], axis=0).T for q in at]
        for q, y in zip(at, turned):
            xt[:, q, :] = y


def cholesky_lanes(a):
    sub = lax.broadcasted_iota(jnp.int32, (8, a.shape[2]), 0)

    def cols(block):
        return pl.ds(8 * block, 8)

    for panel in range(K // 8):
        base = 8 * panel
        scale = []
        rows = [a[base + k, pl.ds(base, 8), :] for k in range(8)]
        for k in range(8):
            scale.append(lax.rsqrt(rows[k][k : k + 1, :]))
            rows[k] = rows[k] * scale[k]
            for i in range(k + 1, 8):
                rows[i] = rows[i] - rows[k][i : i + 1, :] * rows[k]
        for k in range(8):
            a[base + k, pl.ds(base, 8), :] = jnp.where(sub >= k, rows[k], 0.0)
        for j in range(panel + 1, K // 8):
            new = []
            for k in range(8):
                acc = a[base + k, pl.ds(8 * j, 8), :]
                for p in range(k):
                    acc = acc - rows[p][k : k + 1, :] * new[p]
                new.append(acc * scale[k])
            for k in range(8):
                a[base + k, pl.ds(8 * j, 8), :] = new[k]
        if panel < K // 8 - 1:

            for i_block in range(panel + 1, K // 8):
                left = [a[base + k, cols(i_block), :] for k in range(8)]

                for j_block in range(i_block, K // 8):
                    right = [a[base + k, cols(j_block), :] for k in range(8)]
                    for i in range(8):
                        acc = a[8 * i_block + i, cols(j_block), :]
                        for k in range(8):
                            acc = acc - left[k][i : i + 1, :] * right[k]
                        a[8 * i_block + i, cols(j_block), :] = acc

    for i in range(8, K):
        a[i, pl.ds(0, i // 8 * 8), :] = jnp.zeros((i // 8 * 8, a.shape[2]), F32)


def factor_halved(s, a):
    @pl.loop(0, H // TURN)
    def _(step):
        at = [step * TURN + v for v in range(TURN)]
        turned = [s[:, q, :].T for q in at]
        for q, y in zip(at, turned):
            a[q] = y[:K]
            a[q + H] = y[K:]

    cholesky_lanes(a)

    @pl.loop(0, H // TURN)
    def _(step):
        at = [step * TURN + v for v in range(TURN)]
        turned = [jnp.concatenate([a[q], a[q + H]], axis=0).T for q in at]
        for q, y in zip(at, turned):
            s[:, q, :] = y


def packed(matrices):
    return matrices % 4 == 0


def slabs(matrices):
    return matrices // 4 * 5 if packed(matrices) else 2 * matrices


def lane(low, high):
    at = lax.broadcasted_iota(jnp.int32, (Q, 2 * K), 1)
    return (at >= low) & (at < high)


def pack(four):
    top = [x[:Q] for x in four]
    low = [jnp.where(lane(0, Q), pltpu.roll(x[Q:], Q, 1), x[Q:]) for x in four]
    gap = lane(K, K + H)
    return jnp.concatenate(
        [
            jnp.where(gap, pltpu.roll(top[3], K, 1), top[0]),
            jnp.where(gap, pltpu.roll(top[3], H, 1), top[1]),
            jnp.where(gap, pltpu.roll(top[3], 2 * K - H, 1), top[2]),
            jnp.where(lane(0, K), low[0], pltpu.roll(low[1], K, 1)),
            jnp.where(lane(0, K), low[2], pltpu.roll(low[3], K, 1)),
        ],
        axis=0,
    )


def rolled(x, by):
    return jnp.concatenate([x[:, 2 * K - by :], x[:, : 2 * K - by]], axis=1)


def unpack(unit):
    zero = jnp.zeros_like(unit[0])
    full = []
    for m in range(3):
        full.append((unit[m], jnp.where(lane(H, K), rolled(unit[m], K), zero)))
    first = jnp.where(lane(0, H), rolled(unit[0], K), rolled(unit[1], 2 * K - H))
    full.append((first, jnp.where(lane(H, K), rolled(unit[2], 2 * K - H), zero)))
    out = []
    for m, (block0, block2) in enumerate(full):
        low = unit[3 + m // 2] if m % 2 == 0 else rolled(unit[3 + m // 2], K)
        block1 = jnp.where(lane(Q, K), low, zero)
        block3 = jnp.where(lane(K - Q, K), rolled(low, K - Q), zero)
        out.append(jnp.concatenate([block0, block1, block2, block3], axis=0)[:, :K])
    return out


def factor_kernel(
    own,
    cols,
    at_ref,
    all_basis_ref,
    all_xfer_ref,
    fac_ref,
    gram1_ref,
    *refs,
):
    sent_refs = refs[:cols]
    xt, s, a, g0, basis_ref, xfer_ref, basis_sem, sem = refs[cols:]
    col = at_ref[1]
    first = col * own
    pairs = min(PAIRS, own // 2)

    def chunk(step):
        rows = pl.ds(2 * pairs * step, 2 * pairs)
        return pltpu.make_async_copy(all_basis_ref.at[rows], basis_ref.at[rows], basis_sem.at[step])

    for step in range(own // 2 // pairs):
        chunk(step).start()
    copy = pltpu.make_async_copy(all_xfer_ref.at[:, :, pl.ds(0, LANES)], xfer_ref, sem)
    copy.start()

    @pl.loop(0, own // 2 // pairs)
    def _(step):
        chunk(step).wait()
        at = [2 * step * pairs + c for c in range(2 * pairs)]
        points = [basis_ref[c] for c in at]
        grams = [mul(x, x, NT) for x in points]
        for c, gram in zip(at, grams):
            g0[c] = gram
            s[c] = halve(gram)

    copy.wait()
    unpack_transfers(xfer_ref, xt)

    @pl.loop(0, own // 2 // pairs)
    def _(step):
        base = step * pairs
        at = [2 * base + c for c in range(2 * pairs)]
        parents = lift_pairs([g0[c] for c in at], [unhalf(xt[first + c]) for c in at])
        for p, gram in enumerate(parents):
            gram1_ref[base + p] = gram
            s[own + base + p] = halve(gram)

    factor_halved(s, a)
    count = own + own // 2
    for g in range(count // 4):
        fac_ref[g] = pack([s[4 * g + m] for m in range(4)]).astype(BF)
    for e in range(cols):
        mine = [s[r * cols + jnp.bitwise_xor(col, e)] for r in range(count // cols)]
        start = 0
        for x in [pack(mine[n : n + 4]) for n in range(0, len(mine), 4)] if packed(len(mine)) else mine:
            for n in range(x.shape[0] // Q):
                sent_refs[e][start + n] = x[Q * n : Q * (n + 1)].astype(BF)
            start += x.shape[0] // Q


def own_factors(at, basis, xfer_lanes, cols):
    own = basis.shape[0]
    count = own + own // 2
    rows = (count + 7) // 8 * 8
    shapes = (
        jax.ShapeDtypeStruct((count // 4, 5 * Q, 2 * K), BF),
        jax.ShapeDtypeStruct((own // 2, K, K), F32),
    ) + (jax.ShapeDtypeStruct((slabs(count // cols), Q, 2 * K), BF),) * cols
    return pl.pallas_call(
        functools.partial(factor_kernel, own, cols),
        out_shape=shapes,
        in_specs=[
            SMEM,
            HBM,
            HBM,
        ],
        out_specs=(VMEM,) * len(shapes),
        scratch_shapes=[
            pltpu.VMEM((LANES, H, 2 * K), F32),
            pltpu.VMEM((rows, H, 2 * K), F32),
            pltpu.VMEM((K, K, rows), F32),
            pltpu.VMEM((own, K, K), F32),
            pltpu.VMEM(basis.shape, F32),
            pltpu.VMEM((K, K, LANES), F32),
            pltpu.SemaphoreType.DMA((own // 2 // min(PAIRS, own // 2),)),
            pltpu.SemaphoreType.DMA,
        ],
        compiler_params=pltpu.CompilerParams(vmem_limit_bytes=52 * 2**20),
        cost_estimate=cost(own * 2**24, 2**23),
    )(at, basis, xfer_lanes)


def chain_kernel(own, cols, at_ref, gram1_ref, xfer_ref, out_ref, xt):
    col = at_ref[1]
    unpack_transfers(xfer_ref, xt)
    grams = [gram1_ref[c] for c in range(own // 2)]
    offset = 0
    width = own * cols // 2
    while len(grams) > 1:
        here = len(grams)
        xfers = [unhalf(xt[offset + col * here + c]) for c in range(here)]
        offset += width
        width //= 2
        if here < 4:
            grams = lift_pairs(grams, xfers)
            continue
        here //= 2
        upper = [unhalf(xt[offset + col * here + c]) for c in range(here)]
        offset += width
        width //= 2
        xfers = [mul(upper[c // 2], x, NN) for c, x in enumerate(xfers)]
        low = lift_pairs(grams, xfers)
        grams = [x + y for x, y in zip(low[0::2], low[1::2])]
    shift = 0
    whole = None
    while width >= 1:
        xfer = unhalf(xt[offset + jnp.right_shift(col, shift)])
        whole = xfer if whole is None else mul(xfer, whole, NN)
        offset += width
        width //= 2
        shift += 1
    rest = halve(lift_all(grams, [whole])[0])
    for n in range(TERMS):
        term = rest.astype(BF)
        out_ref[2 * n] = term[:Q]
        out_ref[2 * n + 1] = term[Q:]
        rest = rest - term.astype(F32)


def lifted_root(at, gram1, xfer_lanes, own, cols):
    return pl.pallas_call(
        functools.partial(chain_kernel, own, cols),
        out_shape=jax.ShapeDtypeStruct((2 * TERMS, Q, 2 * K), BF),
        grid=(1,),
        in_specs=[
            SMEM,
            pl.BlockSpec(gram1.shape, lambda i: (0, 0, 0)),
            pl.BlockSpec((K, K, LANES), lambda i: (0, 0, 1)),
        ],
        out_specs=pl.BlockSpec((2 * TERMS, Q, 2 * K), lambda i: (0, 0, 0)),
        scratch_shapes=[pltpu.VMEM((LANES, H, 2 * K), F32)],
        compiler_params=PARAMS,
        cost_estimate=cost(own * 2**24, 2**22),
    )(at, gram1, xfer_lanes)


def top_kernel(leaves, at_ref, top_ref, *refs):
    pairs = leaves // 2
    parts, (anc_ref, root_ref, level_ref, s, a) = refs[:-5], refs[-5:]
    pair = jnp.right_shift(at_ref[0], 1)
    for m in range(pairs):
        terms = [part[m].reshape(H, 2 * K) for part in parts]
        while len(terms) > 1:
            terms = [x + y for x, y in zip(terms[0::2], terms[1::2])]
        level_ref[jnp.bitwise_xor(pair, m)] = terms[0]
    level = [unhalf(level_ref[m]) for m in range(pairs)]
    heights = []
    slot = 0
    off_top = 0
    while True:
        heights.append(slot)
        for m, gram in enumerate(level):
            s[slot + m] = halve(gram)
        slot += len(level)
        if len(level) == 1:
            break
        level_xfers = [top_ref[off_top + m].T for m in range(len(level))]
        off_top += len(level)
        level = lift_pairs(level, level_xfers)
    factor_halved(s, a)
    for h, start in enumerate(heights):
        anc_ref[0, h] = unhalf(s[start + jnp.right_shift(at_ref[0], h + 1)])
    root_ref[...] = unhalf(s[heights[-1]])


def top_factors(at, parts, top_transfer, leaves):
    height = leaves.bit_length() - 1
    rows = (leaves - 1 + 7) // 8 * 8
    return pl.pallas_call(
        functools.partial(top_kernel, leaves),
        out_shape=(
            jax.ShapeDtypeStruct((1, height, K, K), F32),
            jax.ShapeDtypeStruct((K, K), F32),
        ),
        in_specs=[SMEM, VMEM] + [VMEM] * len(parts),
        out_specs=(VMEM, VMEM),
        scratch_shapes=[
            pltpu.VMEM((leaves // 2, H, 2 * K), F32),
            pltpu.VMEM((rows, H, 2 * K), F32),
            pltpu.VMEM((K, K, rows), F32),
        ],
        compiler_params=PARAMS,
        cost_estimate=cost(2**22, 2**17),
    )(at, top_transfer, *parts)


def lane_groups(sizes):
    return [(which, lane) for which, size in enumerate(sizes) for lane in range(0, size, LANES)]


def turn_kernel(groups, *refs):
    blocks, cells_ref, bt = refs[:-2], refs[-2], refs[-1]
    for g, (which, first) in enumerate(groups):
        src = blocks[which]

        @pl.loop(0, H // TURN)
        def _(step):
            lanes = pl.ds(first, LANES)
            at = [step * TURN + v for v in range(TURN)]
            x = [jnp.concatenate([src[q, :, lanes], src[q + H, :, lanes]], axis=0) for q in at]
            turned = [y.astype(F32).T for y in x]
            for q, y in zip(at, turned):
                bt[:, q, :] = y

        @pl.loop(0, LANES // TURN)
        def _(step):
            at = [step * TURN + u for u in range(TURN)]
            cells = [unhalf(bt[b].astype(BF)) for b in at]
            for b, x in zip(at, cells):
                cells_ref[LANES * g + b] = x


def turned_blocks(blocks):
    groups = lane_groups([x.shape[2] for x in blocks])
    return pl.pallas_call(
        functools.partial(turn_kernel, groups),
        out_shape=jax.ShapeDtypeStruct((LANES * len(groups), K, K), BF),
        in_specs=[VMEM] * len(blocks),
        out_specs=VMEM,
        scratch_shapes=[pltpu.VMEM((LANES, H, 2 * K), F32)],
        compiler_params=PARAMS,
        cost_estimate=cost(2**20, 2**20),
    )(*blocks)


def join_kernel(inputs, *refs):
    pieces, out = refs[: inputs[0]], refs[sum(inputs) :]
    start = 0
    for x in pieces:
        out[0][pl.ds(start, x.shape[0])] = x[...]
        start += x.shape[0]
    if len(out) == 1:
        return
    for n, x in enumerate(pieces):
        last = x.shape[0] - 2 * TERMS
        total = x[last : last + 2].astype(F32)
        for t in range(1, TERMS):
            total = total + x[last + 2 * t : last + 2 * t + 2].astype(F32)
        out[1][n] = total
    start = 0
    for x in refs[inputs[0] : sum(inputs)]:
        out[2][pl.ds(start, x.shape[0])] = x[...]
        start += x.shape[0]


def joined(pieces, packs=()):
    shapes = [jax.ShapeDtypeStruct((sum(x.shape[0] for x in pieces), Q, 2 * K), BF)]
    if packs:
        shapes.append(jax.ShapeDtypeStruct((len(pieces), 2, Q, 2 * K), F32))
        shapes.append(jax.ShapeDtypeStruct((sum(x.shape[0] for x in packs), 5 * Q, 2 * K), BF))
    return pl.pallas_call(
        functools.partial(join_kernel, (len(pieces), len(packs))),
        out_shape=tuple(shapes),
        in_specs=[VMEM] * (len(pieces) + len(packs)),
        out_specs=(VMEM,) * len(shapes),
        compiler_params=PARAMS,
        cost_estimate=cost(0, 2**18),
    )(*pieces, *packs)


def bits(size):
    assert size & (size - 1) == 0
    return size.bit_length() - 1


def row_entry(sizes, at_ref, level, row):
    own, cols = sizes[:2]
    size = own >> level
    row = row - at_ref[0] * (size * cols)
    owner = jnp.bitwise_xor(jnp.right_shift(row, bits(size)), at_ref[1])
    return owner * (own + own // 2) + level * own + jnp.bitwise_and(row, size - 1)


def column_entry(sizes, at_ref, level, column):
    own, cols, leaves = sizes
    size = own >> level
    count = own + own // 2
    owner = jnp.right_shift(column, bits(size))
    away = jnp.bitwise_xor(jnp.right_shift(owner, bits(cols)), at_ref[0])
    part = jnp.bitwise_xor(jnp.bitwise_and(owner, cols - 1), at_ref[1])
    piece = jnp.bitwise_and(away, 1) * (leaves // 2) + jnp.right_shift(away, 1)
    entry = piece * count + part * (count // cols)
    within = jnp.right_shift(jnp.bitwise_and(column, size - 1), bits(cols))
    return entry + level * (own // cols) + within


def fill_column_table(table, start, ref, sizes):
    own, cols, leaves = sizes
    count = own + own // 2
    parts = count // cols
    step = slabs(parts)
    length = ref.shape[0] // (leaves // 2)

    @pl.loop(0, leaves // 2)
    def _(p):
        found = []
        for e in range(cols):
            first = p * length + e * step
            if packed(parts):
                for g in range(parts // 4):
                    found += unpack([ref[first + 5 * g + n] for n in range(5)])
            else:
                for r in range(parts):
                    two = [ref[first + 2 * r + n] for n in range(2)]
                    found.append(unhalf(jnp.concatenate(two, axis=0)))
        for n, x in enumerate(found):
            table[start + p * count + n] = x


def middle_kernel(groups, sizes, at_ref, *refs):
    pairs, (cells_ref, same_ref, other_ref, out_ref, table) = refs[:-5], refs[-5:]
    fill_column_table(table, 0, same_ref, sizes)
    fill_column_table(table, table.shape[0] // 2, other_ref, sizes)
    for g, (level, first) in enumerate(groups):

        @pl.loop(0, LANES // SLOTS)
        def _(step):
            at = [step * SLOTS + u for u in range(SLOTS)]
            cols = [table[column_entry(sizes, at_ref, level, pairs[level][1, first + b])] for b in at]
            cells = [cells_ref[LANES * g + b] for b in at]
            y = [lax.dot_general(x, c, NT, preferred_element_type=F32) for x, c in zip(cells, cols)]
            for b, z in zip(at, y):
                out_ref[LANES * g + b] = z.astype(BF)


def middle_products(sizes, at, pairs, cells, same_core, other_core):
    groups = lane_groups([x.shape[1] for x in pairs])
    return pl.pallas_call(
        functools.partial(middle_kernel, groups, sizes),
        out_shape=jax.ShapeDtypeStruct((cells.shape[0], K, K), BF),
        in_specs=[SMEM] * (1 + len(pairs)) + [VMEM] * 3,
        out_specs=VMEM,
        scratch_shapes=[pltpu.VMEM((sizes[2] * (sizes[0] + sizes[0] // 2), K, K), BF)],
        compiler_params=pltpu.CompilerParams(vmem_limit_bytes=36 * 2**20),
        cost_estimate=cost(cells.shape[0] * 2**19, 2**20),
    )(at, *pairs, cells, same_core, other_core)


def outer_kernel(groups, sizes, outs, orders, at_ref, *refs):
    pairs, counts, middle_ref = refs[:outs], refs[outs : 2 * outs], refs[2 * outs]
    pieces, out_refs = refs[2 * outs + 1 : -outs - 4], refs[-outs - 4 : -4]
    pt, table, ready, sem = refs[-4:]
    packs = (sizes[0] + sizes[0] // 2) // 4
    together = math.gcd(packs, 6)
    for piece, order in zip(pieces, orders):
        for n, e in enumerate(order):

            @pl.loop(0, packs // together)
            def _(step):
                at = [step * together + g for g in range(together)]
                units = [[piece[n * packs + g, Q * u : Q * (u + 1)] for u in range(5)] for g in at]
                full = [unpack(five) for five in units]
                for g, four in zip(at, full):
                    for m in range(4):
                        table[4 * (e * packs + g) + m] = four[m]

    copies = []
    for g, (which, first) in enumerate(groups):

        @pl.loop(0, LANES // SLOTS)
        def _(step):
            at = [step * SLOTS + u for u in range(SLOTS)]
            rows = [table[row_entry(sizes, at_ref, which, pairs[which][0, first + b])] for b in at]
            right = [middle_ref[LANES * g + b] for b in at]
            y = [lax.dot_general(r, x, NN, preferred_element_type=F32) for r, x in zip(rows, right)]
            y = [halve(z) for z in y]
            for b, z in zip(at, y):
                pt[b] = z

        keep = lax.broadcasted_iota(jnp.int32, (2 * K, LANES), 1) < counts[which][0] - first

        @pl.loop(0, H // TURN)
        def _(step):
            at = [step * TURN + v for v in range(TURN)]
            turned = [pt[:, q, :].T for q in at]
            for q, y in zip(at, turned):
                y = jnp.where(keep, y, 0.0).astype(BF)
                ready[g, q] = y[:K]
                ready[g, q + H] = y[K:]

        out = out_refs[which].at[:, :, pl.ds(first, LANES)]
        copies.append(pltpu.make_async_copy(ready.at[g], out, sem.at[g]))
        copies[-1].start()
    for copy in copies:
        copy.wait()


def outer_products(sizes, at, pairs, counts, middle, pieces, orders):
    slots = [x.shape[1] for x in pairs]
    groups = lane_groups(slots)
    entries = 4 * sum(x.shape[0] for x in pieces)
    return pl.pallas_call(
        functools.partial(outer_kernel, groups, sizes, len(slots), orders),
        out_shape=tuple(jax.ShapeDtypeStruct((K, K, size), BF) for size in slots),
        in_specs=[SMEM] * (1 + 2 * len(slots)) + [VMEM] * (1 + len(pieces)),
        out_specs=(ANY,) * len(slots),
        scratch_shapes=[
            pltpu.VMEM((LANES, H, 2 * K), F32),
            pltpu.VMEM((entries, K, K), BF),
            pltpu.VMEM((len(groups), K, K, LANES), BF),
            pltpu.SemaphoreType.DMA((len(groups),)),
        ],
        compiler_params=PARAMS,
        cost_estimate=cost(len(groups) * 2**26, 2**22),
    )(at, *pairs, *counts, middle, *pieces)


def swapped(x, axis, d):
    return lax.ppermute(x, axis, [(i, i ^ d) for i in range(lax.axis_size(axis))])


def on_device(basis, transfer, top_transfer, blocks0, pairs0, counts0, blocks1, pairs1, counts1):
    own = basis.shape[0]
    cols = lax.axis_size("col")
    leaves = lax.axis_size("leaf")
    at = jnp.stack([lax.axis_index("leaf"), lax.axis_index("col")]).astype(jnp.int32)
    xfer_lanes = jnp.transpose(transfer, (1, 2, 0))
    lanes0, lanes1 = jnp.transpose(blocks0, (1, 2, 0)), jnp.transpose(blocks1, (1, 2, 0))
    sizes = (own, cols, leaves)
    pairs = (jnp.transpose(pairs0), jnp.transpose(pairs1))

    factors, gram1, *sent = own_factors(at, basis, xfer_lanes, cols)
    received = [swapped(sent[d], "col", d) for d in range(1, cols)]
    terms = lifted_root(at, gram1, xfer_lanes, own, cols)
    received, terms, factors, lanes0, lanes1 = lax.optimization_barrier(
        (received, terms, factors, lanes0, lanes1)
    )

    (part,) = joined([sent[0]] + received + [terms])
    chips = [swapped(part, "leaf", d) for d in range(2, leaves, 2)]
    bit = cols // 2
    early = swapped(factors, "col", bit)
    cells = turned_blocks((lanes0, lanes1))
    chips, early, cells = lax.optimization_barrier((chips, early, cells))

    same_core, pair_part, rows = joined([part] + chips, [factors, early])
    other_core = swapped(same_core, "leaf", 1)
    orders = [0, bit]
    while True:
        bit //= 2
        forwarded = swapped(rows, "col", bit)
        orders = [orders, [e ^ bit for e in orders]]
        if bit == 1:
            break
        rows = jnp.concatenate([rows, forwarded], axis=0)
        orders = orders[0] + orders[1]
    there = other_core.reshape(leaves // 2, part.shape[0], Q, 2 * K)[:, -2 * TERMS :].astype(F32)
    other_part = there[:, 0:2]
    for t in range(1, TERMS):
        other_part = other_part + there[:, 2 * t : 2 * t + 2]
    pair_part = pair_part + other_part
    tops = [pair_part] + [swapped(pair_part, "col", d) for d in range(1, cols)]
    middle = middle_products(sizes, at, pairs, cells, same_core, other_core)
    ancestors, root = top_factors(at, tops, top_transfer, leaves)
    middle, ancestors, root = lax.optimization_barrier((middle, ancestors, root))
    out0, out1 = outer_products(
        sizes, at, pairs, (counts0, counts1), middle, [rows, forwarded], orders
    )
    return (jnp.transpose(out0, (2, 0, 1)), jnp.transpose(out1, (2, 0, 1)), root, ancestors)


def solution(mesh):
    in_specs = (
        P(("leaf", "col"), None, None),
        P("leaf", None, None),
        P(),
        P(("leaf", "col"), None, None),
        P(("leaf", "col"), None),
        P(("leaf", "col")),
        P(("leaf", "col"), None, None),
        P(("leaf", "col"), None),
        P(("leaf", "col")),
    )
    out_specs = (
        P(("leaf", "col"), None, None),
        P(("leaf", "col"), None, None),
        P(),
        P("leaf", None, None, None),
    )
    return jax.shard_map(
        on_device, mesh=mesh, in_specs=in_specs, out_specs=out_specs, check_vma=False
    )
```

```python
import functools
import math

import jax
import jax.numpy as jnp
from jax import lax
from jax.experimental import pallas as pl
from jax.experimental.pallas import tpu as pltpu
from jax.sharding import PartitionSpec as P

BF, F32 = jnp.bfloat16, jnp.float32
EXACT = lax.Precision.HIGHEST
NT = (((1,), (1,)), ((), ()))
NN = (((1,), (0,)), ((), ()))
K = 64
H = K // 2
Q = K // 4
LANES = 128
SMEM = pl.BlockSpec(memory_space=pltpu.SMEM)
VMEM = pl.BlockSpec(memory_space=pltpu.VMEM)
ANY = pl.BlockSpec(memory_space=pl.ANY)
HBM = pl.BlockSpec(memory_space=pltpu.HBM)
TERMS = 3
TURN = 16
SLOTS = 128
PAIRS = 8
PARAMS = pltpu.CompilerParams(vmem_limit_bytes=24 * 2**20)


def unhalf(x):
    return jnp.concatenate([x[:, :K], x[:, K:]], axis=0)


def halve(x):
    return jnp.concatenate([x[:H], x[H:]], axis=1)


def bf16_terms(x):
    high = x.astype(BF)
    rest = x - high.astype(F32)
    mid = rest.astype(BF)
    return high, mid, (rest - mid.astype(F32)).astype(BF)


def mul(x, y, dims):
    if x.shape[1] != K:
        return lax.dot_general(x, y, dims, precision=EXACT, preferred_element_type=F32)
    h, m, l = bf16_terms(x)
    p, q, r = bf16_terms(y)
    axis = dims[0][1][0]
    dot = functools.partial(lax.dot_general, dimension_numbers=dims, preferred_element_type=F32)
    main = dot(jnp.concatenate([h, h, m, m], axis=1), jnp.concatenate([p, q, p, q], axis=axis))
    return main + dot(jnp.concatenate([h, l], axis=1), jnp.concatenate([r, p], axis=axis))


def lift_all(grams, xfers_t):
    halfway = [mul(f, g, NN) for f, g in zip(xfers_t, grams)]
    return [mul(t, f, NT) for t, f in zip(halfway, xfers_t)]


def lift_pairs(grams, xfers_t):
    lifted = lift_all(grams, xfers_t)
    return [low + high for low, high in zip(lifted[0::2], lifted[1::2])]


def cost(flops, size):
    return pl.CostEstimate(flops=flops, bytes_accessed=size, transcendentals=0)


def unpack_transfers(xfer_ref, xt):
    @pl.loop(0, H // TURN)
    def _(step):
        at = [step * TURN + v for v in range(TURN)]
        turned = [jnp.concatenate([xfer_ref[:, q, :], xfer_ref[:, q + H, :]], axis=0).T for q in at]
        for q, y in zip(at, turned):
            xt[:, q, :] = y


def cholesky_lanes(a):
    sub = lax.broadcasted_iota(jnp.int32, (8, a.shape[2]), 0)

    def cols(block):
        return pl.ds(8 * block, 8)

    for panel in range(K // 8):
        base = 8 * panel
        scale = []
        rows = [a[base + k, pl.ds(base, 8), :] for k in range(8)]
        for k in range(8):
            scale.append(lax.rsqrt(rows[k][k : k + 1, :]))
            rows[k] = rows[k] * scale[k]
            for i in range(k + 1, 8):
                rows[i] = rows[i] - rows[k][i : i + 1, :] * rows[k]
        for k in range(8):
            a[base + k, pl.ds(base, 8), :] = jnp.where(sub >= k, rows[k], 0.0)
        for j in range(panel + 1, K // 8):
            new = []
            for k in range(8):
                acc = a[base + k, pl.ds(8 * j, 8), :]
                for p in range(k):
                    acc = acc - rows[p][k : k + 1, :] * new[p]
                new.append(acc * scale[k])
            for k in range(8):
                a[base + k, pl.ds(8 * j, 8), :] = new[k]
        if panel < K // 8 - 1:

            for i_block in range(panel + 1, K // 8):
                left = [a[base + k, cols(i_block), :] for k in range(8)]

                for j_block in range(i_block, K // 8):
                    right = [a[base + k, cols(j_block), :] for k in range(8)]
                    for i in range(8):
                        acc = a[8 * i_block + i, cols(j_block), :]
                        for k in range(8):
                            acc = acc - left[k][i : i + 1, :] * right[k]
                        a[8 * i_block + i, cols(j_block), :] = acc

    for i in range(8, K):
        a[i, pl.ds(0, i // 8 * 8), :] = jnp.zeros((i // 8 * 8, a.shape[2]), F32)


def factor_halved(s, a):
    @pl.loop(0, H // TURN)
    def _(step):
        at = [step * TURN + v for v in range(TURN)]
        turned = [s[:, q, :].T for q in at]
        for q, y in zip(at, turned):
            a[q] = y[:K]
            a[q + H] = y[K:]

    cholesky_lanes(a)

    @pl.loop(0, H // TURN)
    def _(step):
        at = [step * TURN + v for v in range(TURN)]
        turned = [jnp.concatenate([a[q], a[q + H]], axis=0).T for q in at]
        for q, y in zip(at, turned):
            s[:, q, :] = y


def packed(matrices):
    return matrices % 4 == 0


def slabs(matrices):
    return matrices // 4 * 5 if packed(matrices) else 2 * matrices


def lane(low, high):
    at = lax.broadcasted_iota(jnp.int32, (Q, 2 * K), 1)
    return (at >= low) & (at < high)


def pack(four):
    top = [x[:Q] for x in four]
    low = [jnp.where(lane(0, Q), pltpu.roll(x[Q:], Q, 1), x[Q:]) for x in four]
    gap = lane(K, K + H)
    return jnp.concatenate(
        [
            jnp.where(gap, pltpu.roll(top[3], K, 1), top[0]),
            jnp.where(gap, pltpu.roll(top[3], H, 1), top[1]),
            jnp.where(gap, pltpu.roll(top[3], 2 * K - H, 1), top[2]),
            jnp.where(lane(0, K), low[0], pltpu.roll(low[1], K, 1)),
            jnp.where(lane(0, K), low[2], pltpu.roll(low[3], K, 1)),
        ],
        axis=0,
    )


def rolled(x, by):
    return jnp.concatenate([x[:, 2 * K - by :], x[:, : 2 * K - by]], axis=1)


def unpack(unit):
    zero = jnp.zeros_like(unit[0])
    full = []
    for m in range(3):
        full.append((unit[m], jnp.where(lane(H, K), rolled(unit[m], K), zero)))
    first = jnp.where(lane(0, H), rolled(unit[0], K), rolled(unit[1], 2 * K - H))
    full.append((first, jnp.where(lane(H, K), rolled(unit[2], 2 * K - H), zero)))
    out = []
    for m, (block0, block2) in enumerate(full):
        low = unit[3 + m // 2] if m % 2 == 0 else rolled(unit[3 + m // 2], K)
        block1 = jnp.where(lane(Q, K), low, zero)
        block3 = jnp.where(lane(K - Q, K), rolled(low, K - Q), zero)
        out.append(jnp.concatenate([block0, block1, block2, block3], axis=0)[:, :K])
    return out


def factor_kernel(
    own,
    cols,
    at_ref,
    all_basis_ref,
    all_xfer_ref,
    fac_ref,
    gram1_ref,
    *refs,
):
    sent_refs = refs[:cols]
    xt, s, a, g0, basis_ref, xfer_ref, basis_sem, sem = refs[cols:]
    col = at_ref[1]
    first = col * own
    pairs = min(PAIRS, own // 2)

    def chunk(step):
        rows = pl.ds(2 * pairs * step, 2 * pairs)
        return pltpu.make_async_copy(all_basis_ref.at[rows], basis_ref.at[rows], basis_sem.at[step])

    for step in range(own // 2 // pairs):
        chunk(step).start()
    copy = pltpu.make_async_copy(all_xfer_ref.at[:, :, pl.ds(0, LANES)], xfer_ref, sem)
    copy.start()

    @pl.loop(0, own // 2 // pairs)
    def _(step):
        chunk(step).wait()
        at = [2 * step * pairs + c for c in range(2 * pairs)]
        points = [basis_ref[c] for c in at]
        grams = [mul(x, x, NT) for x in points]
        for c, gram in zip(at, grams):
            g0[c] = gram
            s[c] = halve(gram)

    copy.wait()
    unpack_transfers(xfer_ref, xt)

    @pl.loop(0, own // 2 // pairs)
    def _(step):
        base = step * pairs
        at = [2 * base + c for c in range(2 * pairs)]
        parents = lift_pairs([g0[c] for c in at], [unhalf(xt[first + c]) for c in at])
        for p, gram in enumerate(parents):
            gram1_ref[base + p] = gram
            s[own + base + p] = halve(gram)

    factor_halved(s, a)
    count = own + own // 2
    for g in range(count // 4):
        fac_ref[g] = pack([s[4 * g + m] for m in range(4)]).astype(BF)
    for e in range(cols):
        mine = [s[r * cols + jnp.bitwise_xor(col, e)] for r in range(count // cols)]
        start = 0
        for x in [pack(mine[n : n + 4]) for n in range(0, len(mine), 4)] if packed(len(mine)) else mine:
            for n in range(x.shape[0] // Q):
                sent_refs[e][start + n] = x[Q * n : Q * (n + 1)].astype(BF)
            start += x.shape[0] // Q


def own_factors(at, basis, xfer_lanes, cols):
    own = basis.shape[0]
    count = own + own // 2
    rows = (count + 7) // 8 * 8
    shapes = (
        jax.ShapeDtypeStruct((count // 4, 5 * Q, 2 * K), BF),
        jax.ShapeDtypeStruct((own // 2, K, K), F32),
    ) + (jax.ShapeDtypeStruct((slabs(count // cols), Q, 2 * K), BF),) * cols
    return pl.pallas_call(
        functools.partial(factor_kernel, own, cols),
        out_shape=shapes,
        in_specs=[
            SMEM,
            HBM,
            HBM,
        ],
        out_specs=(VMEM,) * len(shapes),
        scratch_shapes=[
            pltpu.VMEM((LANES, H, 2 * K), F32),
            pltpu.VMEM((rows, H, 2 * K), F32),
            pltpu.VMEM((K, K, rows), F32),
            pltpu.VMEM((own, K, K), F32),
            pltpu.VMEM(basis.shape, F32),
            pltpu.VMEM((K, K, LANES), F32),
            pltpu.SemaphoreType.DMA((own // 2 // min(PAIRS, own // 2),)),
            pltpu.SemaphoreType.DMA,
        ],
        compiler_params=pltpu.CompilerParams(vmem_limit_bytes=52 * 2**20),
        cost_estimate=cost(own * 2**24, 2**23),
    )(at, basis, xfer_lanes)


def chain_kernel(own, cols, at_ref, gram1_ref, xfer_ref, out_ref, xt):
    col = at_ref[1]
    unpack_transfers(xfer_ref, xt)
    grams = [gram1_ref[c] for c in range(own // 2)]
    offset = 0
    width = own * cols // 2
    while len(grams) > 1:
        here = len(grams)
        xfers = [unhalf(xt[offset + col * here + c]) for c in range(here)]
        offset += width
        width //= 2
        if here < 4:
            grams = lift_pairs(grams, xfers)
            continue
        here //= 2
        upper = [unhalf(xt[offset + col * here + c]) for c in range(here)]
        offset += width
        width //= 2
        xfers = [mul(upper[c // 2], x, NN) for c, x in enumerate(xfers)]
        low = lift_pairs(grams, xfers)
        grams = [x + y for x, y in zip(low[0::2], low[1::2])]
    shift = 0
    whole = None
    while width >= 1:
        xfer = unhalf(xt[offset + jnp.right_shift(col, shift)])
        whole = xfer if whole is None else mul(xfer, whole, NN)
        offset += width
        width //= 2
        shift += 1
    rest = halve(lift_all(grams, [whole])[0])
    for n in range(TERMS):
        term = rest.astype(BF)
        out_ref[2 * n] = term[:Q]
        out_ref[2 * n + 1] = term[Q:]
        rest = rest - term.astype(F32)


def lifted_root(at, gram1, xfer_lanes, own, cols):
    return pl.pallas_call(
        functools.partial(chain_kernel, own, cols),
        out_shape=jax.ShapeDtypeStruct((2 * TERMS, Q, 2 * K), BF),
        grid=(1,),
        in_specs=[
            SMEM,
            pl.BlockSpec(gram1.shape, lambda i: (0, 0, 0)),
            pl.BlockSpec((K, K, LANES), lambda i: (0, 0, 1)),
        ],
        out_specs=pl.BlockSpec((2 * TERMS, Q, 2 * K), lambda i: (0, 0, 0)),
        scratch_shapes=[pltpu.VMEM((LANES, H, 2 * K), F32)],
        compiler_params=PARAMS,
        cost_estimate=cost(own * 2**24, 2**22),
    )(at, gram1, xfer_lanes)


def top_kernel(leaves, at_ref, top_ref, *refs):
    pairs = leaves // 2
    parts, (anc_ref, root_ref, level_ref, s, a) = refs[:-5], refs[-5:]
    pair = jnp.right_shift(at_ref[0], 1)
    for m in range(pairs):
        terms = [part[m].reshape(H, 2 * K) for part in parts]
        while len(terms) > 1:
            terms = [x + y for x, y in zip(terms[0::2], terms[1::2])]
        level_ref[jnp.bitwise_xor(pair, m)] = terms[0]
    level = [unhalf(level_ref[m]) for m in range(pairs)]
    heights = []
    slot = 0
    off_top = 0
    while True:
        heights.append(slot)
        for m, gram in enumerate(level):
            s[slot + m] = halve(gram)
        slot += len(level)
        if len(level) == 1:
            break
        level_xfers = [top_ref[off_top + m].T for m in range(len(level))]
        off_top += len(level)
        level = lift_pairs(level, level_xfers)
    factor_halved(s, a)
    for h, start in enumerate(heights):
        anc_ref[0, h] = unhalf(s[start + jnp.right_shift(at_ref[0], h + 1)])
    root_ref[...] = unhalf(s[heights[-1]])


def top_factors(at, parts, top_transfer, leaves):
    height = leaves.bit_length() - 1
    rows = (leaves - 1 + 7) // 8 * 8
    return pl.pallas_call(
        functools.partial(top_kernel, leaves),
        out_shape=(
            jax.ShapeDtypeStruct((1, height, K, K), F32),
            jax.ShapeDtypeStruct((K, K), F32),
        ),
        in_specs=[SMEM, VMEM] + [VMEM] * len(parts),
        out_specs=(VMEM, VMEM),
        scratch_shapes=[
            pltpu.VMEM((leaves // 2, H, 2 * K), F32),
            pltpu.VMEM((rows, H, 2 * K), F32),
            pltpu.VMEM((K, K, rows), F32),
        ],
        compiler_params=PARAMS,
        cost_estimate=cost(2**22, 2**17),
    )(at, top_transfer, *parts)


def lane_groups(sizes):
    return [(which, lane) for which, size in enumerate(sizes) for lane in range(0, size, LANES)]


def turn_kernel(groups, *refs):
    blocks, cells_ref, bt = refs[:-2], refs[-2], refs[-1]
    for g, (which, first) in enumerate(groups):
        src = blocks[which]

        @pl.loop(0, H // TURN)
        def _(step):
            lanes = pl.ds(first, LANES)
            at = [step * TURN + v for v in range(TURN)]
            x = [jnp.concatenate([src[q, :, lanes], src[q + H, :, lanes]], axis=0) for q in at]
            turned = [y.astype(F32).T for y in x]
            for q, y in zip(at, turned):
                bt[:, q, :] = y

        @pl.loop(0, LANES // TURN)
        def _(step):
            at = [step * TURN + u for u in range(TURN)]
            cells = [unhalf(bt[b].astype(BF)) for b in at]
            for b, x in zip(at, cells):
                cells_ref[LANES * g + b] = x


def turned_blocks(blocks):
    groups = lane_groups([x.shape[2] for x in blocks])
    return pl.pallas_call(
        functools.partial(turn_kernel, groups),
        out_shape=jax.ShapeDtypeStruct((LANES * len(groups), K, K), BF),
        in_specs=[VMEM] * len(blocks),
        out_specs=VMEM,
        scratch_shapes=[pltpu.VMEM((LANES, H, 2 * K), F32)],
        compiler_params=PARAMS,
        cost_estimate=cost(2**20, 2**20),
    )(*blocks)


def join_kernel(inputs, *refs):
    pieces, out = refs[: inputs[0]], refs[sum(inputs) :]
    start = 0
    for x in pieces:
        out[0][pl.ds(start, x.shape[0])] = x[...]
        start += x.shape[0]
    if len(out) == 1:
        return
    for n, x in enumerate(pieces):
        last = x.shape[0] - 2 * TERMS
        total = x[last : last + 2].astype(F32)
        for t in range(1, TERMS):
            total = total + x[last + 2 * t : last + 2 * t + 2].astype(F32)
        out[1][n] = total
    start = 0
    for x in refs[inputs[0] : sum(inputs)]:
        out[2][pl.ds(start, x.shape[0])] = x[...]
        start += x.shape[0]


def joined(pieces, packs=()):
    shapes = [jax.ShapeDtypeStruct((sum(x.shape[0] for x in pieces), Q, 2 * K), BF)]
    if packs:
        shapes.append(jax.ShapeDtypeStruct((len(pieces), 2, Q, 2 * K), F32))
        shapes.append(jax.ShapeDtypeStruct((sum(x.shape[0] for x in packs), 5 * Q, 2 * K), BF))
    return pl.pallas_call(
        functools.partial(join_kernel, (len(pieces), len(packs))),
        out_shape=tuple(shapes),
        in_specs=[VMEM] * (len(pieces) + len(packs)),
        out_specs=(VMEM,) * len(shapes),
        compiler_params=PARAMS,
        cost_estimate=cost(0, 2**18),
    )(*pieces, *packs)


def bits(size):
    assert size & (size - 1) == 0
    return size.bit_length() - 1


def row_entry(sizes, at_ref, level, row):
    own, cols = sizes[:2]
    size = own >> level
    row = row - at_ref[0] * (size * cols)
    owner = jnp.bitwise_xor(jnp.right_shift(row, bits(size)), at_ref[1])
    return owner * (own + own // 2) + level * own + jnp.bitwise_and(row, size - 1)


def column_entry(sizes, at_ref, level, column):
    own, cols, leaves = sizes
    size = own >> level
    count = own + own // 2
    owner = jnp.right_shift(column, bits(size))
    away = jnp.bitwise_xor(jnp.right_shift(owner, bits(cols)), at_ref[0])
    part = jnp.bitwise_xor(jnp.bitwise_and(owner, cols - 1), at_ref[1])
    piece = jnp.bitwise_and(away, 1) * (leaves // 2) + jnp.right_shift(away, 1)
    entry = piece * count + part * (count // cols)
    within = jnp.right_shift(jnp.bitwise_and(column, size - 1), bits(cols))
    return entry + level * (own // cols) + within


def fill_column_table(table, start, ref, sizes):
    own, cols, leaves = sizes
    count = own + own // 2
    parts = count // cols
    step = slabs(parts)
    length = ref.shape[0] // (leaves // 2)

    @pl.loop(0, leaves // 2)
    def _(p):
        found = []
        for e in range(cols):
            first = p * length + e * step
            if packed(parts):
                for g in range(parts // 4):
                    found += unpack([ref[first + 5 * g + n] for n in range(5)])
            else:
                for r in range(parts):
                    two = [ref[first + 2 * r + n] for n in range(2)]
                    found.append(unhalf(jnp.concatenate(two, axis=0)))
        for n, x in enumerate(found):
            table[start + p * count + n] = x


def middle_kernel(groups, sizes, at_ref, *refs):
    pairs, (cells_ref, same_ref, other_ref, out_ref, table) = refs[:-5], refs[-5:]
    fill_column_table(table, 0, same_ref, sizes)
    fill_column_table(table, table.shape[0] // 2, other_ref, sizes)
    for g, (level, first) in enumerate(groups):

        @pl.loop(0, LANES // SLOTS)
        def _(step):
            at = [step * SLOTS + u for u in range(SLOTS)]
            cols = [table[column_entry(sizes, at_ref, level, pairs[level][1, first + b])] for b in at]
            cells = [cells_ref[LANES * g + b] for b in at]
            y = [lax.dot_general(x, c, NT, preferred_element_type=F32) for x, c in zip(cells, cols)]
            for b, z in zip(at, y):
                out_ref[LANES * g + b] = z.astype(BF)


def middle_products(sizes, at, pairs, cells, same_core, other_core):
    groups = lane_groups([x.shape[1] for x in pairs])
    return pl.pallas_call(
        functools.partial(middle_kernel, groups, sizes),
        out_shape=jax.ShapeDtypeStruct((cells.shape[0], K, K), BF),
        in_specs=[SMEM] * (1 + len(pairs)) + [VMEM] * 3,
        out_specs=VMEM,
        scratch_shapes=[pltpu.VMEM((sizes[2] * (sizes[0] + sizes[0] // 2), K, K), BF)],
        compiler_params=pltpu.CompilerParams(vmem_limit_bytes=36 * 2**20),
        cost_estimate=cost(cells.shape[0] * 2**19, 2**20),
    )(at, *pairs, cells, same_core, other_core)


def outer_kernel(groups, sizes, outs, orders, at_ref, *refs):
    pairs, counts, middle_ref = refs[:outs], refs[outs : 2 * outs], refs[2 * outs]
    pieces, out_refs = refs[2 * outs + 1 : -outs - 4], refs[-outs - 4 : -4]
    pt, table, ready, sem = refs[-4:]
    packs = (sizes[0] + sizes[0] // 2) // 4
    together = math.gcd(packs, 6)
    for piece, order in zip(pieces, orders):
        for n, e in enumerate(order):

            @pl.loop(0, packs // together)
            def _(step):
                at = [step * together + g for g in range(together)]
                units = [[piece[n * packs + g, Q * u : Q * (u + 1)] for u in range(5)] for g in at]
                full = [unpack(five) for five in units]
                for g, four in zip(at, full):
                    for m in range(4):
                        table[4 * (e * packs + g) + m] = four[m]

    copies = []
    for g, (which, first) in enumerate(groups):

        @pl.loop(0, LANES // SLOTS)
        def _(step):
            at = [step * SLOTS + u for u in range(SLOTS)]
            rows = [table[row_entry(sizes, at_ref, which, pairs[which][0, first + b])] for b in at]
            right = [middle_ref[LANES * g + b] for b in at]
            y = [lax.dot_general(r, x, NN, preferred_element_type=F32) for r, x in zip(rows, right)]
            y = [halve(z) for z in y]
            for b, z in zip(at, y):
                pt[b] = z

        keep = lax.broadcasted_iota(jnp.int32, (2 * K, LANES), 1) < counts[which][0] - first

        @pl.loop(0, H // TURN)
        def _(step):
            at = [step * TURN + v for v in range(TURN)]
            turned = [pt[:, q, :].T for q in at]
            for q, y in zip(at, turned):
                y = jnp.where(keep, y, 0.0).astype(BF)
                ready[g, q] = y[:K]
                ready[g, q + H] = y[K:]

        out = out_refs[which].at[:, :, pl.ds(first, LANES)]
        copies.append(pltpu.make_async_copy(ready.at[g], out, sem.at[g]))
        copies[-1].start()
    for copy in copies:
        copy.wait()


def outer_products(sizes, at, pairs, counts, middle, pieces, orders):
    slots = [x.shape[1] for x in pairs]
    groups = lane_groups(slots)
    entries = 4 * sum(x.shape[0] for x in pieces)
    return pl.pallas_call(
        functools.partial(outer_kernel, groups, sizes, len(slots), orders),
        out_shape=tuple(jax.ShapeDtypeStruct((K, K, size), BF) for size in slots),
        in_specs=[SMEM] * (1 + 2 * len(slots)) + [VMEM] * (1 + len(pieces)),
        out_specs=(ANY,) * len(slots),
        scratch_shapes=[
            pltpu.VMEM((LANES, H, 2 * K), F32),
            pltpu.VMEM((entries, K, K), BF),
            pltpu.VMEM((len(groups), K, K, LANES), BF),
            pltpu.SemaphoreType.DMA((len(groups),)),
        ],
        compiler_params=PARAMS,
        cost_estimate=cost(len(groups) * 2**26, 2**22),
    )(at, *pairs, *counts, middle, *pieces)


def swapped(x, axis, d):
    return lax.ppermute(x, axis, [(i, i ^ d) for i in range(lax.axis_size(axis))])


def on_device(basis, transfer, top_transfer, blocks0, pairs0, counts0, blocks1, pairs1, counts1):
    own = basis.shape[0]
    cols = lax.axis_size("col")
    leaves = lax.axis_size("leaf")
    at = jnp.stack([lax.axis_index("leaf"), lax.axis_index("col")]).astype(jnp.int32)
    xfer_lanes = jnp.transpose(transfer, (1, 2, 0))
    lanes0, lanes1 = jnp.transpose(blocks0, (1, 2, 0)), jnp.transpose(blocks1, (1, 2, 0))
    sizes = (own, cols, leaves)
    pairs = (jnp.transpose(pairs0), jnp.transpose(pairs1))

    factors, gram1, *sent = own_factors(at, basis, xfer_lanes, cols)
    received = [swapped(sent[d], "col", d) for d in range(1, cols)]
    terms = lifted_root(at, gram1, xfer_lanes, own, cols)
    received, terms, factors, lanes0, lanes1 = lax.optimization_barrier(
        (received, terms, factors, lanes0, lanes1)
    )

    (part,) = joined([sent[0]] + received + [terms])
    chips = [swapped(part, "leaf", d) for d in range(2, leaves, 2)]
    bit = cols // 2
    early = swapped(factors, "col", bit)
    cells = turned_blocks((lanes0, lanes1))
    chips, early, cells = lax.optimization_barrier((chips, early, cells))

    same_core, pair_part, rows = joined([part] + chips, [factors, early])
    other_core = swapped(same_core, "leaf", 1)
    orders = [0, bit]
    while True:
        bit //= 2
        forwarded = swapped(rows, "col", bit)
        orders = [orders, [e ^ bit for e in orders]]
        if bit == 1:
            break
        rows = jnp.concatenate([rows, forwarded], axis=0)
        orders = orders[0] + orders[1]
    there = other_core.reshape(leaves // 2, part.shape[0], Q, 2 * K)[:, -2 * TERMS :].astype(F32)
    other_part = there[:, 0:2]
    for t in range(1, TERMS):
        other_part = other_part + there[:, 2 * t : 2 * t + 2]
    pair_part = pair_part + other_part
    tops = [pair_part] + [swapped(pair_part, "col", d) for d in range(1, cols)]
    middle = middle_products(sizes, at, pairs, cells, same_core, other_core)
    out0, out1 = outer_products(
        sizes, at, pairs, (counts0, counts1), middle, [rows, forwarded], orders
    )
    ancestors, root = top_factors(at, tops, top_transfer, leaves)
    return (jnp.transpose(out0, (2, 0, 1)), jnp.transpose(out1, (2, 0, 1)), root, ancestors)


def solution(mesh):
    in_specs = (
        P(("leaf", "col"), None, None),
        P("leaf", None, None),
        P(),
        P(("leaf", "col"), None, None),
        P(("leaf", "col"), None),
        P(("leaf", "col")),
        P(("leaf", "col"), None, None),
        P(("leaf", "col"), None),
        P(("leaf", "col")),
    )
    out_specs = (
        P(("leaf", "col"), None, None),
        P(("leaf", "col"), None, None),
        P(),
        P("leaf", None, None, None),
    )
    return jax.shard_map(
        on_device, mesh=mesh, in_specs=in_specs, out_specs=out_specs, check_vma=False
    )
```
